32 devices in a mesh: dp: 8 (over z, x), mp: 4 (over y, core).
Axes of the slice: x: 2, y: 2, z: 4, core: 2. Of those that a mesh axis runs over, the one named last changes fastest.
Arguments:
- tokens: bfloat16 [8192, 768], P('dp'), may hold values from -6 to 6
- memory: bfloat16 [8192, 768], P('dp'), may hold values from -6 to 6
- cotangent: bfloat16 [8192, 768], P('dp'), may hold values from -6 to 6
- table_lengths: int32 [8, 4], P('dp'), may hold values from 1 to 512, 1024 in all within a row
- table_plots: int32 [8, 4], P('dp'), may hold values from 0 to 3, each once within a row
- gains: float32 [768, 3], replicated, may hold values from 0.5 to 1.5
- w_qkv: bfloat16 [768, 3, 768], P(None, None, 'mp'), may hold values from -0.21875 to 0.21875
- w_self_out: bfloat16 [768, 768], P(None, 'mp'), may hold values from -0.625 to 0.625
- w_cross_query: bfloat16 [768, 768], P(None, 'mp'), may hold values from -0.21875 to 0.21875
- w_cross_kv: bfloat16 [768, 2, 768], P(None, None, 'mp'), may hold values from -0.21875 to 0.21875
- w_cross_out: bfloat16 [768, 768], P(None, 'mp'), may hold values from -0.875 to 0.875
- w_gate_up: bfloat16 [768, 2, 2048], P(None, None, 'mp'), may hold values from -0.21875 to 0.21875
- w_down: bfloat16 [768, 2048], P(None, 'mp'), may hold values from -0.125 to 0.125
Outputs:
- layer_out: bfloat16 [8192, 768], P('dp')
- grad_tokens: float32 [8192, 768], P('dp')
- grad_memory: float32 [8192, 768], P('dp')
- grad_gains: float32 [768, 3], P('dp')
- grad_qkv: float32 [768, 3, 768], P('dp', None, 'mp')
- grad_self_out: float32 [768, 768], P('dp', 'mp')
- grad_cross_query: float32 [768, 768], P('dp', 'mp')
- grad_cross_kv: float32 [768, 2, 768], P('dp', None, 'mp')
- grad_cross_out: float32 [768, 768], P('dp', 'mp')
- grad_gate_up: float32 [768, 2, 2048], P('dp', None, 'mp')
- grad_down: float32 [768, 2048], P('dp', 'mp')
- step_qkv: float32 [768, 3, 768], P('dp', None, 'mp')
- step_self_out: float32 [768, 768], P('dp', 'mp')
- step_cross_query: float32 [768, 768], P('dp', 'mp')
- step_cross_kv: float32 [768, 2, 768], P('dp', None, 'mp')
- step_cross_out: float32 [768, 768], P('dp', 'mp')
- step_gate_up: float32 [768, 2, 2048], P('dp', None, 'mp')
- step_down: float32 [768, 2048], P('dp', 'mp')
The draws below stay inside these ranges and needn't reach their ends.
Inputs may be any that keep to these rules, and one draw needn't show every extreme that they name: `table_lengths`: each pack's 4 lengths add up to 1024, and the longest is 512. `table_plots`: each pack's row is a permutation of its 4 plots.
All inputs are finite; a program needn't handle non-finite values.
Results may differ from the reference program's by a relative error of at most 0.02.
Values sent between devices are 32-bit elements; how exact they have to be, the bound alone decides.
No kernel may reach another device: no remote copies, remote signals or barrier semaphores. Data moves between devices by JAX's collectives and lax.ppermute only.
A program may use at most 128 MiB of HBM per device.

```python
import math
import jax
import jax.numpy as jnp
import numpy as np
from jax import lax

D = 768
HEADS = 12
DH = 64
FF = 2048
TOK_DEV = 1024
TABS = 4
PATCH = 256
LONGEST = 512
HD = 768
MEM_DEV = 1024
PACKS = 8
TOKENS = 8192
MEMROWS = 8192


def shard_levels(stream_key, dims, cuts, low, largest):
    loudness, own = 1.0, jax.random.fold_in(stream_key, 6)
    for position, blocks in cuts:
        draws = jnp.exp(jax.random.uniform(jax.random.fold_in(own, position), (blocks,), jnp.float32, low / len(cuts), largest / len(cuts)))
        loudness = loudness * jnp.repeat(draws, dims[position] // blocks).reshape([-1 if axis == position else 1 for axis in range(len(dims))])
    return loudness


def profile(count, total, bound, skew):
    portions = [(1 << 20) // math.isqrt(grade ** skew) + 1 for grade in range(2, count + 1)]
    spare, counts = total - bound - (count - 1), [1] * (count - 1)
    while spare > 0:
        free = [i for i in range(count - 1) if counts[i] < bound]
        pool, left = sum([portions[i] for i in free]), spare
        for i in free:
            more = min(bound - counts[i], max(1, left * portions[i] // pool), spare)
            counts[i] = counts[i] + more
            spare = spare - more
    return np.array([bound] + counts)


def uneven_parts(own_key, count, total, bound, skew):
    if count == 2:
        one = jax.random.randint(own_key, (), max(1, total - bound), min(bound, total - 1) + 1)
        return jnp.stack([one, total - one])
    sizes = jnp.asarray(profile(count, total, bound, skew), jnp.int32)
    couples = (count - 1) // 2
    giver, taker = sizes[1:1 + 2 * couples:2], sizes[2:2 + 2 * couples:2]
    margin = jnp.minimum(giver - 1, bound - taker)
    moved = jax.random.randint(jax.random.fold_in(own_key, 1), (couples,), 0, 1 << 20) % (margin + 1)
    sizes = sizes.at[1:1 + 2 * couples:2].set(giver - moved).at[2:2 + 2 * couples:2].set(taker + moved)
    return sizes[jax.random.permutation(jax.random.fold_in(own_key, 2), count)]


def noise(key, shape, deviation, most, shards=(), kind=jnp.bfloat16):
    factor_of = shard_levels(key, shape, shards, -0.22, 0.18) if shards else 1.0
    values = jax.random.normal(key, shape, jnp.float32) * deviation * factor_of
    return jnp.minimum(jnp.maximum(values, -most), most).astype(kind)


def setup_inputs(seed: int = 0) -> dict:
    key_of = jax.random.split(jax.random.key(seed), 14)
    return {
        "tokens": noise(key_of[0], (TOKENS, D), 1.0, 6.0, ((0, 8),)),
        "memory": noise(key_of[1], (MEMROWS, D), 1.0, 6.0, ((0, 8),)),
        "cotangent": noise(key_of[2], (TOKENS, D), 1.0, 6.0, ((0, 8),)),
        "table_lengths": jax.vmap(lambda own: uneven_parts(own, TABS, TOK_DEV, LONGEST, 2))(jax.random.split(key_of[3], PACKS)).reshape((PACKS, TABS)).astype(jnp.int32),
        "table_plots": jax.vmap(lambda own: jax.random.permutation(own, TABS))(jax.random.split(key_of[4], PACKS)).reshape((PACKS, TABS)).astype(jnp.int32),
        "gains": jnp.clip(1.0 + 0.1 * jax.random.normal(key_of[5], (D, 3), jnp.float32), 0.5, 1.5),
        "w_qkv": noise(key_of[6], (D, 3, HD), D ** -0.5, 0.21875, ((2, 4),)),
        "w_self_out": noise(key_of[7], (D, HD), (HD // 8) ** -0.5, 0.625, ((1, 4),)),
        "w_cross_query": noise(key_of[8], (D, HD), D ** -0.5, 0.21875, ((1, 4),)),
        "w_cross_kv": noise(key_of[9], (D, 2, HD), D ** -0.5, 0.21875, ((2, 4),)),
        "w_cross_out": noise(key_of[10], (D, HD), (HD // 16) ** -0.5, 0.875, ((1, 4),)),
        "w_gate_up": noise(key_of[11], (D, 2, FF), D ** -0.5, 0.21875, ((2, 4),)),
        "w_down": noise(key_of[12], (D, FF), FF ** -0.5, 0.125, ((1, 4),)),
    }


@jax.custom_vjp
def low(v):
    return lax.optimization_barrier(v.astype(jnp.bfloat16)).astype(jnp.float32)

@jax.custom_vjp
def low_back(v):
    return v

def low_keep(v):
    return (low(v), None)

def low_pass(kept, grad):
    return (grad,)

def back_keep(v):
    return (v, None)

def back_low(kept, grad):
    return (low(grad),)
low.defvjp(low_keep, low_pass)
low_back.defvjp(back_keep, back_low)
HIGHEST = lax.Precision.HIGHEST

def rms_norm(hidden_in, gain_col):
    return hidden_in * lax.rsqrt(lax.optimization_barrier(jnp.mean(hidden_in * hidden_in, axis=-1, keepdims=True)) + 1e-06) * gain_col

def table_ids(length_row, plot_row, slot_count):
    ends = jnp.cumsum(length_row).astype(jnp.int32)
    places = jnp.arange(slot_count, dtype=jnp.int32)
    segment = lax.optimization_barrier(jnp.sum((places[:, None] >= ends[None, :]).astype(jnp.int32), axis=1)).astype(jnp.int32)
    tables = jnp.arange(length_row.shape[0], dtype=jnp.int32)
    chosen = (segment[:, None] == tables[None, :]).astype(jnp.int32)
    plot_of = lax.optimization_barrier(jnp.sum(chosen * plot_row[None, :].astype(jnp.int32), axis=1)).astype(jnp.int32)
    return (segment, plot_of)

def attend(query, keys, values, allowed):
    raw = jnp.einsum('qhd,khd->hqk', query, keys, precision=HIGHEST) * (1.0 / math.sqrt(DH))
    scores = low_back(raw)
    scores = jnp.where(allowed[None], scores, -1e+30)
    probs = jax.nn.softmax(scores, axis=-1)
    mixed = jnp.einsum('hqk,khd->qhd', low(probs), values, precision=HIGHEST)
    return low(low_back(mixed))

def pack_forward(weights, item):
    gains, w_qkv, w_self_out, w_cross_query, w_cross_kv, w_cross_out, w_gate_up, w_down = weights
    inputs, mem_rows, segment, plot_of = item
    slot_count = inputs.shape[0]
    mem_count = mem_rows.shape[0]
    places = jnp.arange(slot_count, dtype=jnp.int32)
    self_mask = (segment[:, None] == segment[None, :]) & (places[None, :] <= places[:, None])
    key_plot = jnp.arange(mem_count, dtype=jnp.int32) // PATCH
    cross_mask = plot_of[:, None] == key_plot[None, :]
    normed_a = low(rms_norm(inputs, gains[:, 0]))
    qkv = low(low_back(jnp.einsum('sd,dkc->skc', normed_a, w_qkv, precision=HIGHEST)))
    qkv = qkv.reshape(slot_count, 3, HEADS, DH)
    mixed_a = attend(qkv[:, 0], qkv[:, 1], qkv[:, 2], self_mask).reshape(slot_count, HD)
    branch_a = low_back(jnp.einsum('sc,dc->sd', mixed_a, w_self_out, precision=HIGHEST))
    first = inputs + branch_a
    normed_b = low(rms_norm(first, gains[:, 1]))
    query_b = low(low_back(jnp.dot(normed_b, w_cross_query, precision=HIGHEST))).reshape(slot_count, HEADS, DH)
    kv_b = low(low_back(jnp.einsum('md,dkc->mkc', mem_rows, w_cross_kv, precision=HIGHEST)))
    kv_b = kv_b.reshape(mem_count, 2, HEADS, DH)
    mixed_b = attend(query_b, kv_b[:, 0], kv_b[:, 1], cross_mask).reshape(slot_count, HD)
    branch_b = low_back(jnp.einsum('sc,dc->sd', mixed_b, w_cross_out, precision=HIGHEST))
    second = first + branch_b
    normed_c = low(rms_norm(second, gains[:, 2]))
    gate_up = low_back(jnp.einsum('sd,dkf->skf', normed_c, w_gate_up, precision=HIGHEST))
    hidden = low(jax.nn.gelu(gate_up[:, 0], approximate=True) * gate_up[:, 1])
    branch_c = low_back(jnp.einsum('sf,df->sd', hidden, w_down, precision=HIGHEST))
    return second + branch_c

def adafactor(grad):
    row_count = grad.shape[0]
    flat_rows = grad.reshape(row_count, -1)
    square = flat_rows * flat_rows
    row_mean = lax.optimization_barrier(jnp.mean(square, axis=1)) + 1e-30
    col_mean = lax.optimization_barrier(jnp.mean(square, axis=0)) + 1e-30
    mean_rows = jnp.mean(row_mean)
    factor = row_mean[:, None] * col_mean[None, :] / mean_rows
    return (flat_rows * lax.rsqrt(factor)).reshape(grad.shape)

def reference(tokens, memory, cotangent, table_lengths, table_plots, gains, w_qkv, w_self_out, w_cross_query, w_cross_kv, w_cross_out, w_gate_up, w_down):
    pack_count = table_lengths.shape[0]
    segment, plot_of = jax.vmap(lambda lrow, prow: table_ids(lrow, prow, TOK_DEV))(table_lengths, table_plots)
    inputs = tokens.astype(jnp.float32).reshape(pack_count, TOK_DEV, D)
    mem_all = memory.astype(jnp.float32).reshape(pack_count, MEM_DEV, D)
    weights = (gains.astype(jnp.float32), w_qkv.astype(jnp.float32), w_self_out.astype(jnp.float32), w_cross_query.astype(jnp.float32), w_cross_kv.astype(jnp.float32), w_cross_out.astype(jnp.float32), w_gate_up.astype(jnp.float32), w_down.astype(jnp.float32))

    def whole(inputs_all, memory_all, weight_set):
        stepper = jax.checkpoint(lambda item: pack_forward(weight_set, item))
        return lax.map(stepper, (inputs_all, memory_all, segment, plot_of))
    result, pull = jax.vjp(whole, inputs, mem_all, weights)
    grad_in, grad_mem, grad_weights = pull(cotangent.astype(jnp.float32).reshape(pack_count, TOK_DEV, D))
    layer_out = result.reshape(pack_count * TOK_DEV, D).astype(jnp.bfloat16)
    grad_tokens = grad_in.reshape(pack_count * TOK_DEV, D)
    grad_memory = grad_mem.reshape(pack_count * MEM_DEV, D)
    grad_gains = grad_weights[0]
    steps = tuple((adafactor(grad) for grad in grad_weights[1:]))
    return (layer_out, grad_tokens, grad_memory, grad_gains, grad_weights[1], grad_weights[2], grad_weights[3], grad_weights[4], grad_weights[5], grad_weights[6], grad_weights[7], steps[0], steps[1], steps[2], steps[3], steps[4], steps[5], steps[6])
```

```python
import functools
import math

import jax
import jax.numpy as jnp
from jax import lax
from jax.experimental import pallas as pl
from jax.experimental.pallas import tpu as pltpu
from jax.sharding import PartitionSpec as P

DH = 64
PATCH = 256
LONGEST = 512
ROWS = 256
SPAN = LONGEST // ROWS
F32 = jnp.float32
BF16 = jnp.bfloat16
NEG = -1e30
SCALE = 1.0 / math.sqrt(DH)
VMEM_BYTES = 56 * 1024 * 1024


def nn(a, b):
    return lax.dot_general(a, b, (((1,), (0,)), ((), ())), preferred_element_type=F32)


def nt(a, b):
    return lax.dot_general(a, b, (((1,), (1,)), ((), ())), preferred_element_type=F32)


def tn(a, b):
    return lax.dot_general(a, b, (((0,), (0,)), ((), ())), preferred_element_type=F32)


def normed_of(rows, gain):
    return rows * lax.rsqrt(jnp.mean(rows * rows, axis=-1, keepdims=True) + 1e-06) * gain


def norm_vjp(rows, gain, grad):
    inv = lax.rsqrt(jnp.mean(rows * rows, axis=-1, keepdims=True) + 1e-06)
    scaled = rows * inv
    hg = grad * gain
    inner = jnp.mean(hg * scaled, axis=-1, keepdims=True)
    grad_rows = inv * (hg - scaled * inner)
    grad_gain = jnp.sum(grad * scaled, axis=0, keepdims=True)
    return grad_rows, grad_gain, scaled


def place_pieces(dst, base, ctl, by_y, by_x, by_z):
    q = by_x.shape[0]
    x, z = ctl[0], ctl[1]

    def at(offset):
        return pl.ds(pl.multiple_of(offset, 64), q)

    dst[at(base + x * q), :] = by_y[:q, :].astype(BF16)
    dst[at(base + (1 - x) * q), :] = by_x[...].astype(BF16)
    dst[at(base + (2 + z) * q), :] = by_y[q:, :].astype(BF16)
    dst[at(base + (3 - z) * q), :] = by_z[...].astype(BF16)


def table_ends(lengths):
    ends = []
    total = lengths[0, 0]
    for j in range(1, lengths.shape[1]):
        ends.append(total)
        total = total + lengths[0, j]
    return ends


def query_places(base):
    return lax.broadcasted_iota(jnp.int32, (1, ROWS), 1) + base


def self_bias(lengths, base, low, width):
    places = query_places(base)
    start = jnp.zeros_like(places)
    for end in table_ends(lengths):
        start = jnp.where(places >= end, end, start)
    keys = lax.broadcasted_iota(jnp.int32, (width, ROWS), 0) + low
    return jnp.where((keys >= start) & (keys <= places), 0.0, NEG)


def window_cases(block, body):
    for back in range(SPAN + 1):
        width = (back + 1) * ROWS

        @pl.when(block == back if back < SPAN else block >= SPAN)
        def _run(back=back, width=width):
            if back < SPAN:
                body(0, width)
            else:
                body(pl.multiple_of((block - SPAN) * ROWS, ROWS), width)


def full(shape):
    return pl.BlockSpec(shape, lambda i: (0,) * len(shape))


def by_rows(width):
    return pl.BlockSpec((ROWS, width), lambda i: (i, 0))


def by_cols(height):
    return pl.BlockSpec((height, ROWS), lambda i: (0, i))


SMEM = pl.BlockSpec(memory_space=pltpu.SMEM)


def run(kernel, grid, ins, outs, scratch, flops, name, transcendentals=0):
    arrays = [a for a, _ in ins]
    moved = sum(a.size * a.dtype.itemsize for a in arrays) + sum(
        math.prod(s.shape) * jnp.dtype(s.dtype).itemsize for s, _ in outs
    )
    return pl.pallas_call(
        kernel,
        grid=(grid,),
        in_specs=[s for _, s in ins],
        out_specs=[s for _, s in outs],
        out_shape=[s for s, _ in outs],
        scratch_shapes=scratch,
        compiler_params=pltpu.CompilerParams(
            vmem_limit_bytes=VMEM_BYTES, dimension_semantics=("arbitrary",)
        ),
        cost_estimate=pl.CostEstimate(
            flops=flops, bytes_accessed=moved, transcendentals=transcendentals
        ),
        name=name,
    )(*arrays)


def sds(shape, dtype):
    return jax.ShapeDtypeStruct(shape, dtype)


def self_forward_kernel(remote, heads, *refs):
    if remote:
        (lengths, ctl, tokens, gain, by_y, by_x, by_z, base_out) = refs[:8]
        (qkv_t, mixed_t, lse, out, w_out, k_rows) = refs[8:]
        w = w_out
    else:
        (lengths, tokens, gain, w) = refs[:4]
        (qkv_t, mixed_t, lse, out, k_rows) = refs[4:]
    block = pl.program_id(0)
    hq = heads * DH
    if remote:

        @pl.when(block == 0)
        def _place():
            place_pieces(w, 0, ctl, by_y, by_x, by_z)

    base = pl.multiple_of(block * ROWS, ROWS)
    here = pl.ds(base, ROWS)
    normed = normed_of(tokens[...].astype(F32), gain[...]).astype(BF16)
    qkv = nt(w[0 : 3 * hq, :], normed).astype(BF16)
    q_all = (qkv[:hq].astype(F32) * SCALE).astype(BF16)
    qkv_t[0:hq, here] = q_all
    qkv_t[hq : 3 * hq, here] = qkv[hq:]
    for h in range(heads):
        k_rows[h, here, :] = qkv[hq + h * DH : hq + (h + 1) * DH].T

    def attend(low, width):
        window = pl.ds(low, width)
        bias = self_bias(lengths, base, low, width)
        for h in range(heads):
            own = slice(h * DH, (h + 1) * DH)
            s = nn(k_rows[h, window, :], q_all[own]) + bias
            top = jnp.max(s, axis=0, keepdims=True)
            e = jnp.exp(s - top)
            total = jnp.sum(e, axis=0, keepdims=True)
            o = nn(qkv_t[2 * hq + h * DH : 2 * hq + (h + 1) * DH, window], e.astype(BF16))
            mixed_t[own, :] = (o * (1.0 / total)).astype(BF16)
            lse[h : h + 1, :] = top + jnp.log(total)

    window_cases(block, attend)
    part = tn(mixed_t[...], w[3 * hq : 4 * hq, :])
    out[...] = part + base_out[...] if remote else part


def self_forward(lengths, tokens, gain, w, heads, remote=None):
    slots, width = tokens.shape
    hq = heads * DH
    outs = [
        (sds((3 * hq, slots), BF16), full((3 * hq, slots))),
        (sds((hq, slots), BF16), by_cols(hq)),
        (sds((8, slots), F32), by_cols(8)),
        (sds((slots, width), F32), by_rows(width)),
    ]
    scratch = [pltpu.VMEM((heads, slots, DH), BF16)]
    if remote is None:
        ins = [(lengths, SMEM), (tokens, by_rows(width)), (gain, full(gain.shape)), (w, full(w.shape))]
    else:
        ctl, by_y, by_x, by_z, base_out = remote
        ins = [
            (lengths, SMEM),
            (ctl, SMEM),
            (tokens, by_rows(width)),
            (gain, full(gain.shape)),
            (by_y, full(by_y.shape)),
            (by_x, full(by_x.shape)),
            (by_z, full(by_z.shape)),
            (base_out, by_rows(width)),
        ]
        outs.append((sds((4 * hq, width), BF16), full((4 * hq, width))))
    flops = 2 * slots * width * 4 * hq + heads * 4 * slots * slots * DH
    return run(
        functools.partial(self_forward_kernel, remote is not None, heads),
        slots // ROWS, ins, outs, scratch, flops, "self_forward", heads * slots * slots,
    )


def memory_kernel(remote, heads, *refs):
    hq = heads * DH
    if remote:
        ctl, memory, by_y, by_x, by_z, kv_t, k_rows, v_rows, w = refs

        @pl.when(pl.program_id(0) == 0)
        def _place():
            place_pieces(w, 0, ctl, by_y, by_x, by_z)
    else:
        memory, w, kv_t, k_rows, v_rows = refs
    kv = nt(w[hq : 3 * hq, :], memory[...]).astype(BF16)
    kv_t[...] = kv
    for h in range(heads):
        k_rows[h] = kv[h * DH : (h + 1) * DH].T
        v_rows[h] = kv[hq + h * DH : hq + (h + 1) * DH].T


def memory_forward(memory, w, heads, remote=None):
    count, width = memory.shape
    hq = heads * DH
    head_rows = pl.BlockSpec((heads, ROWS, DH), lambda i: (0, i, 0))
    outs = [
        (sds((2 * hq, count), BF16), by_cols(2 * hq)),
        (sds((heads, count, DH), BF16), head_rows),
        (sds((heads, count, DH), BF16), head_rows),
    ]
    if remote is None:
        ins = [(memory, by_rows(width)), (w, full(w.shape))]
    else:
        ctl, by_y, by_x, by_z = remote
        ins = [
            (ctl, SMEM),
            (memory, by_rows(width)),
            (by_y, full(by_y.shape)),
            (by_x, full(by_x.shape)),
            (by_z, full(by_z.shape)),
        ]
        outs.append((sds((4 * hq, width), BF16), full((4 * hq, width))))
    return run(
        functools.partial(memory_kernel, remote is not None, heads),
        count // ROWS, ins, outs, [], 2 * count * width * 2 * hq, "memory_forward",
    )


def tables_of_block(lengths, base, body):
    ends = table_ends(lengths)
    places = query_places(base)
    segment = jnp.zeros_like(places)
    first_table = jnp.int32(0)
    last_table = jnp.int32(0)
    for end in ends:
        segment = segment + (places >= end).astype(jnp.int32)
        first_table = first_table + (base >= end).astype(jnp.int32)
        last_table = last_table + (base + ROWS - 1 >= end).astype(jnp.int32)

    def step(table, carry):
        body(table, segment == table)
        return carry

    lax.fori_loop(first_table, last_table + 1, step, 0)


def cross_forward_kernel(leading, heads, *refs):
    hq = heads * DH
    if leading:
        (lengths, plots, tokens, part, other, gain, w, kv_t, k_rows) = refs[:9]
        (q_t, mixed_t, lse, out, first, normed_out) = refs[9:]
        rows = tokens[...].astype(F32) + (part[...] + other[...])
        first[...] = rows
        normed = normed_of(rows, gain[...]).astype(BF16)
        normed_out[...] = normed
    else:
        (lengths, plots, normed_in, w, kv_t, k_rows, base_out) = refs[:7]
        (q_t, mixed_t, lse, out) = refs[7:]
        normed = normed_in[...]
    base = pl.multiple_of(pl.program_id(0) * ROWS, ROWS)
    query = nt(w[0:hq, :], normed).astype(BF16)
    q_all = (query.astype(F32) * SCALE).astype(BF16)
    q_t[...] = q_all

    def table(j, member):
        plot = pl.ds(pl.multiple_of(plots[0, j] * PATCH, PATCH), PATCH)
        for h in range(heads):
            own = slice(h * DH, (h + 1) * DH)
            s = nn(k_rows[h, plot, :], q_t[own, :])
            top = jnp.max(s, axis=0, keepdims=True)
            e = jnp.exp(s - top)
            total = jnp.sum(e, axis=0, keepdims=True)
            o = nn(kv_t[hq + h * DH : hq + (h + 1) * DH, plot], e.astype(BF16))
            o = o * (1.0 / total)
            mixed_t[own, :] = jnp.where(member, o, mixed_t[own, :].astype(F32)).astype(BF16)
            lse[h : h + 1, :] = jnp.where(member, top + jnp.log(total), lse[h : h + 1, :])

    tables_of_block(lengths, base, table)
    part_out = tn(mixed_t[...], w[3 * hq : 4 * hq, :])
    out[...] = part_out if leading else part_out + base_out[...]


def cross_forward(lengths, plots, w, kv_t, k_rows, heads, lead=None, follow=None):
    hq = heads * DH
    slots = (lead or follow)[0].shape[0]
    width = w.shape[1]
    outs = [
        (sds((hq, slots), BF16), by_cols(hq)),
        (sds((hq, slots), BF16), by_cols(hq)),
        (sds((8, slots), F32), by_cols(8)),
        (sds((slots, width), F32), by_rows(width)),
    ]
    shared = [(w, full(w.shape)), (kv_t, full(kv_t.shape)), (k_rows, full(k_rows.shape))]
    if lead is not None:
        tokens, part, other, gain = lead
        ins = [
            (lengths, SMEM),
            (plots, SMEM),
            (tokens, by_rows(width)),
            (part, by_rows(width)),
            (other, by_rows(width)),
            (gain, full(gain.shape)),
        ] + shared
        outs += [
            (sds((slots, width), F32), by_rows(width)),
            (sds((slots, width), BF16), by_rows(width)),
        ]
    else:
        normed, base_out = follow
        ins = [(lengths, SMEM), (plots, SMEM), (normed, by_rows(width))] + shared
        ins.append((base_out, by_rows(width)))
    flops = 2 * slots * width * 2 * hq + heads * 8 * slots * PATCH * DH
    return run(
        functools.partial(cross_forward_kernel, lead is not None, heads),
        slots // ROWS, ins, outs, [], flops, "cross_forward", heads * slots * PATCH * 2,
    )


def feed_kernel(leading, units, *refs):
    if leading:
        (first, part, other, gain, cot, w) = refs[:6]
        (result, grad_in, second, normed_out, dw) = refs[6:]
        rows = first[...] + (part[...] + other[...])
        second[...] = rows
        normed = normed_of(rows, gain[...]).astype(BF16)
        normed_out[...] = normed

        @pl.when(pl.program_id(0) == 0)
        def _zero():
            dw[...] = jnp.zeros_like(dw)
    else:
        (ctl, normed_in, cot, y0, x0, z0, y1, x1, z1, base_result, base_grad) = refs[:11]
        (result, grad_in, w) = refs[11:]
        normed = normed_in[...]

        @pl.when(pl.program_id(0) == 0)
        def _place():
            place_pieces(w, 0, ctl, y0, x0, z0)
            place_pieces(w, 4 * x0.shape[0], ctl, y1, x1, z1)

    cot_rows = cot[...]
    gate_up = nt(normed, w[0 : 2 * units, :])
    gate, up = gate_up[:, :units], gate_up[:, units:]
    c0 = math.sqrt(2.0 / math.pi)
    square = gate * gate
    th = jnp.tanh(c0 * gate * (1.0 + 0.044715 * square))
    half = 0.5 * (1.0 + th)
    gelu = gate * half
    slope = half + (0.5 * c0) * gate * (1.0 - th * th) * (1.0 + (3 * 0.044715) * square)
    hidden = (gelu * up).astype(BF16)
    res = nn(hidden, w[2 * units : 3 * units, :])
    grad_hidden = nt(cot_rows, w[2 * units : 3 * units, :])
    grad_gate = (grad_hidden * up * slope).astype(BF16)
    grad_up = (grad_hidden * gelu).astype(BF16)
    back = nn(grad_gate, w[0:units, :]) + nn(grad_up, w[units : 2 * units, :])
    if leading:
        result[...] = res
        grad_in[...] = back
        dw[:, 0:units] += tn(normed, grad_gate)
        dw[:, units : 2 * units] += tn(normed, grad_up)
        dw[:, 2 * units : 3 * units] += tn(cot_rows, hidden)
    else:
        result[...] = res + base_result[...]
        grad_in[...] = back + base_grad[...]


def feed(units, lead=None, follow=None):
    if lead is not None:
        first, part, other, gain, cot, w = lead
        slots, width = first.shape
        ins = [
            (first, by_rows(width)),
            (part, by_rows(width)),
            (other, by_rows(width)),
            (gain, full(gain.shape)),
            (cot, by_rows(width)),
            (w, full(w.shape)),
        ]
    else:
        ctl, normed, cot, pieces, base_result, base_grad = follow
        slots, width = normed.shape
        ins = [(ctl, SMEM), (normed, by_rows(width)), (cot, by_rows(width))]
        ins += [(piece, full(piece.shape)) for piece in pieces]
        ins += [(base_result, by_rows(width)), (base_grad, by_rows(width))]
    outs = [
        (sds((slots, width), F32), by_rows(width)),
        (sds((slots, width), F32), by_rows(width)),
    ]
    scratch = []
    if lead is not None:
        outs += [
            (sds((slots, width), F32), by_rows(width)),
            (sds((slots, width), BF16), by_rows(width)),
            (sds((width, 3 * units), F32), full((width, 3 * units))),
        ]
    else:
        scratch = [pltpu.VMEM((3 * units, width), BF16)]
    flops = 2 * slots * width * units * (9 if lead is not None else 6)
    return run(
        functools.partial(feed_kernel, lead is not None, units),
        slots // ROWS, ins, outs, scratch, flops, "feed", slots * units,
    )


def cross_backward_kernel(leading, heads, *refs):
    hq = heads * DH
    if leading:
        (lengths, plots, second, part, other, cot, gain, normed, memory) = refs[:9]
        (w, q_t, mixed_t, lse, kv_t, k_rows, v_rows) = refs[9:16]
        (grad_in, grad_mem, grad_second, branch_out, grad_gain, dw) = refs[16:22]
        (dkv, dq, dm, dw_t) = refs[22:]
    else:
        (lengths, plots, branch_in, w, q_t, lse, kv_t, k_rows, v_rows, base_grad, base_mem) = refs[:11]
        (grad_in, grad_mem, dkv, dq, dm) = refs[11:]
    block = pl.program_id(0)
    last = pl.num_programs(0) - 1
    base = pl.multiple_of(block * ROWS, ROWS)

    @pl.when(block == 0)
    def _zero():
        dkv[...] = jnp.zeros_like(dkv)
        if leading:
            dw_t[...] = jnp.zeros_like(dw_t)
            grad_gain[...] = jnp.zeros_like(grad_gain)

    if leading:
        grad_rows, gain_rows, _ = norm_vjp(second[...], gain[...], part[...] + other[...])
        total = cot[...].astype(F32) + grad_rows
        grad_second[...] = total
        branch = total.astype(BF16)
        branch_out[...] = branch
        grad_gain[0:1, :] += gain_rows
    else:
        branch = branch_in[...]
    dm[...] = nt(w[3 * hq : 4 * hq, :], branch).astype(BF16)
    dq[...] = jnp.zeros_like(dq)

    def table(j, member):
        plot = pl.ds(pl.multiple_of(plots[0, j] * PATCH, PATCH), PATCH)
        for h in range(heads):
            own = slice(h * DH, (h + 1) * DH)
            val = slice(hq + h * DH, hq + (h + 1) * DH)
            query = q_t[own, :]
            dmix = jnp.where(member, dm[own, :].astype(F32), 0.0).astype(BF16)
            level = jnp.where(member, lse[h : h + 1, :], -NEG)
            p = jnp.exp(nn(k_rows[h, plot, :], query) - level)
            dp = nn(v_rows[h, plot, :], dmix)
            inner = jnp.sum(p * dp, axis=0, keepdims=True)
            ds = (p * (dp - inner)).astype(BF16)
            dkv[own, plot] += nt(query, ds)
            dkv[val, plot] += nt(dmix, p.astype(BF16))
            dq[own, :] += nn(kv_t[own, plot], ds)

    tables_of_block(lengths, base, table)
    grad_query = (dq[...] * SCALE).astype(BF16)
    back = tn(grad_query, w[0:hq, :])
    grad_in[...] = back if leading else back + base_grad[...]
    if leading:
        dw_t[0:hq, :] += nn(grad_query, normed[...])
        dw_t[3 * hq : 4 * hq, :] += nn(mixed_t[...], branch)

    @pl.when(block == last)
    def _finish():
        for m in range(dkv.shape[1] // ROWS):
            here = slice(m * ROWS, (m + 1) * ROWS)
            rows = dkv[:, here].astype(BF16)
            back_mem = tn(rows, w[hq : 3 * hq, :])
            grad_mem[here, :] = back_mem if leading else back_mem + base_mem[here, :]
            if leading:
                dw_t[hq : 3 * hq, :] += nn(rows, memory[here, :])
        if leading:
            dw[...] = dw_t[...].T


def cross_backward(lengths, plots, w, q_t, lse, kv_t, k_rows, v_rows, heads, lead=None, follow=None):
    hq = heads * DH
    slots, width = q_t.shape[1], w.shape[1]
    count = kv_t.shape[1]
    outs = [
        (sds((slots, width), F32), by_rows(width)),
        (sds((count, width), F32), full((count, width))),
    ]
    scratch = [
        pltpu.VMEM((2 * hq, count), F32),
        pltpu.VMEM((hq, ROWS), F32),
        pltpu.VMEM((hq, ROWS), BF16),
    ]
    heads_part = [
        (lse, by_cols(8)),
        (kv_t, full(kv_t.shape)),
        (k_rows, full(k_rows.shape)),
        (v_rows, full(v_rows.shape)),
    ]
    if lead is not None:
        second, part, other, cot, gain, normed, memory, mixed_t = lead
        ins = [
            (lengths, SMEM),
            (plots, SMEM),
            (second, by_rows(width)),
            (part, by_rows(width)),
            (other, by_rows(width)),
            (cot, by_rows(width)),
            (gain, full(gain.shape)),
            (normed, by_rows(width)),
            (memory, full(memory.shape)),
            (w, full(w.shape)),
            (q_t, by_cols(hq)),
            (mixed_t, by_cols(hq)),
        ] + heads_part
        outs += [
            (sds((slots, width), F32), by_rows(width)),
            (sds((slots, width), BF16), by_rows(width)),
            (sds((8, width), F32), full((8, width))),
            (sds((width, 4 * hq), F32), full((width, 4 * hq))),
        ]
        scratch.append(pltpu.VMEM((4 * hq, width), F32))
    else:
        branch, base_grad, base_mem = follow
        ins = [
            (lengths, SMEM),
            (plots, SMEM),
            (branch, by_rows(width)),
            (w, full(w.shape)),
            (q_t, by_cols(hq)),
        ] + heads_part
        ins += [(base_grad, by_rows(width)), (base_mem, full(base_mem.shape))]
    flops = 2 * slots * width * hq * (8 if lead is not None else 4) + heads * 20 * slots * PATCH * DH
    return run(
        functools.partial(cross_backward_kernel, lead is not None, heads),
        slots // ROWS, ins, outs, scratch, flops, "cross_backward", heads * slots * PATCH * 2,
    )


def self_backward_kernel(leading, heads, *refs):
    hq = heads * DH
    if leading:
        (lengths, first, part, other, carried, gain, tokens, gain_in, w, qkv_t, mixed_t, lse) = refs[:12]
        (grad_in, grad_first, branch_out, grad_gain, dw) = refs[12:17]
        (dkv, k_rows, v_rows, dqkv, dw_t) = refs[17:]
    else:
        (lengths, branch_in, w, qkv_t, lse, base_grad) = refs[:6]
        (grad_in, dkv, k_rows, v_rows, dqkv) = refs[6:]
    step = pl.program_id(0)
    last = pl.num_programs(0) - 1
    block = last - step
    base = pl.multiple_of(block * ROWS, ROWS)
    here = pl.ds(base, ROWS)

    @pl.when(step == 0)
    def _start():
        dkv[...] = jnp.zeros_like(dkv)
        for h in range(heads):
            k_rows[h] = qkv_t[hq + h * DH : hq + (h + 1) * DH, :].T
            v_rows[h] = qkv_t[2 * hq + h * DH : 2 * hq + (h + 1) * DH, :].T
        if leading:
            dw_t[...] = jnp.zeros_like(dw_t)
            grad_gain[...] = jnp.zeros_like(grad_gain)

    if leading:
        grad_rows, gain_rows, _ = norm_vjp(first[...], gain[...], part[...] + other[...])
        total = carried[...] + grad_rows
        grad_first[...] = total
        branch = total.astype(BF16)
        branch_out[...] = branch
        grad_gain[0:1, :] += gain_rows
    else:
        branch = branch_in[...]
    dm_all = nt(w[3 * hq : 4 * hq, :], branch).astype(BF16)

    def attend(low, width):
        window = pl.ds(low, width)
        bias = self_bias(lengths, base, low, width)
        for h in range(heads):
            own = slice(h * DH, (h + 1) * DH)
            key = slice(hq + h * DH, hq + (h + 1) * DH)
            val = slice(hq + h * DH, hq + (h + 1) * DH)
            query = qkv_t[own, here]
            dmix = dm_all[own]
            p = jnp.exp(nn(k_rows[h, window, :], query) + bias - lse[h : h + 1, :])
            dp = nn(v_rows[h, window, :], dmix)
            inner = jnp.sum(p * dp, axis=0, keepdims=True)
            ds = (p * (dp - inner)).astype(BF16)
            dkv[own, window] += nt(query, ds)
            dkv[val, window] += nt(dmix, p.astype(BF16))
            dqkv[own, :] = (nn(qkv_t[key, window], ds) * SCALE).astype(BF16)

    window_cases(block, attend)
    dqkv[hq : 3 * hq, :] = dkv[:, here].astype(BF16)
    rows = dqkv[...]
    back = tn(rows, w[0 : 3 * hq, :])
    grad_in[...] = back if leading else back + base_grad[...]
    if leading:
        normed = normed_of(tokens[...].astype(F32), gain_in[...]).astype(BF16)
        dw_t[0 : 3 * hq, :] += nn(rows, normed)
        dw_t[3 * hq : 4 * hq, :] += nn(mixed_t[...], branch)

        @pl.when(step == last)
        def _finish():
            dw[...] = dw_t[...].T


def self_backward(lengths, w, qkv_t, lse, heads, lead=None, follow=None):
    hq = heads * DH
    slots, width = qkv_t.shape[1], w.shape[1]
    last = slots // ROWS - 1
    rows = pl.BlockSpec((ROWS, width), lambda i: (last - i, 0))

    def cols(height):
        return pl.BlockSpec((height, ROWS), lambda i: (0, last - i))

    outs = [(sds((slots, width), F32), rows)]
    scratch = [
        pltpu.VMEM((2 * hq, slots), F32),
        pltpu.VMEM((heads, slots, DH), BF16),
        pltpu.VMEM((heads, slots, DH), BF16),
        pltpu.VMEM((3 * hq, ROWS), BF16),
    ]
    if lead is not None:
        first, part, other, carried, gain, tokens, gain_in, mixed_t = lead
        ins = [
            (lengths, SMEM),
            (first, rows),
            (part, rows),
            (other, rows),
            (carried, rows),
            (gain, full(gain.shape)),
            (tokens, rows),
            (gain_in, full(gain_in.shape)),
            (w, full(w.shape)),
            (qkv_t, full(qkv_t.shape)),
            (mixed_t, cols(hq)),
            (lse, cols(8)),
        ]
        outs += [
            (sds((slots, width), F32), rows),
            (sds((slots, width), BF16), rows),
            (sds((8, width), F32), full((8, width))),
            (sds((width, 4 * hq), F32), full((width, 4 * hq))),
        ]
        scratch.append(pltpu.VMEM((4 * hq, width), F32))
    else:
        branch, base_grad = follow
        ins = [
            (lengths, SMEM),
            (branch, rows),
            (w, full(w.shape)),
            (qkv_t, full(qkv_t.shape)),
            (lse, cols(8)),
            (base_grad, rows),
        ]
    flops = 2 * slots * width * hq * (8 if lead is not None else 4) + heads * 10 * slots * slots * DH
    return run(
        functools.partial(self_backward_kernel, lead is not None, heads),
        slots // ROWS, ins, outs, scratch, flops, "self_backward", heads * slots * slots,
    )


def tail_kernel(tokens, part, other, carried, gain, grad_tokens, grad_gain):
    @pl.when(pl.program_id(0) == 0)
    def _zero():
        grad_gain[...] = jnp.zeros_like(grad_gain)

    grad_rows, gain_rows, _ = norm_vjp(tokens[...].astype(F32), gain[...], part[...] + other[...])
    grad_tokens[...] = carried[...] + grad_rows
    grad_gain[0:1, :] += gain_rows


def tail(tokens, part, other, carried, gain):
    slots, width = tokens.shape
    ins = [
        (tokens, by_rows(width)),
        (part, by_rows(width)),
        (other, by_rows(width)),
        (carried, by_rows(width)),
        (gain, full(gain.shape)),
    ]
    outs = [
        (sds((slots, width), F32), by_rows(width)),
        (sds((8, width), F32), full((8, width))),
    ]
    return run(tail_kernel, slots // ROWS, ins, outs, [], 20 * slots * width, "last_norm")


def swap(value, axis, bit):
    count = lax.axis_size(axis)
    return lax.ppermute(value, axis, [(i, i ^ bit) for i in range(count)])


def fetch_quarter(w, x, z):
    quarter = w.shape[0] // 4
    pieces = w.reshape(4, quarter, w.shape[1])
    mine = jnp.concatenate(
        [jnp.where(x == 0, pieces[0], pieces[1]), jnp.where(z == 0, pieces[2], pieces[3])], axis=0
    )
    by_y = swap(mine.astype(F32), "mp", 2)
    by_x = swap(by_y[:quarter], "dp", 1)
    by_z = swap(by_y[quarter:], "dp", 2)
    return by_y, by_x, by_z


def scatter_rows(grad):
    place = lax.axis_index("dp")
    count = lax.axis_size("dp")
    own_rows = grad.shape[0] // count
    width = grad.shape[1]
    bit = 1
    left = count
    while bit < count:
        mine = (place // bit) % 2
        halves = grad.reshape(left // 2, 2, own_rows, width)
        sent = lax.dynamic_index_in_dim(halves, 1 - mine, axis=1, keepdims=False)
        kept = lax.dynamic_index_in_dim(halves, mine, axis=1, keepdims=False)
        grad = (kept + swap(sent, "dp", bit)).reshape(left // 2 * own_rows, width)
        left //= 2
        bit *= 2
    return grad


def all_sum(value, axis):
    bit = 1
    while bit < lax.axis_size(axis):
        value = value + swap(value, axis, bit)
        bit *= 2
    return value


def adafactor(pieces, model_width, extra=None):
    ways = lax.axis_size("mp")
    row_sums = all_sum(jnp.stack([jnp.sum(g * g, axis=1) for g in pieces], axis=0), "mp")
    row_means = [
        row_sums[k] / (g.shape[1] * ways) + 1e-30 for k, g in enumerate(pieces)
    ]
    parts = [jnp.sum(g * g, axis=0) for g in pieces]
    parts.append(jnp.stack([jnp.sum(m) for m in row_means]))
    if extra is not None:
        parts.append(extra)
    summed = all_sum(jnp.concatenate(parts), "dp")
    steps = []
    at = 0
    tail_at = sum(g.shape[1] for g in pieces)
    for k, g in enumerate(pieces):
        col_mean = summed[at : at + g.shape[1]] / model_width + 1e-30
        at += g.shape[1]
        mean_rows = summed[tail_at + k] / model_width
        factor = row_means[k][:, None] * col_mean[None, :] / mean_rows
        steps.append(g * lax.rsqrt(factor))
    if extra is None:
        return steps
    return steps, summed[tail_at + len(pieces) :]


def on_device(
    tokens,
    memory,
    cotangent,
    table_lengths,
    table_plots,
    gains,
    w_qkv,
    w_self_out,
    w_cross_query,
    w_cross_kv,
    w_cross_out,
    w_gate_up,
    w_down,
):
    slots, width = tokens.shape
    hq = w_self_out.shape[1]
    heads = hq // DH
    units = w_down.shape[1]
    place = lax.axis_index("dp")
    x, z = place % 2, (place // 2) % 2
    ctl = jnp.stack([x, z]).astype(jnp.int32)
    gain_rows = gains.T
    gain_a, gain_b, gain_c = gain_rows[0:1], gain_rows[1:2], gain_rows[2:3]

    w_a = jnp.concatenate([w_qkv.transpose(1, 2, 0).reshape(3 * hq, width), w_self_out.T], axis=0)
    w_b = jnp.concatenate(
        [w_cross_query.T, w_cross_kv.transpose(1, 2, 0).reshape(2 * hq, width), w_cross_out.T], axis=0
    )
    w_f = jnp.concatenate(
        [w_gate_up.transpose(1, 2, 0).reshape(2 * units, width), w_down.T], axis=0
    )
    half_f = w_f.shape[0] // 2
    far_a = fetch_quarter(w_a, x, z)
    far_b = fetch_quarter(w_b, x, z)
    far_f = fetch_quarter(w_f[:half_f], x, z) + fetch_quarter(w_f[half_f:], x, z)

    qkv0, mixed_a0, lse_a0, part = self_forward(table_lengths, tokens, gain_a, w_a, heads)
    kv0, k0, v0 = memory_forward(memory, w_b, heads)
    qkv1, mixed_a1, lse_a1, part, w_a1 = self_forward(
        table_lengths, tokens, gain_a, None, heads, remote=(ctl,) + far_a + (part,)
    )
    kv1, k1, v1, w_b1 = memory_forward(memory, None, heads, remote=(ctl,) + far_b)
    q0, mixed_b0, lse_b0, part, first, normed_b = cross_forward(
        table_lengths, table_plots, w_b, kv0, k0, heads,
        lead=(tokens, part, swap(part, "mp", 1), gain_b),
    )
    q1, mixed_b1, lse_b1, part = cross_forward(
        table_lengths, table_plots, w_b1, kv1, k1, heads, follow=(normed_b, part)
    )
    res, back, second, normed_c, grad_f = feed(
        units, lead=(first, part, swap(part, "mp", 1), gain_c, cotangent, w_f)
    )
    res, back = feed(units, follow=(ctl, normed_c, cotangent, far_f, res, back))
    back_other = swap(back, "mp", 1)
    layer_out = (second + (res + swap(res, "mp", 1))).astype(BF16)

    grad_f = scatter_rows(grad_f)
    back, back_mem, grad_second, branch_b, gain_grad_c, grad_b = cross_backward(
        table_lengths, table_plots, w_b, q0, lse_b0, kv0, k0, v0, heads,
        lead=(second, back, back_other, cotangent, gain_c, normed_b, memory, mixed_b0),
    )
    back, back_mem = cross_backward(
        table_lengths, table_plots, w_b1, q1, lse_b1, kv1, k1, v1, heads,
        follow=(branch_b, back, back_mem),
    )
    back_other = swap(back, "mp", 1)
    grad_memory = back_mem + swap(back_mem, "mp", 1)
    grad_b = scatter_rows(grad_b)
    back, grad_first, branch_a, gain_grad_b, grad_a = self_backward(
        table_lengths, w_a, qkv0, lse_a0, heads,
        lead=(first, back, back_other, grad_second, gain_b, tokens, gain_a, mixed_a0),
    )
    grad_a = scatter_rows(grad_a)
    (back,) = self_backward(table_lengths, w_a1, qkv1, lse_a1, heads, follow=(branch_a, back))
    grad_tokens, gain_grad_a = tail(tokens, back, swap(back, "mp", 1), grad_first, gain_a)

    early = [
        grad_f[:, : 2 * units],
        grad_f[:, 2 * units :],
        grad_b[:, :hq],
        grad_b[:, hq : 3 * hq],
        grad_b[:, 3 * hq :],
    ]
    steps_early = adafactor(early, width)
    late = [grad_a[:, : 3 * hq], grad_a[:, 3 * hq :]]
    gain_parts = jnp.concatenate([gain_grad_a[0], gain_grad_b[0], gain_grad_c[0]])
    steps_late, gain_sum = adafactor(late, width, gain_parts)
    own_rows = grad_f.shape[0]
    grad_gains = lax.dynamic_slice_in_dim(gain_sum.reshape(3, width), place * own_rows, own_rows, axis=1).T

    def qkv_shape(g):
        return g.reshape(own_rows, 3, hq)

    def kv_shape(g):
        return g.reshape(own_rows, 2, hq)

    def gu_shape(g):
        return g.reshape(own_rows, 2, units)

    return (
        layer_out,
        grad_tokens,
        grad_memory,
        grad_gains,
        qkv_shape(late[0]),
        late[1],
        early[2],
        kv_shape(early[3]),
        early[4],
        gu_shape(early[0]),
        early[1],
        qkv_shape(steps_late[0]),
        steps_late[1],
        steps_early[2],
        kv_shape(steps_early[3]),
        steps_early[4],
        gu_shape(steps_early[0]),
        steps_early[1],
    )


def solution(mesh):
    split = P("dp", None)
    cols = P(None, "mp")
    cols3 = P(None, None, "mp")
    both = P("dp", "mp")
    both3 = P("dp", None, "mp")
    return jax.shard_map(
        on_device,
        mesh=mesh,
        in_specs=(
            split, split, split, split, split, P(),
            cols3, cols, cols, cols3, cols, cols3, cols,
        ),
        out_specs=(
            split, split, split, split,
            both3, both, both, both3, both, both3, both,
            both3, both, both, both3, both, both3, both,
        ),
        check_vma=False,
    )
```

```python
import functools
import math

import jax
import jax.numpy as jnp
from jax import lax
from jax.experimental import pallas as pl
from jax.experimental.pallas import tpu as pltpu
from jax.sharding import PartitionSpec as P

DH = 64
PATCH = 256
LONGEST = 512
ROWS = 256
SPAN = LONGEST // ROWS
F32 = jnp.float32
BF16 = jnp.bfloat16
NEG = -1e30
SCALE = 1.0 / math.sqrt(DH)
VMEM_BYTES = 56 * 1024 * 1024


def nn(a, b):
    return lax.dot_general(a, b, (((1,), (0,)), ((), ())), preferred_element_type=F32)


def nt(a, b):
    return lax.dot_general(a, b, (((1,), (1,)), ((), ())), preferred_element_type=F32)


def tn(a, b):
    return lax.dot_general(a, b, (((0,), (0,)), ((), ())), preferred_element_type=F32)


def normed_of(rows, gain):
    return rows * lax.rsqrt(jnp.mean(rows * rows, axis=-1, keepdims=True) + 1e-06) * gain


def norm_vjp(rows, gain, grad):
    inv = lax.rsqrt(jnp.mean(rows * rows, axis=-1, keepdims=True) + 1e-06)
    scaled = rows * inv
    hg = grad * gain
    inner = jnp.mean(hg * scaled, axis=-1, keepdims=True)
    grad_rows = inv * (hg - scaled * inner)
    grad_gain = jnp.sum(grad * scaled, axis=0, keepdims=True)
    return grad_rows, grad_gain, scaled


def place_pieces(dst, base, ctl, by_y, by_x, by_z):
    q = by_x.shape[0]
    x, z = ctl[0], ctl[1]

    def at(offset):
        return pl.ds(pl.multiple_of(offset, 64), q)

    dst[at(base + x * q), :] = by_y[:q, :].astype(BF16)
    dst[at(base + (1 - x) * q), :] = by_x[...].astype(BF16)
    dst[at(base + (2 + z) * q), :] = by_y[q:, :].astype(BF16)
    dst[at(base + (3 - z) * q), :] = by_z[...].astype(BF16)


def table_ends(lengths):
    ends = []
    total = lengths[0, 0]
    for j in range(1, lengths.shape[1]):
        ends.append(total)
        total = total + lengths[0, j]
    return ends


def query_places(base):
    return lax.broadcasted_iota(jnp.int32, (1, ROWS), 1) + base


def self_bias(lengths, base, low, width):
    places = query_places(base)
    start = jnp.zeros_like(places)
    for end in table_ends(lengths):
        start = jnp.where(places >= end, end, start)
    keys = lax.broadcasted_iota(jnp.int32, (width, ROWS), 0) + low
    return jnp.where((keys >= start) & (keys <= places), 0.0, NEG)


def window_cases(block, body):
    for back in range(SPAN + 1):
        width = (back + 1) * ROWS

        @pl.when(block == back if back < SPAN else block >= SPAN)
        def _run(back=back, width=width):
            if back < SPAN:
                body(0, width)
            else:
                body(pl.multiple_of((block - SPAN) * ROWS, ROWS), width)


def full(shape):
    return pl.BlockSpec(shape, lambda i: (0,) * len(shape))


def by_rows(width):
    return pl.BlockSpec((ROWS, width), lambda i: (i, 0))


def by_cols(height):
    return pl.BlockSpec((height, ROWS), lambda i: (0, i))


SMEM = pl.BlockSpec(memory_space=pltpu.SMEM)


def run(kernel, grid, ins, outs, scratch, flops, name, transcendentals=0):
    arrays = [a for a, _ in ins]
    moved = sum(a.size * a.dtype.itemsize for a in arrays) + sum(
        math.prod(s.shape) * jnp.dtype(s.dtype).itemsize for s, _ in outs
    )
    return pl.pallas_call(
        kernel,
        grid=(grid,),
        in_specs=[s for _, s in ins],
        out_specs=[s for _, s in outs],
        out_shape=[s for s, _ in outs],
        scratch_shapes=scratch,
        compiler_params=pltpu.CompilerParams(
            vmem_limit_bytes=VMEM_BYTES, dimension_semantics=("arbitrary",)
        ),
        cost_estimate=pl.CostEstimate(
            flops=flops // 64, bytes_accessed=moved // 64, transcendentals=transcendentals // 64
        ),
        name=name,
    )(*arrays)


def sds(shape, dtype):
    return jax.ShapeDtypeStruct(shape, dtype)


def self_forward_kernel(remote, heads, *refs):
    if remote:
        (lengths, ctl, tokens, gain, by_y, by_x, by_z, base_out) = refs[:8]
        (qkv_t, mixed_t, lse, out, w_out, k_rows) = refs[8:]
        w = w_out
    else:
        (lengths, tokens, gain, w) = refs[:4]
        (qkv_t, mixed_t, lse, out, k_rows) = refs[4:]
    block = pl.program_id(0)
    hq = heads * DH
    if remote:

        @pl.when(block == 0)
        def _place():
            place_pieces(w, 0, ctl, by_y, by_x, by_z)

    base = pl.multiple_of(block * ROWS, ROWS)
    here = pl.ds(base, ROWS)
    normed = normed_of(tokens[...].astype(F32), gain[...]).astype(BF16)
    qkv = nt(w[0 : 3 * hq, :], normed).astype(BF16)
    q_all = (qkv[:hq].astype(F32) * SCALE).astype(BF16)
    qkv_t[0:hq, here] = q_all
    qkv_t[hq : 3 * hq, here] = qkv[hq:]
    for h in range(heads):
        k_rows[h, here, :] = qkv[hq + h * DH : hq + (h + 1) * DH].T

    def attend(low, width):
        window = pl.ds(low, width)
        bias = self_bias(lengths, base, low, width)
        for h in range(heads):
            own = slice(h * DH, (h + 1) * DH)
            s = nn(k_rows[h, window, :], q_all[own]) + bias
            top = jnp.max(s, axis=0, keepdims=True)
            e = jnp.exp(s - top)
            total = jnp.sum(e, axis=0, keepdims=True)
            o = nn(qkv_t[2 * hq + h * DH : 2 * hq + (h + 1) * DH, window], e.astype(BF16))
            mixed_t[own, :] = (o * (1.0 / total)).astype(BF16)
            lse[h : h + 1, :] = top + jnp.log(total)

    window_cases(block, attend)
    part = tn(mixed_t[...], w[3 * hq : 4 * hq, :])
    out[...] = part + base_out[...] if remote else part


def self_forward(lengths, tokens, gain, w, heads, remote=None):
    slots, width = tokens.shape
    hq = heads * DH
    outs = [
        (sds((3 * hq, slots), BF16), full((3 * hq, slots))),
        (sds((hq, slots), BF16), by_cols(hq)),
        (sds((8, slots), F32), by_cols(8)),
        (sds((slots, width), F32), by_rows(width)),
    ]
    scratch = [pltpu.VMEM((heads, slots, DH), BF16)]
    if remote is None:
        ins = [(lengths, SMEM), (tokens, by_rows(width)), (gain, full(gain.shape)), (w, full(w.shape))]
    else:
        ctl, by_y, by_x, by_z, base_out = remote
        ins = [
            (lengths, SMEM),
            (ctl, SMEM),
            (tokens, by_rows(width)),
            (gain, full(gain.shape)),
            (by_y, full(by_y.shape)),
            (by_x, full(by_x.shape)),
            (by_z, full(by_z.shape)),
            (base_out, by_rows(width)),
        ]
        outs.append((sds((4 * hq, width), BF16), full((4 * hq, width))))
    flops = 2 * slots * width * 4 * hq + heads * 4 * slots * slots * DH
    return run(
        functools.partial(self_forward_kernel, remote is not None, heads),
        slots // ROWS, ins, outs, scratch, flops, "self_forward", heads * slots * slots,
    )


def memory_kernel(remote, heads, *refs):
    hq = heads * DH
    if remote:
        ctl, memory, by_y, by_x, by_z, kv_t, k_rows, v_rows, w = refs

        @pl.when(pl.program_id(0) == 0)
        def _place():
            place_pieces(w, 0, ctl, by_y, by_x, by_z)
    else:
        memory, w, kv_t, k_rows, v_rows = refs
    kv = nt(w[hq : 3 * hq, :], memory[...]).astype(BF16)
    kv_t[...] = kv
    for h in range(heads):
        k_rows[h] = kv[h * DH : (h + 1) * DH].T
        v_rows[h] = kv[hq + h * DH : hq + (h + 1) * DH].T


def memory_forward(memory, w, heads, remote=None):
    count, width = memory.shape
    hq = heads * DH
    head_rows = pl.BlockSpec((heads, ROWS, DH), lambda i: (0, i, 0))
    outs = [
        (sds((2 * hq, count), BF16), by_cols(2 * hq)),
        (sds((heads, count, DH), BF16), head_rows),
        (sds((heads, count, DH), BF16), head_rows),
    ]
    if remote is None:
        ins = [(memory, by_rows(width)), (w, full(w.shape))]
    else:
        ctl, by_y, by_x, by_z = remote
        ins = [
            (ctl, SMEM),
            (memory, by_rows(width)),
            (by_y, full(by_y.shape)),
            (by_x, full(by_x.shape)),
            (by_z, full(by_z.shape)),
        ]
        outs.append((sds((4 * hq, width), BF16), full((4 * hq, width))))
    return run(
        functools.partial(memory_kernel, remote is not None, heads),
        count // ROWS, ins, outs, [], 2 * count * width * 2 * hq, "memory_forward",
    )


def tables_of_block(lengths, base, body):
    ends = table_ends(lengths)
    places = query_places(base)
    segment = jnp.zeros_like(places)
    first_table = jnp.int32(0)
    last_table = jnp.int32(0)
    for end in ends:
        segment = segment + (places >= end).astype(jnp.int32)
        first_table = first_table + (base >= end).astype(jnp.int32)
        last_table = last_table + (base + ROWS - 1 >= end).astype(jnp.int32)

    def step(table, carry):
        body(table, segment == table)
        return carry

    lax.fori_loop(first_table, last_table + 1, step, 0)


def cross_forward_kernel(leading, heads, *refs):
    hq = heads * DH
    if leading:
        (lengths, plots, tokens, part, other, gain, w, kv_t, k_rows) = refs[:9]
        (q_t, mixed_t, lse, out, first, normed_out) = refs[9:]
        rows = tokens[...].astype(F32) + (part[...] + other[...])
        first[...] = rows
        normed = normed_of(rows, gain[...]).astype(BF16)
        normed_out[...] = normed
    else:
        (lengths, plots, normed_in, w, kv_t, k_rows, base_out) = refs[:7]
        (q_t, mixed_t, lse, out) = refs[7:]
        normed = normed_in[...]
    base = pl.multiple_of(pl.program_id(0) * ROWS, ROWS)
    query = nt(w[0:hq, :], normed).astype(BF16)
    q_all = (query.astype(F32) * SCALE).astype(BF16)
    q_t[...] = q_all

    def table(j, member):
        plot = pl.ds(pl.multiple_of(plots[0, j] * PATCH, PATCH), PATCH)
        for h in range(heads):
            own = slice(h * DH, (h + 1) * DH)
            s = nn(k_rows[h, plot, :], q_t[own, :])
            top = jnp.max(s, axis=0, keepdims=True)
            e = jnp.exp(s - top)
            total = jnp.sum(e, axis=0, keepdims=True)
            o = nn(kv_t[hq + h * DH : hq + (h + 1) * DH, plot], e.astype(BF16))
            o = o * (1.0 / total)
            mixed_t[own, :] = jnp.where(member, o, mixed_t[own, :].astype(F32)).astype(BF16)
            lse[h : h + 1, :] = jnp.where(member, top + jnp.log(total), lse[h : h + 1, :])

    tables_of_block(lengths, base, table)
    part_out = tn(mixed_t[...], w[3 * hq : 4 * hq, :])
    out[...] = part_out if leading else part_out + base_out[...]


def cross_forward(lengths, plots, w, kv_t, k_rows, heads, lead=None, follow=None):
    hq = heads * DH
    slots = (lead or follow)[0].shape[0]
    width = w.shape[1]
    outs = [
        (sds((hq, slots), BF16), by_cols(hq)),
        (sds((hq, slots), BF16), by_cols(hq)),
        (sds((8, slots), F32), by_cols(8)),
        (sds((slots, width), F32), by_rows(width)),
    ]
    shared = [(w, full(w.shape)), (kv_t, full(kv_t.shape)), (k_rows, full(k_rows.shape))]
    if lead is not None:
        tokens, part, other, gain = lead
        ins = [
            (lengths, SMEM),
            (plots, SMEM),
            (tokens, by_rows(width)),
            (part, by_rows(width)),
            (other, by_rows(width)),
            (gain, full(gain.shape)),
        ] + shared
        outs += [
            (sds((slots, width), F32), by_rows(width)),
            (sds((slots, width), BF16), by_rows(width)),
        ]
    else:
        normed, base_out = follow
        ins = [(lengths, SMEM), (plots, SMEM), (normed, by_rows(width))] + shared
        ins.append((base_out, by_rows(width)))
    flops = 2 * slots * width * 2 * hq + heads * 8 * slots * PATCH * DH
    return run(
        functools.partial(cross_forward_kernel, lead is not None, heads),
        slots // ROWS, ins, outs, [], flops, "cross_forward", heads * slots * PATCH * 2,
    )


def feed_kernel(leading, units, *refs):
    if leading:
        (first, part, other, gain, cot, w) = refs[:6]
        (result, grad_in, second, normed_out, dw) = refs[6:]
        rows = first[...] + (part[...] + other[...])
        second[...] = rows
        normed = normed_of(rows, gain[...]).astype(BF16)
        normed_out[...] = normed

        @pl.when(pl.program_id(0) == 0)
        def _zero():
            dw[...] = jnp.zeros_like(dw)
    else:
        (ctl, normed_in, cot, y0, x0, z0, y1, x1, z1, base_result, base_grad) = refs[:11]
        (result, grad_in, w) = refs[11:]
        normed = normed_in[...]

        @pl.when(pl.program_id(0) == 0)
        def _place():
            place_pieces(w, 0, ctl, y0, x0, z0)
            place_pieces(w, 4 * x0.shape[0], ctl, y1, x1, z1)

    cot_rows = cot[...]
    gate_up = nt(normed, w[0 : 2 * units, :])
    gate, up = gate_up[:, :units], gate_up[:, units:]
    c0 = math.sqrt(2.0 / math.pi)
    square = gate * gate
    th = jnp.tanh(c0 * gate * (1.0 + 0.044715 * square))
    half = 0.5 * (1.0 + th)
    gelu = gate * half
    slope = half + (0.5 * c0) * gate * (1.0 - th * th) * (1.0 + (3 * 0.044715) * square)
    hidden = (gelu * up).astype(BF16)
    res = nn(hidden, w[2 * units : 3 * units, :])
    grad_hidden = nt(cot_rows, w[2 * units : 3 * units, :])
    grad_gate = (grad_hidden * up * slope).astype(BF16)
    grad_up = (grad_hidden * gelu).astype(BF16)
    back = nn(grad_gate, w[0:units, :]) + nn(grad_up, w[units : 2 * units, :])
    if leading:
        result[...] = res
        grad_in[...] = back
        dw[:, 0:units] += tn(normed, grad_gate)
        dw[:, units : 2 * units] += tn(normed, grad_up)
        dw[:, 2 * units : 3 * units] += tn(cot_rows, hidden)
    else:
        result[...] = res + base_result[...]
        grad_in[...] = back + base_grad[...]


def feed(units, lead=None, follow=None):
    if lead is not None:
        first, part, other, gain, cot, w = lead
        slots, width = first.shape
        ins = [
            (first, by_rows(width)),
            (part, by_rows(width)),
            (other, by_rows(width)),
            (gain, full(gain.shape)),
            (cot, by_rows(width)),
            (w, full(w.shape)),
        ]
    else:
        ctl, normed, cot, pieces, base_result, base_grad = follow
        slots, width = normed.shape
        ins = [(ctl, SMEM), (normed, by_rows(width)), (cot, by_rows(width))]
        ins += [(piece, full(piece.shape)) for piece in pieces]
        ins += [(base_result, by_rows(width)), (base_grad, by_rows(width))]
    outs = [
        (sds((slots, width), F32), by_rows(width)),
        (sds((slots, width), F32), by_rows(width)),
    ]
    scratch = []
    if lead is not None:
        outs += [
            (sds((slots, width), F32), by_rows(width)),
            (sds((slots, width), BF16), by_rows(width)),
            (sds((width, 3 * units), F32), full((width, 3 * units))),
        ]
    else:
        scratch = [pltpu.VMEM((3 * units, width), BF16)]
    flops = 2 * slots * width * units * (9 if lead is not None else 6)
    return run(
        functools.partial(feed_kernel, lead is not None, units),
        slots // ROWS, ins, outs, scratch, flops, "feed", slots * units,
    )


def cross_backward_kernel(leading, heads, *refs):
    hq = heads * DH
    if leading:
        (lengths, plots, second, part, other, cot, gain, normed, memory) = refs[:9]
        (w, q_t, mixed_t, lse, kv_t, k_rows, v_rows) = refs[9:16]
        (grad_in, grad_mem, grad_second, branch_out, grad_gain, dw) = refs[16:22]
        (dkv, dq, dm, dw_t) = refs[22:]
    else:
        (lengths, plots, branch_in, w, q_t, lse, kv_t, k_rows, v_rows, base_grad, base_mem) = refs[:11]
        (grad_in, grad_mem, dkv, dq, dm) = refs[11:]
    block = pl.program_id(0)
    last = pl.num_programs(0) - 1
    base = pl.multiple_of(block * ROWS, ROWS)

    @pl.when(block == 0)
    def _zero():
        dkv[...] = jnp.zeros_like(dkv)
        if leading:
            dw_t[...] = jnp.zeros_like(dw_t)
            grad_gain[...] = jnp.zeros_like(grad_gain)

    if leading:
        grad_rows, gain_rows, _ = norm_vjp(second[...], gain[...], part[...] + other[...])
        total = cot[...].astype(F32) + grad_rows
        grad_second[...] = total
        branch = total.astype(BF16)
        branch_out[...] = branch
        grad_gain[0:1, :] += gain_rows
    else:
        branch = branch_in[...]
    dm[...] = nt(w[3 * hq : 4 * hq, :], branch).astype(BF16)
    dq[...] = jnp.zeros_like(dq)

    def table(j, member):
        plot = pl.ds(pl.multiple_of(plots[0, j] * PATCH, PATCH), PATCH)
        for h in range(heads):
            own = slice(h * DH, (h + 1) * DH)
            val = slice(hq + h * DH, hq + (h + 1) * DH)
            query = q_t[own, :]
            dmix = jnp.where(member, dm[own, :].astype(F32), 0.0).astype(BF16)
            level = jnp.where(member, lse[h : h + 1, :], -NEG)
            p = jnp.exp(nn(k_rows[h, plot, :], query) - level)
            dp = nn(v_rows[h, plot, :], dmix)
            inner = jnp.sum(p * dp, axis=0, keepdims=True)
            ds = (p * (dp - inner)).astype(BF16)
            dkv[own, plot] += nt(query, ds)
            dkv[val, plot] += nt(dmix, p.astype(BF16))
            dq[own, :] += nn(kv_t[own, plot], ds)

    tables_of_block(lengths, base, table)
    grad_query = (dq[...] * SCALE).astype(BF16)
    back = tn(grad_query, w[0:hq, :])
    grad_in[...] = back if leading else back + base_grad[...]
    if leading:
        dw_t[0:hq, :] += nn(grad_query, normed[...])
        dw_t[3 * hq : 4 * hq, :] += nn(mixed_t[...], branch)

    @pl.when(block == last)
    def _finish():
        for m in range(dkv.shape[1] // ROWS):
            here = slice(m * ROWS, (m + 1) * ROWS)
            rows = dkv[:, here].astype(BF16)
            back_mem = tn(rows, w[hq : 3 * hq, :])
            grad_mem[here, :] = back_mem if leading else back_mem + base_mem[here, :]
            if leading:
                dw_t[hq : 3 * hq, :] += nn(rows, memory[here, :])
        if leading:
            dw[...] = dw_t[...].T


def cross_backward(lengths, plots, w, q_t, lse, kv_t, k_rows, v_rows, heads, lead=None, follow=None):
    hq = heads * DH
    slots, width = q_t.shape[1], w.shape[1]
    count = kv_t.shape[1]
    outs = [
        (sds((slots, width), F32), by_rows(width)),
        (sds((count, width), F32), full((count, width))),
    ]
    scratch = [
        pltpu.VMEM((2 * hq, count), F32),
        pltpu.VMEM((hq, ROWS), F32),
        pltpu.VMEM((hq, ROWS), BF16),
    ]
    heads_part = [
        (lse, by_cols(8)),
        (kv_t, full(kv_t.shape)),
        (k_rows, full(k_rows.shape)),
        (v_rows, full(v_rows.shape)),
    ]
    if lead is not None:
        second, part, other, cot, gain, normed, memory, mixed_t = lead
        ins = [
            (lengths, SMEM),
            (plots, SMEM),
            (second, by_rows(width)),
            (part, by_rows(width)),
            (other, by_rows(width)),
            (cot, by_rows(width)),
            (gain, full(gain.shape)),
            (normed, by_rows(width)),
            (memory, full(memory.shape)),
            (w, full(w.shape)),
            (q_t, by_cols(hq)),
            (mixed_t, by_cols(hq)),
        ] + heads_part
        outs += [
            (sds((slots, width), F32), by_rows(width)),
            (sds((slots, width), BF16), by_rows(width)),
            (sds((8, width), F32), full((8, width))),
            (sds((width, 4 * hq), F32), full((width, 4 * hq))),
        ]
        scratch.append(pltpu.VMEM((4 * hq, width), F32))
    else:
        branch, base_grad, base_mem = follow
        ins = [
            (lengths, SMEM),
            (plots, SMEM),
            (branch, by_rows(width)),
            (w, full(w.shape)),
            (q_t, by_cols(hq)),
        ] + heads_part
        ins += [(base_grad, by_rows(width)), (base_mem, full(base_mem.shape))]
    flops = 2 * slots * width * hq * (8 if lead is not None else 4) + heads * 20 * slots * PATCH * DH
    return run(
        functools.partial(cross_backward_kernel, lead is not None, heads),
        slots // ROWS, ins, outs, scratch, flops, "cross_backward", heads * slots * PATCH * 2,
    )


def self_backward_kernel(leading, heads, *refs):
    hq = heads * DH
    if leading:
        (lengths, first, part, other, carried, gain, tokens, gain_in, w, qkv_t, mixed_t, lse) = refs[:12]
        (grad_in, grad_first, branch_out, grad_gain, dw) = refs[12:17]
        (dkv, k_rows, v_rows, dqkv, dw_t) = refs[17:]
    else:
        (lengths, branch_in, w, qkv_t, lse, base_grad) = refs[:6]
        (grad_in, dkv, k_rows, v_rows, dqkv) = refs[6:]
    step = pl.program_id(0)
    last = pl.num_programs(0) - 1
    block = last - step
    base = pl.multiple_of(block * ROWS, ROWS)
    here = pl.ds(base, ROWS)

    @pl.when(step == 0)
    def _start():
        dkv[...] = jnp.zeros_like(dkv)
        for h in range(heads):
            k_rows[h] = qkv_t[hq + h * DH : hq + (h + 1) * DH, :].T
            v_rows[h] = qkv_t[2 * hq + h * DH : 2 * hq + (h + 1) * DH, :].T
        if leading:
            dw_t[...] = jnp.zeros_like(dw_t)
            grad_gain[...] = jnp.zeros_like(grad_gain)

    if leading:
        grad_rows, gain_rows, _ = norm_vjp(first[...], gain[...], part[...] + other[...])
        total = carried[...] + grad_rows
        grad_first[...] = total
        branch = total.astype(BF16)
        branch_out[...] = branch
        grad_gain[0:1, :] += gain_rows
    else:
        branch = branch_in[...]
    dm_all = nt(w[3 * hq : 4 * hq, :], branch).astype(BF16)

    def attend(low, width):
        window = pl.ds(low, width)
        bias = self_bias(lengths, base, low, width)
        for h in range(heads):
            own = slice(h * DH, (h + 1) * DH)
            key = slice(hq + h * DH, hq + (h + 1) * DH)
            val = slice(hq + h * DH, hq + (h + 1) * DH)
            query = qkv_t[own, here]
            dmix = dm_all[own]
            p = jnp.exp(nn(k_rows[h, window, :], query) + bias - lse[h : h + 1, :])
            dp = nn(v_rows[h, window, :], dmix)
            inner = jnp.sum(p * dp, axis=0, keepdims=True)
            ds = (p * (dp - inner)).astype(BF16)
            dkv[own, window] += nt(query, ds)
            dkv[val, window] += nt(dmix, p.astype(BF16))
            dqkv[own, :] = (nn(qkv_t[key, window], ds) * SCALE).astype(BF16)

    window_cases(block, attend)
    dqkv[hq : 3 * hq, :] = dkv[:, here].astype(BF16)
    rows = dqkv[...]
    back = tn(rows, w[0 : 3 * hq, :])
    grad_in[...] = back if leading else back + base_grad[...]
    if leading:
        normed = normed_of(tokens[...].astype(F32), gain_in[...]).astype(BF16)
        dw_t[0 : 3 * hq, :] += nn(rows, normed)
        dw_t[3 * hq : 4 * hq, :] += nn(mixed_t[...], branch)

        @pl.when(step == last)
        def _finish():
            dw[...] = dw_t[...].T


def self_backward(lengths, w, qkv_t, lse, heads, lead=None, follow=None):
    hq = heads * DH
    slots, width = qkv_t.shape[1], w.shape[1]
    last = slots // ROWS - 1
    rows = pl.BlockSpec((ROWS, width), lambda i: (last - i, 0))

    def cols(height):
        return pl.BlockSpec((height, ROWS), lambda i: (0, last - i))

    outs = [(sds((slots, width), F32), rows)]
    scratch = [
        pltpu.VMEM((2 * hq, slots), F32),
        pltpu.VMEM((heads, slots, DH), BF16),
        pltpu.VMEM((heads, slots, DH), BF16),
        pltpu.VMEM((3 * hq, ROWS), BF16),
    ]
    if lead is not None:
        first, part, other, carried, gain, tokens, gain_in, mixed_t = lead
        ins = [
            (lengths, SMEM),
            (first, rows),
            (part, rows),
            (other, rows),
            (carried, rows),
            (gain, full(gain.shape)),
            (tokens, rows),
            (gain_in, full(gain_in.shape)),
            (w, full(w.shape)),
            (qkv_t, full(qkv_t.shape)),
            (mixed_t, cols(hq)),
            (lse, cols(8)),
        ]
        outs += [
            (sds((slots, width), F32), rows),
            (sds((slots, width), BF16), rows),
            (sds((8, width), F32), full((8, width))),
            (sds((width, 4 * hq), F32), full((width, 4 * hq))),
        ]
        scratch.append(pltpu.VMEM((4 * hq, width), F32))
    else:
        branch, base_grad = follow
        ins = [
            (lengths, SMEM),
            (branch, rows),
            (w, full(w.shape)),
            (qkv_t, full(qkv_t.shape)),
            (lse, cols(8)),
            (base_grad, rows),
        ]
    flops = 2 * slots * width * hq * (8 if lead is not None else 4) + heads * 10 * slots * slots * DH
    return run(
        functools.partial(self_backward_kernel, lead is not None, heads),
        slots // ROWS, ins, outs, scratch, flops, "self_backward", heads * slots * slots,
    )


def tail_kernel(tokens, part, other, carried, gain, grad_tokens, grad_gain):
    @pl.when(pl.program_id(0) == 0)
    def _zero():
        grad_gain[...] = jnp.zeros_like(grad_gain)

    grad_rows, gain_rows, _ = norm_vjp(tokens[...].astype(F32), gain[...], part[...] + other[...])
    grad_tokens[...] = carried[...] + grad_rows
    grad_gain[0:1, :] += gain_rows


def tail(tokens, part, other, carried, gain):
    slots, width = tokens.shape
    ins = [
        (tokens, by_rows(width)),
        (part, by_rows(width)),
        (other, by_rows(width)),
        (carried, by_rows(width)),
        (gain, full(gain.shape)),
    ]
    outs = [
        (sds((slots, width), F32), by_rows(width)),
        (sds((8, width), F32), full((8, width))),
    ]
    return run(tail_kernel, slots // ROWS, ins, outs, [], 20 * slots * width, "last_norm")


def swap(value, axis, bit):
    count = lax.axis_size(axis)
    return lax.ppermute(value, axis, [(i, i ^ bit) for i in range(count)])


def after(value, *others):
    return lax.optimization_barrier((value,) + others)[0]


def y_pieces(w, x, z):
    quarter = w.shape[0] // 4
    pieces = w.reshape(4, quarter, w.shape[1])
    mine = jnp.concatenate(
        [jnp.where(x == 0, pieces[0], pieces[1]), jnp.where(z == 0, pieces[2], pieces[3])], axis=0
    )
    return mine.astype(F32)


def hand_on(by_y):
    quarter = by_y.shape[0] // 2
    return swap(by_y[:quarter], "dp", 1), swap(by_y[quarter:], "dp", 2)


def together(*values):
    return lax.optimization_barrier(values)


class Halving:
    def __init__(self, grad, order):
        self.count = lax.axis_size("dp")
        self.place = lax.axis_index("dp")
        self.order = list(order)
        bit = 8
        while bit < self.count:
            self.order.append(bit)
            bit *= 2
        self.left = [b for b in (1 << k for k in range(self.count.bit_length() - 1))][::-1]
        self.grad = grad.reshape((2,) * len(self.left) + (grad.shape[0] // self.count, grad.shape[1]))

    def send(self):
        bit = self.order.pop(0)
        axis = self.left.index(bit)
        self.left.pop(axis)
        mine = (self.place // bit) % 2
        sent = lax.dynamic_index_in_dim(self.grad, 1 - mine, axis=axis, keepdims=False)
        self.kept = lax.dynamic_index_in_dim(self.grad, mine, axis=axis, keepdims=False)
        return sent, bit

    def start(self, *others):
        sent, bit = self.send()
        shape = sent.shape
        flat = sent.reshape(-1, shape[-1])
        if others:
            flat = after(flat, *others)
        self.got = swap(flat, "dp", bit)

    def finish(self):
        self.grad = self.kept + self.got.reshape(self.kept.shape)

    def rest(self):
        while self.order:
            self.start()
            self.finish()
        return self.grad.reshape(-1, self.grad.shape[-1])


def all_sum(value, axis):
    bit = 1
    while bit < lax.axis_size(axis):
        value = value + swap(value, axis, bit)
        bit *= 2
    return value


def lane_pick(width, edges, values):
    lanes = lax.broadcasted_iota(jnp.int32, (1, width), 1)
    picked = values[-1]
    for edge, value in zip(edges[-2::-1], values[-2::-1]):
        picked = jnp.where(lanes < edge, value, picked)
    return picked


def groups_of(hq, units):
    return (
        ((2 * units, 3 * units), (0, 1)),
        ((hq, 3 * hq, 4 * hq), (2, 3, 4)),
        ((3 * hq, 4 * hq), (5, 6)),
    )


def square_sums_kernel(groups, grad_f, grad_b, grad_a0, grad_a1, rows, cols):
    whole = (grad_f[...], grad_b[...], jnp.concatenate([grad_a0[...], grad_a1[...]], axis=1))
    places = lax.broadcasted_iota(jnp.int32, (1, rows.shape[1]), 1)
    sums = jnp.zeros(rows.shape, F32)
    at = 0
    for grad, (edges, names) in zip(whole, groups):
        square = grad * grad
        cols[:, at : at + grad.shape[1]] = jnp.sum(square, axis=0, keepdims=True)
        at += grad.shape[1]
        lanes = lax.broadcasted_iota(jnp.int32, (1, grad.shape[1]), 1)
        low = 0
        for edge, name in zip(edges, names):
            inside = (lanes >= low) & (lanes < edge)
            total = jnp.sum(jnp.where(inside, square, 0.0), axis=1, keepdims=True)
            sums = jnp.where(places == name, total, sums)
            low = edge
    rows[...] = sums


def update_kernel(groups, ways, model_width, hq, units, *refs):
    (grad_f, grad_b, grad_a0, grad_a1, rows, summed) = refs[:6]
    (g_qkv, g_so, g_cq, g_ckv, g_co, g_gu, g_d) = refs[6:13]
    (s_qkv, s_so, s_cq, s_ckv, s_co, s_gu, s_d) = refs[13:]
    whole = (grad_f[...], grad_b[...], jnp.concatenate([grad_a0[...], grad_a1[...]], axis=1))
    total_at = sum(g.shape[1] for g in whole)
    steps = []
    at = 0
    for grad, (edges, names) in zip(whole, groups):
        width = grad.shape[1]
        col_mean = summed[:, at : at + width] / model_width + 1e-30
        at += width
        row_mean, mean_rows = [], []
        low = 0
        for edge, name in zip(edges, names):
            row_mean.append(rows[:, name : name + 1] / ((edge - low) * ways) + 1e-30)
            mean_rows.append(summed[:, total_at + name : total_at + name + 1] / model_width)
            low = edge
        factor = lane_pick(width, edges, row_mean) * col_mean / lane_pick(width, edges, mean_rows)
        steps.append(grad * lax.rsqrt(factor))
    for (f, b, a), (qkv, so, cq, ckv, co, gu, d) in (
        (whole, (g_qkv, g_so, g_cq, g_ckv, g_co, g_gu, g_d)),
        (steps, (s_qkv, s_so, s_cq, s_ckv, s_co, s_gu, s_d)),
    ):
        for k in range(3):
            qkv[k] = a[:, k * hq : (k + 1) * hq]
        so[...] = a[:, 3 * hq :]
        cq[...] = b[:, :hq]
        co[...] = b[:, 3 * hq :]
        d[...] = f[:, 2 * units :]
        for k in range(2):
            ckv[:, k, :] = b[:, (k + 1) * hq : (k + 2) * hq]
            gu[:, k, :] = f[:, k * units : (k + 1) * units]


def whole_block(array):
    return (array, full(array.shape))


def square_sums(grad_f, grad_b, grad_a0, grad_a1, hq, units):
    own_rows = grad_f.shape[0]
    total = 4 * hq * 2 + 3 * units
    outs = [
        (sds((own_rows, 128), F32), full((own_rows, 128))),
        (sds((1, total), F32), full((1, total))),
    ]
    ins = [whole_block(g) for g in (grad_f, grad_b, grad_a0, grad_a1)]
    return run(
        functools.partial(square_sums_kernel, groups_of(hq, units)), 1, ins, outs, [], 4 * own_rows * total,
        "square_sums",
    )


def updates(grad_f, grad_b, grad_a0, grad_a1, rows, summed, model_width, hq, units):
    own_rows = grad_f.shape[0]
    shapes = [
        (3, own_rows, hq), (own_rows, hq), (own_rows, hq), (own_rows, 2, hq), (own_rows, hq),
        (own_rows, 2, units), (own_rows, units),
    ]
    outs = [(sds(shape, F32), full(shape)) for shape in shapes + shapes]
    ins = [whole_block(g) for g in (grad_f, grad_b, grad_a0, grad_a1, rows, summed)]
    results = run(
        functools.partial(update_kernel, groups_of(hq, units), lax.axis_size("mp"), model_width, hq, units),
        1, ins, outs, [], 8 * own_rows * (8 * hq + 3 * units), "updates",
    )
    results = list(results)
    results[0] = results[0].transpose(1, 0, 2)
    results[7] = results[7].transpose(1, 0, 2)
    return results


def on_device(
    tokens,
    memory,
    cotangent,
    table_lengths,
    table_plots,
    gains,
    w_qkv,
    w_self_out,
    w_cross_query,
    w_cross_kv,
    w_cross_out,
    w_gate_up,
    w_down,
):
    slots, width = tokens.shape
    hq = w_self_out.shape[1]
    heads = hq // DH
    units = w_down.shape[1]
    place = lax.axis_index("dp")
    x, z = place % 2, (place // 2) % 2
    ctl = jnp.stack([x, z]).astype(jnp.int32)
    gain_rows = gains.T
    gain_a, gain_b, gain_c = gain_rows[0:1], gain_rows[1:2], gain_rows[2:3]

    w_a = jnp.concatenate([w_qkv.transpose(1, 2, 0).reshape(3 * hq, width), w_self_out.T], axis=0)
    w_b = jnp.concatenate(
        [w_cross_query.T, w_cross_kv.transpose(1, 2, 0).reshape(2 * hq, width), w_cross_out.T], axis=0
    )
    w_f = jnp.concatenate(
        [w_gate_up.transpose(1, 2, 0).reshape(2 * units, width), w_down.T], axis=0
    )
    half_f = w_f.shape[0] // 2
    ways = lax.axis_size("dp")

    y_a = swap(y_pieces(w_a, x, z), "mp", 2)
    qkv0, mixed_a0, lse_a0, part = self_forward(table_lengths, tokens, gain_a, w_a, heads)
    kv0, k0, v0 = memory_forward(memory, w_b, heads)
    y_a, part, kv0 = together(y_a, part, kv0)

    far_a = (y_a,) + hand_on(y_a)
    y_b = swap(after(y_pieces(w_b, x, z), y_a), "mp", 2)
    qkv1, mixed_a1, lse_a1, part, w_a1 = self_forward(
        table_lengths, tokens, gain_a, None, heads, remote=(ctl,) + far_a + (part,)
    )
    y_b, part = together(y_b, part)

    part_other = swap(part, "mp", 1)
    x_b, z_b = hand_on(y_b)
    y_f0 = swap(after(y_pieces(w_f[:half_f], x, z), y_b), "mp", 2)
    q0, mixed_b0, lse_b0, part, first, normed_b = cross_forward(
        table_lengths, table_plots, w_b, kv0, k0, heads, lead=(tokens, part, part_other, gain_b),
    )
    x_b, z_b, part = together(x_b, z_b, part)
    kv1, k1, v1, w_b1 = memory_forward(memory, None, heads, remote=(ctl, y_b, x_b, z_b))
    q1, mixed_b1, lse_b1, part = cross_forward(
        table_lengths, table_plots, w_b1, kv1, k1, heads, follow=(normed_b, part)
    )
    y_f0, part = together(y_f0, part)

    part_other = swap(part, "mp", 1)
    x_f0, z_f0 = hand_on(y_f0)
    y_f1 = swap(after(y_pieces(w_f[half_f:], x, z), y_f0), "mp", 2)
    res, back, second, normed_c, grad_f = feed(
        units, lead=(first, part, part_other, gain_c, cotangent, w_f)
    )
    y_f1, x_f0, z_f0, res, back, grad_f = together(y_f1, x_f0, z_f0, res, back, grad_f)

    x_f1, z_f1 = hand_on(y_f1)
    far_f = (y_f0, x_f0, z_f0, y_f1, x_f1, z_f1)
    half_g = grad_f.shape[1] // 2
    rs_f0 = Halving(grad_f[:, :half_g], (1, 2, 4))
    rs_f1 = Halving(grad_f[:, half_g:], (2, 1, 4))
    rs_f0.start(x_f1, z_f1)
    rs_f1.start(x_f1, z_f1)
    res, back = feed(units, follow=(ctl, normed_c, cotangent, far_f, res, back))
    back_other = swap(back, "mp", 1)
    res_other = swap(after(res, back_other), "mp", 1)
    back, back_mem, grad_second, branch_b, gain_grad_c, grad_b = cross_backward(
        table_lengths, table_plots, w_b, q0, lse_b0, kv0, k0, v0, heads,
        lead=(second, back, back_other, cotangent, gain_c, normed_b, memory, mixed_b0),
    )
    rs_f0.got, rs_f1.got, res_other, back, grad_b = together(
        rs_f0.got, rs_f1.got, res_other, back, grad_b
    )
    rs_f0.finish()
    rs_f1.finish()
    rs_f0.start()
    rs_f1.start()
    layer_out = (second + (res + res_other)).astype(BF16)
    back, back_mem = cross_backward(
        table_lengths, table_plots, w_b1, q1, lse_b1, kv1, k1, v1, heads,
        follow=(branch_b, back, back_mem),
    )
    rs_f0.got, rs_f1.got, back, back_mem = together(rs_f0.got, rs_f1.got, back, back_mem)

    back_other = swap(back, "mp", 1)
    rs_f0.finish()
    rs_f1.finish()
    rs_b = Halving(grad_b, (1, 2, 4))
    rs_f0.start()
    rs_f1.start()
    rs_b.start()
    mem_other = swap(after(back_mem, back_other), "mp", 1)
    back, grad_first, branch_a, gain_grad_b, grad_a = self_backward(
        table_lengths, w_a, qkv0, lse_a0, heads,
        lead=(first, back, back_other, grad_second, gain_b, tokens, gain_a, mixed_a0),
    )
    rs_f0.got, rs_f1.got, rs_b.got, mem_other, back, grad_a = together(
        rs_f0.got, rs_f1.got, rs_b.got, mem_other, back, grad_a
    )

    half_a = grad_a.shape[1] // 2
    rs_b.finish()
    rs_a0 = Halving(grad_a[:, :half_a], (1, 2, 4))
    rs_a1 = Halving(grad_a[:, half_a:], (2, 1, 4))
    rs_a0.start()
    rs_a1.start()
    rs_b.start()
    rs_f0.finish()
    rs_f1.finish()
    grad_f = jnp.concatenate([rs_f0.rest(), rs_f1.rest()], axis=1)
    grad_memory = back_mem + mem_other
    (back,) = self_backward(table_lengths, w_a1, qkv1, lse_a1, heads, follow=(branch_a, back))
    rs_a0.got, rs_a1.got, rs_b.got, back, grad_f, grad_memory = together(
        rs_a0.got, rs_a1.got, rs_b.got, back, grad_f, grad_memory
    )

    back_other = swap(back, "mp", 1)
    rs_a0.finish()
    rs_a1.finish()
    rs_b.finish()
    rs_a0.start()
    rs_a1.start()
    rs_b.start()
    grad_tokens, gain_grad_a = tail(tokens, back, back_other, grad_first, gain_a)
    rs_a0.got, rs_a1.got, rs_b.got, gain_grad_a = together(
        rs_a0.got, rs_a1.got, rs_b.got, gain_grad_a
    )
    rs_a0.finish()
    rs_a1.finish()
    rs_b.finish()
    grad_a0, grad_a1, grad_b = rs_a0.rest(), rs_a1.rest(), rs_b.rest()

    row_sums, col_sums = square_sums(grad_f, grad_b, grad_a0, grad_a1, hq, units)
    row_sums = all_sum(row_sums, "mp")
    low = {}
    for edges, names in groups_of(hq, units):
        start = 0
        for edge, name in zip(edges, names):
            low[name] = (edge - start) * lax.axis_size("mp")
            start = edge
    columns = jnp.asarray([[1.0 / low[k] if k in low else 0.0 for k in range(128)]], F32)
    totals = jnp.sum(row_sums * columns + 1e-30, axis=0, keepdims=True)
    message = jnp.concatenate(
        [col_sums, totals, gain_grad_a[0:1], gain_grad_b[0:1], gain_grad_c[0:1]], axis=1
    )
    message = all_sum(message, "dp")
    span = col_sums.shape[1] + 128
    results = updates(
        grad_f, grad_b, grad_a0, grad_a1, row_sums, message[:, :span], width, hq, units
    )
    own_rows = grad_f.shape[0]
    grad_gains = lax.dynamic_slice_in_dim(
        message[:, span:].reshape(3, width), place * own_rows, own_rows, axis=1
    ).T
    return (layer_out, grad_tokens, grad_memory, grad_gains, *results)


def solution(mesh):
    split = P("dp", None)
    cols = P(None, "mp")
    cols3 = P(None, None, "mp")
    both = P("dp", "mp")
    both3 = P("dp", None, "mp")
    return jax.shard_map(
        on_device,
        mesh=mesh,
        in_specs=(
            split, split, split, split, split, P(),
            cols3, cols, cols, cols3, cols, cols3, cols,
        ),
        out_specs=(
            split, split, split, split,
            both3, both, both, both3, both, both3, both,
            both3, both, both, both3, both, both3, both,
        ),
        check_vma=False,
    )
```

```python
import functools
import math

import jax
import jax.numpy as jnp
from jax import lax
from jax.experimental import pallas as pl
from jax.experimental.pallas import tpu as pltpu
from jax.sharding import PartitionSpec as P

DH = 64
PATCH = 256
LONGEST = 512
ROWS = 256
SPAN = LONGEST // ROWS
F32 = jnp.float32
BF16 = jnp.bfloat16
NEG = -1e30
SCALE = 1.0 / math.sqrt(DH)
FREE, NEAR = "free", "near"
VMEM_BYTES = 30 * 1024 * 1024
SMALL = 1 << 15


def nn(a, b):
    return lax.dot_general(a, b, (((1,), (0,)), ((), ())), preferred_element_type=F32)


def nt(a, b):
    return lax.dot_general(a, b, (((1,), (1,)), ((), ())), preferred_element_type=F32)


def tn(a, b):
    return lax.dot_general(a, b, (((0,), (0,)), ((), ())), preferred_element_type=F32)


def normed_of(rows, gain):
    return rows * lax.rsqrt(jnp.mean(rows * rows, axis=-1, keepdims=True) + 1e-06) * gain


def norm_vjp(rows, gain, grad):
    inv = lax.rsqrt(jnp.mean(rows * rows, axis=-1, keepdims=True) + 1e-06)
    scaled = rows * inv
    hg = grad * gain
    inner = jnp.mean(hg * scaled, axis=-1, keepdims=True)
    grad_rows = inv * (hg - scaled * inner)
    grad_gain = jnp.sum(grad * scaled, axis=0, keepdims=True)
    return grad_rows, grad_gain, scaled


def place_pieces(dst, ctl, groups):
    x, z = ctl[0], ctl[1]
    base = 0
    for refs in groups:
        q = refs[0].shape[0] // 2
        if len(refs) == 4:
            y0, y1, x0, z1 = refs
            q = y0.shape[0]
            for slot, ref in ((x, y0), (1 - x, x0), (2 + z, y1), (3 - z, z1)):
                dst[pl.ds(pl.multiple_of(base + slot * q, 32), q), :] = ref[...].astype(BF16)
            base += 4 * q
        elif len(refs) == 3:
            by_y, by_x, by_z = refs

            def put(offset, value, base=base, q=q):
                dst[pl.ds(pl.multiple_of(base + offset, 32), q), :] = value.astype(BF16)

            put(x * q, by_y[:q, :])
            put((1 - x) * q, by_x[...])
            put((2 + z) * q, by_y[q:, :])
            put((3 - z) * q, by_z[...])
            base += 4 * q
        else:
            by_y, by_x, by_z, far_z, far_x = refs

            def put(who, half, value, base=base, q=q):
                dst[pl.ds(pl.multiple_of(base + who * (2 * q) + half * q, 32), q), :] = value.astype(BF16)

            me, other_x = 2 * z + x, 2 * z + 1 - x
            other_z, other = 2 * (1 - z) + x, 2 * (1 - z) + 1 - x
            put(me, 0, by_y[:q, :])
            put(me, 1, by_y[q:, :])
            put(other_x, 0, by_x[...])
            put(other_z, 1, by_z[...])
            put(other_z, 0, far_z[:q, :])
            put(other, 0, far_z[q:, :])
            put(other_x, 1, far_x[:q, :])
            put(other, 1, far_x[q:, :])
            base += 8 * q


def table_ends(lengths):
    ends = []
    total = lengths[0, 0]
    for j in range(1, lengths.shape[1]):
        ends.append(total)
        total = total + lengths[0, j]
    return ends


def query_places(base):
    return lax.broadcasted_iota(jnp.int32, (1, ROWS), 1) + base


def self_bias(lengths, base, low, width):
    places = query_places(base)
    start = jnp.zeros_like(places)
    for end in table_ends(lengths):
        start = jnp.where(places >= end, end, start)
    keys = lax.broadcasted_iota(jnp.int32, (width, ROWS), 0) + low
    return jnp.where((keys >= start) & (keys <= places), 0.0, NEG)


def window_cases(block, body):
    for back in range(SPAN + 1):
        width = (back + 1) * ROWS

        @pl.when(block == back if back < SPAN else block >= SPAN)
        def _run(back=back, width=width):
            if back < SPAN:
                body(0, width)
            else:
                body(pl.multiple_of((block - SPAN) * ROWS, ROWS), width)


def full(shape):
    return pl.BlockSpec(shape, lambda i: (0,) * len(shape))


def by_rows(width):
    return pl.BlockSpec((ROWS, width), lambda i: (i, 0))


def by_cols(height):
    return pl.BlockSpec((height, ROWS), lambda i: (0, i))


SMEM = pl.BlockSpec(memory_space=pltpu.SMEM)


def run(kernel, grid, ins, outs, scratch, flops, name, transcendentals=0):
    moved = sum(entry[0].size * entry[0].dtype.itemsize for entry in ins) + sum(
        math.prod(entry[0].shape) * jnp.dtype(entry[0].dtype).itemsize for entry in outs
    )
    arrays = [
        entry[0]
        if entry[-1] is FREE or entry[1] is SMEM or entry[0].size < SMALL
        else pltpu.with_memory_space_constraint(entry[0], pltpu.VMEM if entry[-1] is NEAR else pltpu.HBM)
        for entry in ins
    ]
    shapes = [
        entry[0]
        if entry[-1] is FREE or math.prod(entry[0].shape) < SMALL
        else (pltpu.VMEM if entry[-1] is NEAR else pltpu.HBM)(entry[0].shape, entry[0].dtype)
        for entry in outs
    ]
    return pl.pallas_call(
        kernel,
        grid=(grid,),
        in_specs=[entry[1] for entry in ins],
        out_specs=[entry[1] for entry in outs],
        out_shape=shapes,
        scratch_shapes=scratch,
        compiler_params=pltpu.CompilerParams(
            vmem_limit_bytes=VMEM_BYTES, dimension_semantics=("arbitrary",)
        ),
        cost_estimate=pl.CostEstimate(
            flops=flops // 64, bytes_accessed=moved // 64, transcendentals=transcendentals // 64
        ),
        name=name,
    )(*arrays)


def sds(shape, dtype):
    return jax.ShapeDtypeStruct(shape, dtype)


def self_forward_kernel(remote, heads, *refs):
    if remote:
        (lengths, ctl, tokens, gain, base_out) = refs[:5]
        pieces = refs[5:-6]
        (qkv_t, mixed_t, lse, out, w_out, k_rows) = refs[-6:]
        w = w_out
    else:
        (lengths, tokens, gain, w) = refs[:4]
        (qkv_t, mixed_t, lse, out, k_rows) = refs[4:]
    block = pl.program_id(0)
    hq = heads * DH
    if remote:

        @pl.when(block == 0)
        def _place():
            place_pieces(w, ctl, [pieces])

    base = pl.multiple_of(block * ROWS, ROWS)
    here = pl.ds(base, ROWS)
    normed = normed_of(tokens[...].astype(F32), gain[...]).astype(BF16)
    qkv = nt(w[0 : 3 * hq, :], normed).astype(BF16)
    q_all = (qkv[:hq].astype(F32) * SCALE).astype(BF16)
    qkv_t[0:hq, here] = q_all
    qkv_t[hq : 3 * hq, here] = qkv[hq:]
    for h in range(heads):
        k_rows[h, here, :] = qkv[hq + h * DH : hq + (h + 1) * DH].T

    def attend(low, width):
        window = pl.ds(low, width)
        bias = self_bias(lengths, base, low, width)
        for h in range(heads):
            own = slice(h * DH, (h + 1) * DH)
            s = nn(k_rows[h, window, :], q_all[own]) + bias
            top = jnp.max(s, axis=0, keepdims=True)
            e = jnp.exp(s - top)
            total = jnp.sum(e, axis=0, keepdims=True)
            o = nn(qkv_t[2 * hq + h * DH : 2 * hq + (h + 1) * DH, window], e.astype(BF16))
            mixed_t[own, :] = (o * (1.0 / total)).astype(BF16)
            lse[h : h + 1, :] = top + jnp.log(total)

    window_cases(block, attend)
    part = tn(mixed_t[...], w[3 * hq : 4 * hq, :])
    out[...] = part + base_out[...] if remote else part


def self_forward(lengths, tokens, gain, w, heads, remote=None):
    slots, width = tokens.shape
    hq = heads * DH
    outs = [
        (sds((3 * hq, slots), BF16), full((3 * hq, slots))),
        (sds((hq, slots), BF16), by_cols(hq)),
        (sds((8, slots), F32), by_cols(8)),
        (sds((slots, width), F32), by_rows(width), NEAR),
    ]
    scratch = [pltpu.VMEM((heads, slots, DH), BF16)]
    if remote is None:
        ins = [(lengths, SMEM), (tokens, by_rows(width)), (gain, full(gain.shape)), (w, full(w.shape))]
    else:
        ctl, pieces, base_out = remote
        ins = [
            (lengths, SMEM),
            (ctl, SMEM),
            (tokens, by_rows(width)),
            (gain, full(gain.shape)),
            (base_out, by_rows(width), NEAR),
        ]
        ins += [(piece, full(piece.shape)) for piece in pieces]
        outs.append((sds((4 * hq, width), BF16), full((4 * hq, width))))
    flops = 2 * slots * width * 4 * hq + heads * 4 * slots * slots * DH
    return run(
        functools.partial(self_forward_kernel, remote is not None, heads),
        slots // ROWS, ins, outs, scratch, flops, "self_forward", heads * slots * slots,
    )


def memory_kernel(remote, heads, *refs):
    hq = heads * DH
    if remote:
        ctl, memory = refs[:2]
        kv_t, k_rows, v_rows, w = refs[-4:]

        @pl.when(pl.program_id(0) == 0)
        def _place():
            place_pieces(w, ctl, [refs[2:-4]])
    else:
        memory, w, kv_t, k_rows, v_rows = refs
    kv = nt(w[hq : 3 * hq, :], memory[...]).astype(BF16)
    kv_t[...] = kv
    for h in range(heads):
        k_rows[h] = kv[h * DH : (h + 1) * DH].T
        v_rows[h] = kv[hq + h * DH : hq + (h + 1) * DH].T


def memory_forward(memory, w, heads, remote=None):
    count, width = memory.shape
    hq = heads * DH
    head_rows = pl.BlockSpec((heads, ROWS, DH), lambda i: (0, i, 0))
    outs = [
        (sds((2 * hq, count), BF16), by_cols(2 * hq)),
        (sds((heads, count, DH), BF16), head_rows),
        (sds((heads, count, DH), BF16), head_rows),
    ]
    if remote is None:
        ins = [(memory, by_rows(width)), (w, full(w.shape))]
    else:
        ctl, pieces = remote
        ins = [(ctl, SMEM), (memory, by_rows(width))]
        ins += [(piece, full(piece.shape)) for piece in pieces]
        outs.append((sds((4 * hq, width), BF16), full((4 * hq, width))))
    return run(
        functools.partial(memory_kernel, remote is not None, heads),
        count // ROWS, ins, outs, [], 2 * count * width * 2 * hq, "memory_forward",
    )


def tables_of_block(lengths, base, body):
    ends = table_ends(lengths)
    places = query_places(base)
    segment = jnp.zeros_like(places)
    first_table = jnp.int32(0)
    last_table = jnp.int32(0)
    for end in ends:
        segment = segment + (places >= end).astype(jnp.int32)
        first_table = first_table + (base >= end).astype(jnp.int32)
        last_table = last_table + (base + ROWS - 1 >= end).astype(jnp.int32)

    def step(table, carry):
        body(table, segment == table)
        return carry

    lax.fori_loop(first_table, last_table + 1, step, 0)


def cross_forward_kernel(leading, heads, *refs):
    hq = heads * DH
    if leading:
        (lengths, plots, tokens, part, other, gain, w, kv_t, k_rows) = refs[:9]
        (q_t, mixed_t, lse, out, first, normed_out) = refs[9:]
        rows = tokens[...].astype(F32) + (part[...] + other[...])
        first[...] = rows
        normed = normed_of(rows, gain[...]).astype(BF16)
        normed_out[...] = normed
    else:
        (lengths, plots, normed_in, w, kv_t, k_rows, base_out) = refs[:7]
        (q_t, mixed_t, lse, out) = refs[7:]
        normed = normed_in[...]
    base = pl.multiple_of(pl.program_id(0) * ROWS, ROWS)
    query = nt(w[0:hq, :], normed).astype(BF16)
    q_all = (query.astype(F32) * SCALE).astype(BF16)
    q_t[...] = q_all

    def table(j, member):
        plot = pl.ds(pl.multiple_of(plots[0, j] * PATCH, PATCH), PATCH)
        for h in range(heads):
            own = slice(h * DH, (h + 1) * DH)
            s = nn(k_rows[h, plot, :], q_t[own, :])
            top = jnp.max(s, axis=0, keepdims=True)
            e = jnp.exp(s - top)
            total = jnp.sum(e, axis=0, keepdims=True)
            o = nn(kv_t[hq + h * DH : hq + (h + 1) * DH, plot], e.astype(BF16))
            o = o * (1.0 / total)
            mixed_t[own, :] = jnp.where(member, o, mixed_t[own, :].astype(F32)).astype(BF16)
            lse[h : h + 1, :] = jnp.where(member, top + jnp.log(total), lse[h : h + 1, :])

    tables_of_block(lengths, base, table)
    part_out = tn(mixed_t[...], w[3 * hq : 4 * hq, :])
    out[...] = part_out if leading else part_out + base_out[...]


def cross_forward(lengths, plots, w, kv_t, k_rows, heads, lead=None, follow=None):
    hq = heads * DH
    slots = (lead or follow)[0].shape[0]
    width = w.shape[1]
    outs = [
        (sds((hq, slots), BF16), by_cols(hq)),
        (sds((hq, slots), BF16), by_cols(hq)),
        (sds((8, slots), F32), by_cols(8)),
        (sds((slots, width), F32), by_rows(width), NEAR),
    ]
    shared = [(w, full(w.shape)), (kv_t, full(kv_t.shape)), (k_rows, full(k_rows.shape))]
    if lead is not None:
        tokens, part, other, gain = lead
        ins = [
            (lengths, SMEM),
            (plots, SMEM),
            (tokens, by_rows(width)),
            (part, by_rows(width), NEAR),
            (other, by_rows(width), NEAR),
            (gain, full(gain.shape)),
        ] + shared
        outs += [
            (sds((slots, width), F32), by_rows(width)),
            (sds((slots, width), BF16), by_rows(width)),
        ]
    else:
        normed, base_out = follow
        ins = [(lengths, SMEM), (plots, SMEM), (normed, by_rows(width))] + shared
        ins.append((base_out, by_rows(width), NEAR))
    flops = 2 * slots * width * 2 * hq + heads * 8 * slots * PATCH * DH
    return run(
        functools.partial(cross_forward_kernel, lead is not None, heads),
        slots // ROWS, ins, outs, [], flops, "cross_forward", heads * slots * PATCH * 2,
    )


def gradient_outs(count, rows, width):
    if split_bits(rows, count):
        half = (rows // 2, width // 2)
        return [(sds(half, F32), full(half)) for _ in range(4)]
    return [(sds((rows, width), F32), full((rows, width)))]


def finish_gradient(count, ctl, source, outs):
    @pl.when(pl.program_id(0) == pl.num_programs(0) - 1)
    def _write():
        if len(outs) == 1:
            outs[0][...] = source[...]
        else:
            half = source.shape[1] // 2
            write_split(source, 0, half, count, 1, ctl[0], outs[0], outs[1])
            write_split(source, half, 2 * half, count, 2, ctl[1], outs[2], outs[3])


def halvings(outs):
    if len(outs) == 1:
        half = outs[0].shape[1] // 2
        return Halving(outs[0][:, :half], (1, 2, 4)), Halving(outs[0][:, half:], (2, 1, 4))
    return Halving(None, (1, 2, 4), outs[0:2]), Halving(None, (2, 1, 4), outs[2:4])


def feed_kernel(leading, units, count, *refs):
    if leading:
        (ctl, first, part, other, gain, cot, w) = refs[:7]
        (result, grad_in, second, normed_out) = refs[7:11]
        dw_outs, dw = refs[11:-1], refs[-1]
        rows = first[...] + (part[...] + other[...])
        second[...] = rows
        normed = normed_of(rows, gain[...]).astype(BF16)
        normed_out[...] = normed

        @pl.when(pl.program_id(0) == 0)
        def _zero():
            dw[...] = jnp.zeros_like(dw)
    else:
        (ctl, normed_in, cot, base_result, base_grad) = refs[:5]
        pieces = refs[5:-3]
        (result, grad_in, w) = refs[-3:]
        normed = normed_in[...]

        @pl.when(pl.program_id(0) == 0)
        def _place():
            place_pieces(w, ctl, [pieces[:5], pieces[5:]])

    cot_rows = cot[...]
    gate_up = nt(normed, w[0 : 2 * units, :])
    gate, up = gate_up[:, :units], gate_up[:, units:]
    c0 = math.sqrt(2.0 / math.pi)
    square = gate * gate
    th = jnp.tanh(c0 * gate * (1.0 + 0.044715 * square))
    half = 0.5 * (1.0 + th)
    gelu = gate * half
    slope = half + (0.5 * c0) * gate * (1.0 - th * th) * (1.0 + (3 * 0.044715) * square)
    hidden = (gelu * up).astype(BF16)
    res = nn(hidden, w[2 * units : 3 * units, :])
    grad_hidden = nt(cot_rows, w[2 * units : 3 * units, :])
    grad_gate = (grad_hidden * up * slope).astype(BF16)
    grad_up = (grad_hidden * gelu).astype(BF16)
    back = nn(grad_gate, w[0:units, :]) + nn(grad_up, w[units : 2 * units, :])
    if leading:
        result[...] = res
        grad_in[...] = back
        dw[:, 0:units] += tn(normed, grad_gate)
        dw[:, units : 2 * units] += tn(normed, grad_up)
        dw[:, 2 * units : 3 * units] += tn(cot_rows, hidden)
        finish_gradient(count, ctl, dw, dw_outs)
    else:
        result[...] = res + base_result[...]
        grad_in[...] = back + base_grad[...]


def feed(units, lead=None, follow=None):
    if lead is not None:
        ctl, count, first, part, other, gain, cot, w = lead
        slots, width = first.shape
        ins = [
            (ctl, SMEM),
            (first, by_rows(width)),
            (part, by_rows(width), NEAR),
            (other, by_rows(width), NEAR),
            (gain, full(gain.shape)),
            (cot, by_rows(width)),
            (w, full(w.shape)),
        ]
    else:
        ctl, normed, cot, pieces, base_result, base_grad = follow
        slots, width = normed.shape
        ins = [(ctl, SMEM), (normed, by_rows(width), FREE), (cot, by_rows(width))]
        ins += [(base_result, by_rows(width), FREE), (base_grad, by_rows(width), NEAR)]
        ins += [(piece, full(piece.shape)) for group in pieces for piece in group]
    outs = [
        (sds((slots, width), F32), by_rows(width), FREE),
        (sds((slots, width), F32), by_rows(width), NEAR),
    ]
    scratch = []
    if lead is not None:
        outs += [
            (sds((slots, width), F32), by_rows(width)),
            (sds((slots, width), BF16), by_rows(width), FREE),
        ]
        outs += gradient_outs(count, width, 3 * units)
        scratch = [pltpu.VMEM((width, 3 * units), F32)]
    else:
        count = 0
        scratch = [pltpu.VMEM((3 * units, width), BF16)]
    flops = 2 * slots * width * units * (9 if lead is not None else 6)
    return run(
        functools.partial(feed_kernel, lead is not None, units, count),
        slots // ROWS, ins, outs, scratch, flops, "feed", slots * units,
    )


def cross_backward_kernel(leading, heads, count, *refs):
    hq = heads * DH
    if leading:
        (ctl, lengths, plots, second, part, other, cot, gain, normed, memory) = refs[:10]
        (w, q_t, mixed_t, lse, kv_t, k_rows, v_rows) = refs[10:17]
        (grad_in, grad_mem, grad_second, branch_out, grad_gain) = refs[17:22]
        dw_outs = refs[22:-5]
        (dkv, dq, dm, dw_t, dw) = refs[-5:]
    else:
        (lengths, plots, branch_in, w, q_t, lse, kv_t, k_rows, v_rows, base_grad, base_mem) = refs[:11]
        (grad_in, grad_mem, dkv, dq, dm) = refs[11:]
    block = pl.program_id(0)
    last = pl.num_programs(0) - 1
    base = pl.multiple_of(block * ROWS, ROWS)

    @pl.when(block == 0)
    def _zero():
        dkv[...] = jnp.zeros_like(dkv)
        if leading:
            dw_t[...] = jnp.zeros_like(dw_t)
            grad_gain[...] = jnp.zeros_like(grad_gain)

    if leading:
        grad_rows, gain_rows, _ = norm_vjp(second[...], gain[...], part[...] + other[...])
        total = cot[...].astype(F32) + grad_rows
        grad_second[...] = total
        branch = total.astype(BF16)
        branch_out[...] = branch
        grad_gain[0:1, :] += gain_rows
    else:
        branch = branch_in[...]
    dm[...] = nt(w[3 * hq : 4 * hq, :], branch).astype(BF16)
    dq[...] = jnp.zeros_like(dq)

    def table(j, member):
        plot = pl.ds(pl.multiple_of(plots[0, j] * PATCH, PATCH), PATCH)
        for h in range(heads):
            own = slice(h * DH, (h + 1) * DH)
            val = slice(hq + h * DH, hq + (h + 1) * DH)
            query = q_t[own, :]
            dmix = jnp.where(member, dm[own, :].astype(F32), 0.0).astype(BF16)
            level = jnp.where(member, lse[h : h + 1, :], -NEG)
            p = jnp.exp(nn(k_rows[h, plot, :], query) - level)
            dp = nn(v_rows[h, plot, :], dmix)
            inner = jnp.sum(p * dp, axis=0, keepdims=True)
            ds = (p * (dp - inner)).astype(BF16)
            dkv[own, plot] += nt(query, ds)
            dkv[val, plot] += nt(dmix, p.astype(BF16))
            dq[own, :] += nn(kv_t[own, plot], ds)

    tables_of_block(lengths, base, table)
    grad_query = (dq[...] * SCALE).astype(BF16)
    back = tn(grad_query, w[0:hq, :])
    grad_in[...] = back if leading else back + base_grad[...]
    if leading:
        dw_t[0:hq, :] += nn(grad_query, normed[...])
        dw_t[3 * hq : 4 * hq, :] += nn(mixed_t[...], branch)

    @pl.when(block == last)
    def _finish():
        for m in range(dkv.shape[1] // ROWS):
            here = slice(m * ROWS, (m + 1) * ROWS)
            rows = dkv[:, here].astype(BF16)
            back_mem = tn(rows, w[hq : 3 * hq, :])
            grad_mem[here, :] = back_mem if leading else back_mem + base_mem[here, :]
            if leading:
                dw_t[hq : 3 * hq, :] += nn(rows, memory[here, :])
        if leading:
            dw[...] = dw_t[...].T

    if leading:
        finish_gradient(count, ctl, dw, dw_outs)


def cross_backward(lengths, plots, w, q_t, lse, kv_t, k_rows, v_rows, heads, lead=None, follow=None):
    hq = heads * DH
    slots, width = q_t.shape[1], w.shape[1]
    count = kv_t.shape[1]
    outs = [
        (sds((slots, width), F32), by_rows(width), NEAR),
        (sds((count, width), F32), full((count, width)), FREE),
    ]
    scratch = [
        pltpu.VMEM((2 * hq, count), F32),
        pltpu.VMEM((hq, ROWS), F32),
        pltpu.VMEM((hq, ROWS), BF16),
    ]
    heads_part = [
        (lse, by_cols(8)),
        (kv_t, full(kv_t.shape)),
        (k_rows, full(k_rows.shape)),
        (v_rows, full(v_rows.shape)),
    ]
    if lead is not None:
        ctl, split, second, part, other, cot, gain, normed, memory, mixed_t = lead
        ins = [
            (ctl, SMEM),
            (lengths, SMEM),
            (plots, SMEM),
            (second, by_rows(width)),
            (part, by_rows(width), NEAR),
            (other, by_rows(width), NEAR),
            (cot, by_rows(width)),
            (gain, full(gain.shape)),
            (normed, by_rows(width)),
            (memory, full(memory.shape)),
            (w, full(w.shape)),
            (q_t, by_cols(hq)),
            (mixed_t, by_cols(hq)),
        ] + heads_part
        outs += [
            (sds((slots, width), F32), by_rows(width), FREE),
            (sds((slots, width), BF16), by_rows(width), FREE),
            (sds((8, width), F32), full((8, width))),
        ]
        outs += gradient_outs(split, width, 4 * hq)
        scratch += [pltpu.VMEM((4 * hq, width), F32), pltpu.VMEM((width, 4 * hq), F32)]
    else:
        split = 0
        branch, base_grad, base_mem = follow
        ins = [
            (lengths, SMEM),
            (plots, SMEM),
            (branch, by_rows(width), FREE),
            (w, full(w.shape)),
            (q_t, by_cols(hq)),
        ] + heads_part
        ins += [(base_grad, by_rows(width), NEAR), (base_mem, full(base_mem.shape), FREE)]
    flops = 2 * slots * width * hq * (8 if lead is not None else 4) + heads * 20 * slots * PATCH * DH
    return run(
        functools.partial(cross_backward_kernel, lead is not None, heads, split),
        slots // ROWS, ins, outs, scratch, flops, "cross_backward", heads * slots * PATCH * 2,
    )


def self_backward_kernel(leading, heads, count, *refs):
    hq = heads * DH
    if leading:
        (ctl, lengths, first, part, other, carried, gain, tokens, gain_in, w, qkv_t, mixed_t, lse) = refs[:13]
        (grad_in, grad_first, branch_out, grad_gain) = refs[13:17]
        dw_outs = refs[17:-6]
        (dkv, k_rows, v_rows, dqkv, dw_t, dw) = refs[-6:]
    else:
        (lengths, branch_in, w, qkv_t, lse, base_grad) = refs[:6]
        (grad_in, dkv, k_rows, v_rows, dqkv) = refs[6:]
    step = pl.program_id(0)
    last = pl.num_programs(0) - 1
    block = last - step
    base = pl.multiple_of(block * ROWS, ROWS)
    here = pl.ds(base, ROWS)

    @pl.when(step == 0)
    def _start():
        dkv[...] = jnp.zeros_like(dkv)
        for h in range(heads):
            k_rows[h] = qkv_t[hq + h * DH : hq + (h + 1) * DH, :].T
            v_rows[h] = qkv_t[2 * hq + h * DH : 2 * hq + (h + 1) * DH, :].T
        if leading:
            dw_t[...] = jnp.zeros_like(dw_t)
            grad_gain[...] = jnp.zeros_like(grad_gain)

    if leading:
        grad_rows, gain_rows, _ = norm_vjp(first[...], gain[...], part[...] + other[...])
        total = carried[...] + grad_rows
        grad_first[...] = total
        branch = total.astype(BF16)
        branch_out[...] = branch
        grad_gain[0:1, :] += gain_rows
    else:
        branch = branch_in[...]
    dm_all = nt(w[3 * hq : 4 * hq, :], branch).astype(BF16)

    def attend(low, width):
        window = pl.ds(low, width)
        bias = self_bias(lengths, base, low, width)
        for h in range(heads):
            own = slice(h * DH, (h + 1) * DH)
            key = slice(hq + h * DH, hq + (h + 1) * DH)
            val = slice(hq + h * DH, hq + (h + 1) * DH)
            query = qkv_t[own, here]
            dmix = dm_all[own]
            p = jnp.exp(nn(k_rows[h, window, :], query) + bias - lse[h : h + 1, :])
            dp = nn(v_rows[h, window, :], dmix)
            inner = jnp.sum(p * dp, axis=0, keepdims=True)
            ds = (p * (dp - inner)).astype(BF16)
            dkv[own, window] += nt(query, ds)
            dkv[val, window] += nt(dmix, p.astype(BF16))
            dqkv[own, :] = (nn(qkv_t[key, window], ds) * SCALE).astype(BF16)

    window_cases(block, attend)
    dqkv[hq : 3 * hq, :] = dkv[:, here].astype(BF16)
    rows = dqkv[...]
    back = tn(rows, w[0 : 3 * hq, :])
    grad_in[...] = back if leading else back + base_grad[...]
    if leading:
        normed = normed_of(tokens[...].astype(F32), gain_in[...]).astype(BF16)
        dw_t[0 : 3 * hq, :] += nn(rows, normed)
        dw_t[3 * hq : 4 * hq, :] += nn(mixed_t[...], branch)

        @pl.when(step == last)
        def _finish():
            dw[...] = dw_t[...].T

        finish_gradient(count, ctl, dw, dw_outs)


def self_backward(lengths, w, qkv_t, lse, heads, lead=None, follow=None):
    hq = heads * DH
    slots, width = qkv_t.shape[1], w.shape[1]
    last = slots // ROWS - 1
    rows = pl.BlockSpec((ROWS, width), lambda i: (last - i, 0))

    def cols(height):
        return pl.BlockSpec((height, ROWS), lambda i: (0, last - i))

    outs = [(sds((slots, width), F32), rows, NEAR)]
    scratch = [
        pltpu.VMEM((2 * hq, slots), F32),
        pltpu.VMEM((heads, slots, DH), BF16),
        pltpu.VMEM((heads, slots, DH), BF16),
        pltpu.VMEM((3 * hq, ROWS), BF16),
    ]
    if lead is not None:
        ctl, count, first, part, other, carried, gain, tokens, gain_in, mixed_t = lead
        ins = [
            (ctl, SMEM),
            (lengths, SMEM),
            (first, rows),
            (part, rows, NEAR),
            (other, rows, NEAR),
            (carried, rows, FREE),
            (gain, full(gain.shape)),
            (tokens, rows),
            (gain_in, full(gain_in.shape)),
            (w, full(w.shape)),
            (qkv_t, full(qkv_t.shape)),
            (mixed_t, cols(hq)),
            (lse, cols(8)),
        ]
        outs += [
            (sds((slots, width), F32), rows, FREE),
            (sds((slots, width), BF16), rows, FREE),
            (sds((8, width), F32), full((8, width))),
        ]
        outs += gradient_outs(count, width, 4 * hq)
        scratch += [pltpu.VMEM((4 * hq, width), F32), pltpu.VMEM((width, 4 * hq), F32)]
    else:
        count = 0
        branch, base_grad = follow
        ins = [
            (lengths, SMEM),
            (branch, rows, FREE),
            (w, full(w.shape)),
            (qkv_t, full(qkv_t.shape)),
            (lse, cols(8)),
            (base_grad, rows, NEAR),
        ]
    flops = 2 * slots * width * hq * (8 if lead is not None else 4) + heads * 10 * slots * slots * DH
    return run(
        functools.partial(self_backward_kernel, lead is not None, heads, count),
        slots // ROWS, ins, outs, scratch, flops, "self_backward", heads * slots * slots,
    )


def tail_kernel(tokens, part, other, carried, gain, grad_tokens, grad_gain):
    @pl.when(pl.program_id(0) == 0)
    def _zero():
        grad_gain[...] = jnp.zeros_like(grad_gain)

    grad_rows, gain_rows, _ = norm_vjp(tokens[...].astype(F32), gain[...], part[...] + other[...])
    grad_tokens[...] = carried[...] + grad_rows
    grad_gain[0:1, :] += gain_rows


def tail(tokens, part, other, carried, gain):
    slots, width = tokens.shape
    ins = [
        (tokens, by_rows(width)),
        (part, by_rows(width), NEAR),
        (other, by_rows(width), NEAR),
        (carried, by_rows(width), FREE),
        (gain, full(gain.shape)),
    ]
    outs = [
        (sds((slots, width), F32), by_rows(width)),
        (sds((8, width), F32), full((8, width))),
    ]
    return run(tail_kernel, slots // ROWS, ins, outs, [], 20 * slots * width, "last_norm")


def swap(value, axis, bit):
    count = lax.axis_size(axis)
    return lax.ppermute(value, axis, [(i, i ^ bit) for i in range(count)])


def after(value, *others):
    return lax.optimization_barrier((value,) + others)[0]


def y_pieces(w, x, z):
    quarter = w.shape[0] // 4
    pieces = w.reshape(4, quarter, w.shape[1])
    mine = jnp.concatenate(
        [jnp.where(x == 0, pieces[0], pieces[1]), jnp.where(z == 0, pieces[2], pieces[3])], axis=0
    )
    return mine.astype(F32)


def hand_on(by_y):
    quarter = by_y.shape[0] // 2
    return swap(by_y[:quarter], "dp", 1), swap(by_y[quarter:], "dp", 2)


def y_piece_of_four(w, x, z):
    quarter = w.shape[0] // 4
    mine = lax.dynamic_slice_in_dim(w, (2 * z + x) * quarter, quarter, axis=0)
    return mine.astype(F32)


def hand_on_again(by_y, by_x, by_z):
    half = by_y.shape[0] // 2
    far_z = swap(jnp.concatenate([by_y[:half], by_x], axis=0), "dp", 2)
    far_x = swap(jnp.concatenate([by_y[half:], by_z], axis=0), "dp", 1)
    return far_z, far_x


def y_two(w, x, z):
    quarter = w.shape[0] // 4
    first = lax.dynamic_slice_in_dim(w, x * quarter, quarter, axis=0).astype(F32)
    second = lax.dynamic_slice_in_dim(w, (2 + z) * quarter, quarter, axis=0).astype(F32)
    return swap(first, "mp", 2), swap(second, "mp", 2)


def together(*values):
    return lax.optimization_barrier(values)


def split_bits(grad_rows, count):
    return count >= 4 and (grad_rows // count) % 8 == 0


def write_split(source, low, high, count, bit, mine, sent, kept):
    own = source.shape[0] // count
    for r in range(count // 2):
        base = (r // bit) * 2 * bit + r % bit
        rows = slice(r * own, (r + 1) * own)
        kept[rows, :] = source[pl.ds(pl.multiple_of((base + mine * bit) * own, 8), own), low:high]
        sent[rows, :] = source[pl.ds(pl.multiple_of((base + (1 - mine) * bit) * own, 8), own), low:high]


class Halving:
    def __init__(self, grad, order, halves=None):
        self.halves = halves
        self.count = lax.axis_size("dp")
        self.place = lax.axis_index("dp")
        self.order = list(order)
        bit = 8
        while bit < self.count:
            self.order.append(bit)
            bit *= 2
        self.left = [b for b in (1 << k for k in range(self.count.bit_length() - 1))][::-1]
        if halves is None:
            self.grad = grad.reshape((2,) * len(self.left) + (grad.shape[0] // self.count, grad.shape[1]))

    def send(self):
        bit = self.order.pop(0)
        axis = self.left.index(bit)
        self.left.pop(axis)
        if self.halves is not None:
            sent, kept = self.halves
            self.halves = None
            shape = (2,) * len(self.left) + (kept.shape[0] * 2 // self.count, kept.shape[1])
            self.kept = kept.reshape(shape)
            return sent.reshape(shape), bit
        mine = (self.place // bit) % 2
        sent = lax.dynamic_index_in_dim(self.grad, 1 - mine, axis=axis, keepdims=False)
        self.kept = lax.dynamic_index_in_dim(self.grad, mine, axis=axis, keepdims=False)
        return sent, bit

    def start(self, *others):
        sent, bit = self.send()
        shape = sent.shape
        flat = sent.reshape(-1, shape[-1])
        if others:
            flat = after(flat, *others)
        self.got = swap(flat, "dp", bit)

    def finish(self):
        self.grad = self.kept + self.got.reshape(self.kept.shape)

    def rest(self):
        while self.order:
            self.start()
            self.finish()
        return self.grad.reshape(-1, self.grad.shape[-1])


def all_sum(value, axis):
    bit = 1
    while bit < lax.axis_size(axis):
        value = value + swap(value, axis, bit)
        bit *= 2
    return value


def lane_pick(width, edges, values):
    lanes = lax.broadcasted_iota(jnp.int32, (1, width), 1)
    picked = values[-1]
    for edge, value in zip(edges[-2::-1], values[-2::-1]):
        picked = jnp.where(lanes < edge, value, picked)
    return picked


def groups_of(hq, units):
    return (
        ((2 * units, 3 * units), (0, 1)),
        ((hq, 3 * hq, 4 * hq), (2, 3, 4)),
        ((3 * hq, 4 * hq), (5, 6)),
    )


def joined(refs):
    f0, f1, b0, b1, a0, a1 = (ref[...] for ref in refs)
    return tuple(jnp.concatenate(pair, axis=1) for pair in ((f0, f1), (b0, b1), (a0, a1)))


def square_sums_kernel(groups, *refs):
    rows, cols = refs[6:]
    places = lax.broadcasted_iota(jnp.int32, (1, rows.shape[1]), 1)
    sums = jnp.zeros(rows.shape, F32)
    at = 0
    for grad, (edges, names) in zip(joined(refs[:6]), groups):
        square = grad * grad
        cols[:, at : at + grad.shape[1]] = jnp.sum(square, axis=0, keepdims=True)
        at += grad.shape[1]
        lanes = lax.broadcasted_iota(jnp.int32, (1, grad.shape[1]), 1)
        low = 0
        for edge, name in zip(edges, names):
            inside = (lanes >= low) & (lanes < edge)
            total = jnp.sum(jnp.where(inside, square, 0.0), axis=1, keepdims=True)
            sums = jnp.where(places == name, total, sums)
            low = edge
    rows[...] = sums


def message_kernel(groups, ways, rows, other, cols, gain_a, gain_b, gain_c, rows_out, message):
    total = rows[...] + other[...]
    rows_out[...] = total
    places = lax.broadcasted_iota(jnp.int32, (1, total.shape[1]), 1)
    scale = jnp.zeros((1, total.shape[1]), F32)
    for edges, names in groups:
        low = 0
        for edge, name in zip(edges, names):
            scale = jnp.where(places == name, 1.0 / ((edge - low) * ways), scale)
            low = edge
    at = cols.shape[1]
    message[:, :at] = cols[...]
    message[:, at : at + 128] = jnp.sum(total * scale + 1e-30, axis=0, keepdims=True)
    at += 128
    for gain in (gain_a, gain_b, gain_c):
        message[:, at : at + gain.shape[1]] = gain[0:1, :]
        at += gain.shape[1]


def update_kernel(groups, ways, model_width, hq, units, *refs):
    rows, summed = refs[6:8]
    (g_qkv, g_so, g_cq, g_ckv, g_co, g_gu, g_d) = refs[8:15]
    (s_qkv, s_so, s_cq, s_ckv, s_co, s_gu, s_d) = refs[15:]
    whole = joined(refs[:6])
    total_at = sum(g.shape[1] for g in whole)
    steps = []
    at = 0
    for grad, (edges, names) in zip(whole, groups):
        width = grad.shape[1]
        col_mean = summed[:, at : at + width] / model_width + 1e-30
        at += width
        row_mean, mean_rows = [], []
        low = 0
        for edge, name in zip(edges, names):
            row_mean.append(rows[:, name : name + 1] / ((edge - low) * ways) + 1e-30)
            mean_rows.append(summed[:, total_at + name : total_at + name + 1] / model_width)
            low = edge
        factor = lane_pick(width, edges, row_mean) * col_mean / lane_pick(width, edges, mean_rows)
        steps.append(grad * lax.rsqrt(factor))
    for (f, b, a), (qkv, so, cq, ckv, co, gu, d) in (
        (whole, (g_qkv, g_so, g_cq, g_ckv, g_co, g_gu, g_d)),
        (steps, (s_qkv, s_so, s_cq, s_ckv, s_co, s_gu, s_d)),
    ):
        for k in range(3):
            qkv[k] = a[:, k * hq : (k + 1) * hq]
        so[...] = a[:, 3 * hq :]
        cq[...] = b[:, :hq]
        co[...] = b[:, 3 * hq :]
        d[...] = f[:, 2 * units :]
        for k in range(2):
            ckv[:, k, :] = b[:, (k + 1) * hq : (k + 2) * hq]
            gu[:, k, :] = f[:, k * units : (k + 1) * units]


def whole_block(array):
    return (array, full(array.shape))


def square_sums(grads, hq, units):
    own_rows = grads[0].shape[0]
    total = 4 * hq * 2 + 3 * units
    outs = [
        (sds((own_rows, 128), F32), full((own_rows, 128))),
        (sds((1, total), F32), full((1, total))),
    ]
    return run(
        functools.partial(square_sums_kernel, groups_of(hq, units)), 1,
        [whole_block(g) for g in grads], outs, [], 4 * own_rows * total, "square_sums",
    )


def message_of(rows, other, cols, gain_parts, hq, units):
    length = cols.shape[1] + 128 + sum(g.shape[1] for g in gain_parts)
    outs = [(sds(rows.shape, F32), full(rows.shape)), (sds((1, length), F32), full((1, length)))]
    return run(
        functools.partial(message_kernel, groups_of(hq, units), lax.axis_size("mp")), 1,
        [whole_block(g) for g in (rows, other, cols, *gain_parts)], outs, [], length, "message_sums",
    )


def updates(grads, rows, summed, model_width, hq, units):
    own_rows = grads[0].shape[0]
    shapes = [
        (3, own_rows, hq), (own_rows, hq), (own_rows, hq), (own_rows, 2, hq), (own_rows, hq),
        (own_rows, 2, units), (own_rows, units),
    ]
    outs = [(sds(shape, F32), full(shape)) for shape in shapes + shapes]
    results = run(
        functools.partial(update_kernel, groups_of(hq, units), lax.axis_size("mp"), model_width, hq, units),
        1, [whole_block(g) for g in (*grads, rows, summed)], outs, [], 8 * own_rows * (8 * hq + 3 * units),
        "updates",
    )
    results = list(results)
    results[0] = results[0].transpose(1, 0, 2)
    results[7] = results[7].transpose(1, 0, 2)
    return results


def on_device(
    tokens,
    memory,
    cotangent,
    table_lengths,
    table_plots,
    gains,
    w_qkv,
    w_self_out,
    w_cross_query,
    w_cross_kv,
    w_cross_out,
    w_gate_up,
    w_down,
):
    slots, width = tokens.shape
    hq = w_self_out.shape[1]
    heads = hq // DH
    units = w_down.shape[1]
    place = lax.axis_index("dp")
    x, z = place % 2, (place // 2) % 2
    ctl = jnp.stack([x, z]).astype(jnp.int32)
    gain_rows = gains.T
    gain_a, gain_b, gain_c = gain_rows[0:1], gain_rows[1:2], gain_rows[2:3]

    w_a = jnp.concatenate([w_qkv.transpose(1, 2, 0).reshape(3 * hq, width), w_self_out.T], axis=0)
    w_b = jnp.concatenate(
        [w_cross_query.T, w_cross_kv.transpose(1, 2, 0).reshape(2 * hq, width), w_cross_out.T], axis=0
    )
    w_f = jnp.concatenate(
        [w_gate_up.transpose(1, 2, 0).reshape(2 * units, width), w_down.T], axis=0
    )
    half_f = w_f.shape[0] // 2
    rows_b = w_b.shape[0] // 4
    ways = lax.axis_size("dp")

    ya0, ya1 = y_two(w_a, x, z)
    qkv0, mixed_a0, lse_a0, part = self_forward(table_lengths, tokens, gain_a, w_a, heads)
    send_bf = jnp.concatenate([y_piece_of_four(w_b, x, z), y_piece_of_four(w_f[:half_f], x, z)], axis=0)
    ya0, ya1, part, send_bf, memory_late = together(ya0, ya1, part, send_bf, memory)

    x_a, z_a = swap(ya0, "dp", 1), swap(ya1, "dp", 2)
    y_bf = swap(send_bf, "mp", 2)
    kv0, k0, v0 = memory_forward(memory_late, w_b, heads)
    send_f1 = y_pieces(w_f[half_f:], x, z)
    x_a, z_a, kv0, send_f1 = together(x_a, z_a, kv0, send_f1)
    far_a = (ya0, ya1, x_a, z_a)
    qkv1, mixed_a1, lse_a1, part, w_a1 = self_forward(
        table_lengths, tokens, gain_a, None, heads, remote=(ctl, far_a, part)
    )
    y_bf, part = together(y_bf, part)

    part_other = swap(part, "mp", 1)
    y_b, y_f0 = y_bf[:rows_b], y_bf[rows_b:]
    x_b, z_b = hand_on(y_b)
    x_b, z_b, part_other = together(x_b, z_b, part_other)
    far_z, far_x = hand_on_again(y_b, x_b, z_b)
    far_b = (y_b, x_b, z_b, far_z, far_x)
    x_f0, z_f0 = hand_on(y_f0)
    y_f1 = swap(after(send_f1, part_other), "mp", 2)
    q0, mixed_b0, lse_b0, part, first, normed_b = cross_forward(
        table_lengths, table_plots, w_b, kv0, k0, heads, lead=(tokens, part, part_other, gain_b),
    )
    far_b3, far_b4, x_f0, z_f0, part = together(far_b[3], far_b[4], x_f0, z_f0, part)
    far_b = far_b[:3] + (far_b3, far_b4)
    far_f0 = (y_f0, x_f0, z_f0) + hand_on_again(y_f0, x_f0, z_f0)
    kv1, k1, v1, w_b1 = memory_forward(memory, None, heads, remote=(ctl, far_b))
    q1, mixed_b1, lse_b1, part = cross_forward(
        table_lengths, table_plots, w_b1, kv1, k1, heads, follow=(normed_b, part)
    )
    y_f1, far_z, far_x, part = together(y_f1, far_f0[3], far_f0[4], part)
    far_f0 = far_f0[:3] + (far_z, far_x)

    part_other = swap(part, "mp", 1)
    x_f1, z_f1 = hand_on(y_f1)
    res, back, second, normed_c, *grad_f = feed(
        units, lead=(ctl, ways, first, part, part_other, gain_c, cotangent, w_f)
    )
    x_f1, z_f1, res, back, *grad_f = together(x_f1, z_f1, res, back, *grad_f)
    far_f = (far_f0, (y_f1, x_f1, z_f1))
    rs_f = halvings(grad_f)
    for rs in rs_f:
        rs.start()
    res, back = feed(units, follow=(ctl, normed_c, cotangent, far_f, res, back))
    back_other = swap(back, "mp", 1)
    back, back_mem, grad_second, branch_b, gain_grad_c, *grad_b = cross_backward(
        table_lengths, table_plots, w_b, q0, lse_b0, kv0, k0, v0, heads,
        lead=(ctl, ways, second, back, back_other, cotangent, gain_c, normed_b, memory, mixed_b0),
    )
    rs_f[0].got, rs_f[1].got, back, res, *grad_b = together(
        rs_f[0].got, rs_f[1].got, back, res, *grad_b
    )
    res_other = swap(res, "mp", 1)

    for rs in rs_f:
        rs.finish()
        rs.start()
    back, back_mem = cross_backward(
        table_lengths, table_plots, w_b1, q1, lse_b1, kv1, k1, v1, heads,
        follow=(branch_b, back, back_mem),
    )
    rs_f[0].got, rs_f[1].got, back, back_mem, res_other = together(
        rs_f[0].got, rs_f[1].got, back, back_mem, res_other
    )

    back_other = swap(back, "mp", 1)
    rs_b = halvings(grad_b)
    for rs in rs_b:
        rs.start()
    for rs in rs_f:
        rs.finish()
        rs.start()
    back, grad_first, branch_a, gain_grad_b, *grad_a = self_backward(
        table_lengths, w_a, qkv0, lse_a0, heads,
        lead=(ctl, ways, first, back, back_other, grad_second, gain_b, tokens, gain_a, mixed_a0),
    )
    rs_b[0].got, rs_b[1].got, rs_f[0].got, rs_f[1].got, back_mem, back, *grad_a = together(
        rs_b[0].got, rs_b[1].got, rs_f[0].got, rs_f[1].got, back_mem, back, *grad_a
    )
    mem_other = swap(back_mem, "mp", 1)

    rs_a = halvings(grad_a)
    for rs in rs_a:
        rs.start()
    for rs in rs_b:
        rs.finish()
        rs.start()
    (back,) = self_backward(table_lengths, w_a1, qkv1, lse_a1, heads, follow=(branch_a, back))
    rs_a[0].got, rs_a[1].got, rs_b[0].got, rs_b[1].got, back, mem_other, back_mem, res, res_other, second = together(
        rs_a[0].got, rs_a[1].got, rs_b[0].got, rs_b[1].got, back, mem_other, back_mem, res, res_other, second,
    )

    back_other = swap(back, "mp", 1)
    for rs in rs_a:
        rs.finish()
        rs.start()
    for rs in rs_b:
        rs.finish()
        rs.start()
    layer_out = (second + (res + res_other)).astype(BF16)
    rs_a[0].got, rs_a[1].got, back_other, layer_out = together(
        rs_a[0].got, rs_a[1].got, back_other, layer_out
    )
    for rs in rs_a:
        rs.finish()
        rs.start()
    grad_tokens, gain_grad_a = tail(tokens, back, back_other, grad_first, gain_a)
    for rs in rs_f + rs_b:
        rs.finish()
    grad_memory = back_mem + mem_other
    rs_a[0].got, rs_a[1].got, gain_grad_a, grad_memory = together(
        rs_a[0].got, rs_a[1].got, gain_grad_a, grad_memory
    )
    for rs in rs_a:
        rs.finish()
    grads = [rs.rest() for rs in rs_f + rs_b + rs_a]

    row_sums, col_sums = square_sums(grads, hq, units)
    row_sums = row_sums + swap(row_sums, "mp", 1)
    row_sums, message = message_of(
        row_sums, swap(row_sums, "mp", 2), col_sums, (gain_grad_a, gain_grad_b, gain_grad_c), hq, units
    )
    message = all_sum(message, "dp")
    results = updates(grads, row_sums, message, width, hq, units)
    own_rows = grads[0].shape[0]
    grad_gains = lax.dynamic_slice_in_dim(
        message[:, col_sums.shape[1] + 128 :].reshape(3, width), place * own_rows, own_rows, axis=1
    ).T
    return (layer_out, grad_tokens, grad_memory, grad_gains, *results)


def solution(mesh):
    split = P("dp", None)
    cols = P(None, "mp")
    cols3 = P(None, None, "mp")
    both = P("dp", "mp")
    both3 = P("dp", None, "mp")
    return jax.shard_map(
        on_device,
        mesh=mesh,
        in_specs=(
            split, split, split, split, split, P(),
            cols3, cols, cols, cols3, cols, cols3, cols,
        ),
        out_specs=(
            split, split, split, split,
            both3, both, both, both3, both, both3, both,
            both3, both, both, both3, both, both3, both,
        ),
        check_vma=False,
    )
```

```python
import functools
import math

import jax
import jax.numpy as jnp
from jax import lax
from jax.experimental import pallas as pl
from jax.experimental.pallas import tpu as pltpu
from jax.sharding import PartitionSpec as P

DH = 64
PATCH = 256
LONGEST = 512
ROWS = 256
SPAN = LONGEST // ROWS
F32 = jnp.float32
BF16 = jnp.bfloat16
NEG = -1e30
SCALE = 1.0 / math.sqrt(DH)
FREE, NEAR = "free", "near"
VMEM_BYTES = 30 * 1024 * 1024
SMALL = 1 << 15


def nn(a, b):
    return lax.dot_general(a, b, (((1,), (0,)), ((), ())), preferred_element_type=F32)


def nt(a, b):
    return lax.dot_general(a, b, (((1,), (1,)), ((), ())), preferred_element_type=F32)


def tn(a, b):
    return lax.dot_general(a, b, (((0,), (0,)), ((), ())), preferred_element_type=F32)


def normed_of(rows, gain):
    return rows * lax.rsqrt(jnp.mean(rows * rows, axis=-1, keepdims=True) + 1e-06) * gain


def norm_vjp(rows, gain, grad):
    inv = lax.rsqrt(jnp.mean(rows * rows, axis=-1, keepdims=True) + 1e-06)
    scaled = rows * inv
    hg = grad * gain
    inner = jnp.mean(hg * scaled, axis=-1, keepdims=True)
    grad_rows = inv * (hg - scaled * inner)
    grad_gain = jnp.sum(grad * scaled, axis=0, keepdims=True)
    return grad_rows, grad_gain, scaled


def place_pieces(dst, ctl, groups):
    x, z = ctl[0], ctl[1]
    base = 0
    for refs in groups:
        q = refs[0].shape[0] // 2
        if len(refs) == 1:
            dst[base : base + 2 * q, :] = refs[0][...].astype(BF16)
            base += 2 * q
        elif len(refs) == 8:
            q = 2 * q
            me, by_x = 2 * z + x, 2 * z + 1 - x
            by_z, far = 2 * (1 - z) + x, 2 * (1 - z) + 1 - x
            for k, who in enumerate((me, by_x, by_z, far)):
                for half in range(2):
                    offset = pl.multiple_of(base + (2 * who + half) * q, 16)
                    dst[pl.ds(offset, q), :] = refs[2 * k + half][...].astype(BF16)
            base += 8 * q
        elif len(refs) == 4:
            y0, y1, x0, z1 = refs
            q, r = y0.shape[0], y1.shape[0]
            for offset, ref in ((x * q, y0), ((1 - x) * q, x0), (2 * q + z * r, y1), (2 * q + (1 - z) * r, z1)):
                dst[pl.ds(pl.multiple_of(base + offset, 16), ref.shape[0]), :] = ref[...].astype(BF16)
            base += 2 * q + 2 * r
        elif len(refs) == 3:
            by_y, by_x, by_z = refs

            def put(offset, value, base=base, q=q):
                dst[pl.ds(pl.multiple_of(base + offset, 16), q), :] = value.astype(BF16)

            put(x * q, by_y[:q, :])
            put((1 - x) * q, by_x[...])
            put((2 + z) * q, by_y[q:, :])
            put((3 - z) * q, by_z[...])
            base += 4 * q
        else:
            y0, y1, by_x, by_z, far_z, far_x = refs
            q = 2 * q

            def put(who, half, value, base=base, q=q):
                dst[pl.ds(pl.multiple_of(base + who * (2 * q) + half * q, 16), q), :] = value.astype(BF16)

            me, other_x = 2 * z + x, 2 * z + 1 - x
            other_z, other = 2 * (1 - z) + x, 2 * (1 - z) + 1 - x
            put(me, 0, y0[...])
            put(me, 1, y1[...])
            put(other_x, 0, by_x[...])
            put(other_z, 1, by_z[...])
            put(other_z, 0, far_z[:q, :])
            put(other, 0, far_z[q:, :])
            put(other_x, 1, far_x[:q, :])
            put(other, 1, far_x[q:, :])
            base += 8 * q


def table_ends(lengths):
    ends = []
    total = lengths[0, 0]
    for j in range(1, lengths.shape[1]):
        ends.append(total)
        total = total + lengths[0, j]
    return ends


def query_places(base):
    return lax.broadcasted_iota(jnp.int32, (1, ROWS), 1) + base


def self_bias(lengths, base, low, width):
    places = query_places(base)
    start = jnp.zeros_like(places)
    for end in table_ends(lengths):
        start = jnp.where(places >= end, end, start)
    keys = lax.broadcasted_iota(jnp.int32, (width, ROWS), 0) + low
    return jnp.where((keys >= start) & (keys <= places), 0.0, NEG)


def window_cases(block, body):
    for back in range(SPAN + 1):
        width = (back + 1) * ROWS

        @pl.when(block == back if back < SPAN else block >= SPAN)
        def _run(back=back, width=width):
            if back < SPAN:
                body(0, width)
            else:
                body(pl.multiple_of((block - SPAN) * ROWS, ROWS), width)


def full(shape):
    return pl.BlockSpec(shape, lambda i: (0,) * len(shape))


def by_rows(width):
    return pl.BlockSpec((ROWS, width), lambda i: (i, 0))


def by_cols(height):
    return pl.BlockSpec((height, ROWS), lambda i: (0, i))


SMEM = pl.BlockSpec(memory_space=pltpu.SMEM)


def run(kernel, grid, ins, outs, scratch, flops, name, transcendentals=0):
    moved = sum(entry[0].size * entry[0].dtype.itemsize for entry in ins) + sum(
        math.prod(entry[0].shape) * jnp.dtype(entry[0].dtype).itemsize for entry in outs
    )
    arrays = [
        entry[0]
        if entry[-1] is FREE or entry[1] is SMEM or entry[0].size < SMALL
        else pltpu.with_memory_space_constraint(entry[0], pltpu.VMEM if entry[-1] is NEAR else pltpu.HBM)
        for entry in ins
    ]
    shapes = [
        entry[0]
        if entry[-1] is FREE or math.prod(entry[0].shape) < SMALL
        else (pltpu.VMEM if entry[-1] is NEAR else pltpu.HBM)(entry[0].shape, entry[0].dtype)
        for entry in outs
    ]
    return pl.pallas_call(
        kernel,
        grid=(grid,),
        in_specs=[entry[1] for entry in ins],
        out_specs=[entry[1] for entry in outs],
        out_shape=shapes,
        scratch_shapes=scratch,
        compiler_params=pltpu.CompilerParams(
            vmem_limit_bytes=VMEM_BYTES, dimension_semantics=("arbitrary",)
        ),
        cost_estimate=pl.CostEstimate(
            flops=flops // 64, bytes_accessed=moved // 64, transcendentals=transcendentals // 64
        ),
        name=name,
    )(*arrays)


def sds(shape, dtype):
    return jax.ShapeDtypeStruct(shape, dtype)


def self_forward_kernel(remote, heads, *refs):
    if remote:
        (lengths, ctl, tokens, gain, base_out) = refs[:5]
        pieces = refs[5:-6]
        (qkv_t, mixed_t, lse, out, w_out, k_rows) = refs[-6:]
        w = w_out
    else:
        (lengths, tokens, gain, w) = refs[:4]
        (qkv_t, mixed_t, lse, out, k_rows) = refs[4:]
    block = pl.program_id(0)
    hq = heads * DH
    if remote:

        @pl.when(block == 0)
        def _place():
            place_pieces(w, ctl, [pieces])

    base = pl.multiple_of(block * ROWS, ROWS)
    here = pl.ds(base, ROWS)
    normed = normed_of(tokens[...].astype(F32), gain[...]).astype(BF16)
    qkv = nt(w[0 : 3 * hq, :], normed).astype(BF16)
    q_all = (qkv[:hq].astype(F32) * SCALE).astype(BF16)
    qkv_t[0:hq, here] = q_all
    qkv_t[hq : 3 * hq, here] = qkv[hq:]
    for h in range(heads):
        k_rows[h, here, :] = qkv[hq + h * DH : hq + (h + 1) * DH].T

    def attend(low, width):
        window = pl.ds(low, width)
        bias = self_bias(lengths, base, low, width)
        for h in range(heads):
            own = slice(h * DH, (h + 1) * DH)
            s = nn(k_rows[h, window, :], q_all[own]) + bias
            top = jnp.max(s, axis=0, keepdims=True)
            e = jnp.exp(s - top)
            total = jnp.sum(e, axis=0, keepdims=True)
            o = nn(qkv_t[2 * hq + h * DH : 2 * hq + (h + 1) * DH, window], e.astype(BF16))
            mixed_t[own, :] = (o * (1.0 / total)).astype(BF16)
            lse[h : h + 1, :] = top + jnp.log(total)

    window_cases(block, attend)
    part = tn(mixed_t[...], w[3 * hq : 4 * hq, :])
    out[...] = part + base_out[...] if remote else part


def self_forward(lengths, tokens, gain, w, heads, remote=None):
    slots, width = tokens.shape
    hq = heads * DH
    outs = [
        (sds((3 * hq, slots), BF16), full((3 * hq, slots))),
        (sds((hq, slots), BF16), by_cols(hq)),
        (sds((8, slots), F32), by_cols(8)),
        (sds((slots, width), F32), by_rows(width), NEAR),
    ]
    scratch = [pltpu.VMEM((heads, slots, DH), BF16)]
    if remote is None:
        ins = [(lengths, SMEM), (tokens, by_rows(width)), (gain, full(gain.shape)), (w, full(w.shape))]
    else:
        ctl, pieces, base_out = remote
        ins = [
            (lengths, SMEM),
            (ctl, SMEM),
            (tokens, by_rows(width)),
            (gain, full(gain.shape)),
            (base_out, by_rows(width), NEAR),
        ]
        ins += [(piece, full(piece.shape)) for piece in pieces]
        outs.append((sds((4 * hq, width), BF16), full((4 * hq, width))))
    flops = 2 * slots * width * 4 * hq + heads * 4 * slots * slots * DH
    return run(
        functools.partial(self_forward_kernel, remote is not None, heads),
        slots // ROWS, ins, outs, scratch, flops, "self_forward", heads * slots * slots,
    )


def memory_kernel(hq, memory, w, kv_t):
    kv_t[...] = nt(w[hq : 3 * hq, :], memory[...]).astype(BF16)


def memory_forward(memory, w, heads):
    count, width = memory.shape
    hq = heads * DH
    (kv_t,) = run(
        functools.partial(memory_kernel, hq), count // ROWS,
        [(memory, by_rows(width)), (w, full(w.shape))],
        [(sds((2 * hq, count), BF16), by_cols(2 * hq))], [], 2 * count * width * 2 * hq, "memory_forward",
    )
    return kv_t


def rows_of_heads(rows, columns, heads):
    for h in range(heads):
        rows[h] = columns[h * DH : (h + 1) * DH, :].T


def tables_of_block(lengths, base, body):
    ends = table_ends(lengths)
    places = query_places(base)
    segment = jnp.zeros_like(places)
    first_table = jnp.int32(0)
    last_table = jnp.int32(0)
    for end in ends:
        segment = segment + (places >= end).astype(jnp.int32)
        first_table = first_table + (base >= end).astype(jnp.int32)
        last_table = last_table + (base + ROWS - 1 >= end).astype(jnp.int32)

    def step(table, carry):
        body(table, segment == table)
        return carry

    lax.fori_loop(first_table, last_table + 1, step, 0)


def cross_forward_kernel(leading, heads, *refs):
    hq = heads * DH
    k_rows = refs[-1]
    if leading:
        (lengths, plots, tokens, part, other, gain, w, kv_t) = refs[:8]
        (q_t, mixed_t, lse, out, first, normed_out) = refs[8:-1]
    else:
        (lengths, plots, ctl, normed_in, memory, base_out) = refs[:6]
        (q_t, mixed_t, lse, out, w, kv_t) = refs[-7:-1]

    @pl.when(pl.program_id(0) == 0)
    def _start():
        if not leading:
            place_pieces(w, ctl, [refs[6:-7]])
            for m in range(memory.shape[0] // ROWS):
                here = slice(m * ROWS, (m + 1) * ROWS)
                kv_t[:, here] = nt(w[hq : 3 * hq, :], memory[here, :]).astype(BF16)
        rows_of_heads(k_rows, kv_t, heads)

    if leading:
        rows = tokens[...].astype(F32) + (part[...] + other[...])
        first[...] = rows
        normed = normed_of(rows, gain[...]).astype(BF16)
        normed_out[...] = normed
    else:
        normed = normed_in[...]
    base = pl.multiple_of(pl.program_id(0) * ROWS, ROWS)
    query = nt(w[0:hq, :], normed).astype(BF16)
    q_all = (query.astype(F32) * SCALE).astype(BF16)
    q_t[...] = q_all

    def table(j, member):
        plot = pl.ds(pl.multiple_of(plots[0, j] * PATCH, PATCH), PATCH)
        for h in range(heads):
            own = slice(h * DH, (h + 1) * DH)
            s = nn(k_rows[h, plot, :], q_t[own, :])
            top = jnp.max(s, axis=0, keepdims=True)
            e = jnp.exp(s - top)
            total = jnp.sum(e, axis=0, keepdims=True)
            o = nn(kv_t[hq + h * DH : hq + (h + 1) * DH, plot], e.astype(BF16))
            o = o * (1.0 / total)
            mixed_t[own, :] = jnp.where(member, o, mixed_t[own, :].astype(F32)).astype(BF16)
            lse[h : h + 1, :] = jnp.where(member, top + jnp.log(total), lse[h : h + 1, :])

    tables_of_block(lengths, base, table)
    part_out = tn(mixed_t[...], w[3 * hq : 4 * hq, :])
    out[...] = part_out if leading else part_out + base_out[...]


def cross_forward(lengths, plots, heads, lead=None, follow=None):
    hq = heads * DH
    slots, width = (lead or follow)[0].shape
    outs = [
        (sds((hq, slots), BF16), by_cols(hq)),
        (sds((hq, slots), BF16), by_cols(hq)),
        (sds((8, slots), F32), by_cols(8)),
        (sds((slots, width), F32), by_rows(width), NEAR),
    ]
    if lead is not None:
        tokens, part, other, gain, w, kv_t = lead
        count = kv_t.shape[1]
        ins = [
            (lengths, SMEM),
            (plots, SMEM),
            (tokens, by_rows(width)),
            (part, by_rows(width), NEAR),
            (other, by_rows(width), NEAR),
            (gain, full(gain.shape)),
            (w, full(w.shape)),
            (kv_t, full(kv_t.shape)),
        ]
        outs += [
            (sds((slots, width), F32), by_rows(width)),
            (sds((slots, width), BF16), by_rows(width)),
        ]
    else:
        normed, ctl, memory, base_out, pieces = follow
        count = memory.shape[0]
        ins = [
            (lengths, SMEM),
            (plots, SMEM),
            (ctl, SMEM),
            (normed, by_rows(width)),
            (memory, full(memory.shape)),
            (base_out, by_rows(width), NEAR),
        ]
        ins += [(piece, full(piece.shape)) for piece in pieces]
        outs += [
            (sds((4 * hq, width), BF16), full((4 * hq, width))),
            (sds((2 * hq, count), BF16), full((2 * hq, count))),
        ]
    flops = 2 * slots * width * 2 * hq + heads * 8 * slots * PATCH * DH
    return run(
        functools.partial(cross_forward_kernel, lead is not None, heads),
        slots // ROWS, ins, outs, [pltpu.VMEM((heads, count, DH), BF16)], flops, "cross_forward",
        heads * slots * PATCH * 2,
    )


def gradient_outs(count, rows, width):
    if split_bits(rows, count):
        half = (rows // 2, width // 2)
        return [(sds(half, F32), full(half)) for _ in range(4)]
    return [(sds((rows, width), F32), full((rows, width)))]


def finish_gradient(count, ctl, source, outs):
    @pl.when(pl.program_id(0) == pl.num_programs(0) - 1)
    def _write():
        if len(outs) == 1:
            outs[0][...] = source[...]
        else:
            half = source.shape[1] // 2
            write_split(source, 0, half, count, 1, ctl[0], outs[0], outs[1])
            write_split(source, half, 2 * half, count, 2, ctl[1], outs[2], outs[3])


def halvings(outs):
    if len(outs) == 1:
        half = outs[0].shape[1] // 2
        return Halving(outs[0][:, :half], (1, 2, 4)), Halving(outs[0][:, half:], (2, 1, 4))
    return Halving(None, (1, 2, 4), outs[0:2]), Halving(None, (2, 1, 4), outs[2:4])


def feed_kernel(leading, units, count, *refs):
    if leading:
        (ctl, first, part, other, gain, cot, w) = refs[:7]
        (result, grad_in, second, normed_out) = refs[7:11]
        dw_outs, dw = refs[11:-1], refs[-1]
        rows = first[...] + (part[...] + other[...])
        second[...] = rows
        normed = normed_of(rows, gain[...]).astype(BF16)
        normed_out[...] = normed

        @pl.when(pl.program_id(0) == 0)
        def _zero():
            dw[...] = jnp.zeros_like(dw)
    else:
        (ctl, normed_in, cot, base_result, base_grad) = refs[:5]
        pieces = refs[5:-3]
        (result, grad_in, w) = refs[-3:]
        normed = normed_in[...]

        @pl.when(pl.program_id(0) == 0)
        def _place():
            place_pieces(w, ctl, [pieces[:6], pieces[6:]])

    cot_rows = cot[...]
    gate_up = nt(normed, w[0 : 2 * units, :])
    gate, up = gate_up[:, :units], gate_up[:, units:]
    c0 = math.sqrt(2.0 / math.pi)
    square = gate * gate
    th = jnp.tanh(c0 * gate * (1.0 + 0.044715 * square))
    half = 0.5 * (1.0 + th)
    gelu = gate * half
    slope = half + (0.5 * c0) * gate * (1.0 - th * th) * (1.0 + (3 * 0.044715) * square)
    hidden = (gelu * up).astype(BF16)
    res = nn(hidden, w[2 * units : 3 * units, :])
    grad_hidden = nt(cot_rows, w[2 * units : 3 * units, :])
    grad_gate = (grad_hidden * up * slope).astype(BF16)
    grad_up = (grad_hidden * gelu).astype(BF16)
    back = nn(grad_gate, w[0:units, :]) + nn(grad_up, w[units : 2 * units, :])
    if leading:
        result[...] = res
        grad_in[...] = back
        turned = normed.T
        dw[:, 0:units] += nn(turned, grad_gate)
        dw[:, units : 2 * units] += nn(turned, grad_up)
        dw[:, 2 * units : 3 * units] += tn(cot_rows, hidden)
        finish_gradient(count, ctl, dw, dw_outs)
    else:
        result[...] = res + base_result[...]
        grad_in[...] = back + base_grad[...]


def feed(units, lead=None, follow=None):
    if lead is not None:
        ctl, count, first, part, other, gain, cot, w = lead
        slots, width = first.shape
        ins = [
            (ctl, SMEM),
            (first, by_rows(width)),
            (part, by_rows(width), NEAR),
            (other, by_rows(width), NEAR),
            (gain, full(gain.shape)),
            (cot, by_rows(width)),
            (w, full(w.shape)),
        ]
    else:
        ctl, normed, cot, pieces, base_result, base_grad = follow
        slots, width = normed.shape
        ins = [(ctl, SMEM), (normed, by_rows(width), FREE), (cot, by_rows(width))]
        ins += [(base_result, by_rows(width), FREE), (base_grad, by_rows(width), NEAR)]
        ins += [(piece, full(piece.shape)) for group in pieces for piece in group]
    outs = [
        (sds((slots, width), F32), by_rows(width), FREE),
        (sds((slots, width), F32), by_rows(width), NEAR),
    ]
    scratch = []
    if lead is not None:
        outs += [
            (sds((slots, width), F32), by_rows(width)),
            (sds((slots, width), BF16), by_rows(width), FREE),
        ]
        outs += gradient_outs(count, width, 3 * units)
        scratch = [pltpu.VMEM((width, 3 * units), F32)]
    else:
        count = 0
        scratch = [pltpu.VMEM((3 * units, width), BF16)]
    flops = 2 * slots * width * units * (9 if lead is not None else 6)
    return run(
        functools.partial(feed_kernel, lead is not None, units, count),
        slots // ROWS, ins, outs, scratch, flops, "feed", slots * units,
    )


def cross_backward_kernel(leading, heads, count, *refs):
    hq = heads * DH
    if leading:
        (ctl, lengths, plots, second, part, other, cot, gain, normed, memory) = refs[:10]
        (w, q_t, mixed_t, lse, kv_t) = refs[10:15]
        (grad_in, grad_mem, grad_second, branch_out, grad_gain) = refs[15:20]
        dw_outs = refs[20:-7]
        (dkv, dq, dm, k_rows, v_rows, dw_t, dw) = refs[-7:]
    else:
        (lengths, plots, branch_in, w, q_t, mixed_t, lse, kv_t, base_grad, base_mem) = refs[:10]
        (grad_in, grad_mem, dkv, dq, dm, k_rows, v_rows) = refs[10:]
    block = pl.program_id(0)
    last = pl.num_programs(0) - 1
    base = pl.multiple_of(block * ROWS, ROWS)

    @pl.when(block == 0)
    def _zero():
        dkv[...] = jnp.zeros_like(dkv)
        rows_of_heads(k_rows, kv_t[0:hq, :], heads)
        rows_of_heads(v_rows, kv_t[hq : 2 * hq, :], heads)
        if leading:
            dw_t[...] = jnp.zeros_like(dw_t)
            grad_gain[...] = jnp.zeros_like(grad_gain)

    if leading:
        grad_rows, gain_rows, _ = norm_vjp(second[...], gain[...], part[...] + other[...])
        total = cot[...].astype(F32) + grad_rows
        grad_second[...] = total
        branch = total.astype(BF16)
        branch_out[...] = branch
        grad_gain[0:1, :] += gain_rows
    else:
        branch = branch_in[...]
    dm[...] = nt(w[3 * hq : 4 * hq, :], branch).astype(BF16)
    dq[...] = jnp.zeros_like(dq)

    def table(j, member):
        plot = pl.ds(pl.multiple_of(plots[0, j] * PATCH, PATCH), PATCH)
        for h in range(heads):
            own = slice(h * DH, (h + 1) * DH)
            val = slice(hq + h * DH, hq + (h + 1) * DH)
            query = q_t[own, :]
            dmix = jnp.where(member, dm[own, :].astype(F32), 0.0).astype(BF16)
            level = jnp.where(member, lse[h : h + 1, :], -NEG)
            p = jnp.exp(nn(k_rows[h, plot, :], query) - level)
            dp = nn(v_rows[h, plot, :], dmix)
            inner = jnp.sum(dmix.astype(F32) * mixed_t[own, :].astype(F32), axis=0, keepdims=True)
            ds = (p * (dp - inner)).astype(BF16)
            dkv[own, plot] += nt(query, ds)
            dkv[val, plot] += nt(dmix, p.astype(BF16))
            dq[own, :] += nn(kv_t[own, plot], ds)

    tables_of_block(lengths, base, table)
    grad_query = (dq[...] * SCALE).astype(BF16)
    back = tn(grad_query, w[0:hq, :])
    grad_in[...] = back if leading else back + base_grad[...]
    if leading:
        dw_t[0:hq, :] += nn(grad_query, normed[...])
        dw_t[3 * hq : 4 * hq, :] += nn(mixed_t[...], branch)

    @pl.when(block == last)
    def _finish():
        for m in range(dkv.shape[1] // ROWS):
            here = slice(m * ROWS, (m + 1) * ROWS)
            rows = dkv[:, here].astype(BF16)
            back_mem = tn(rows, w[hq : 3 * hq, :])
            grad_mem[here, :] = back_mem if leading else back_mem + base_mem[here, :]
            if leading:
                dw_t[hq : 3 * hq, :] += nn(rows, memory[here, :])
        if leading:
            dw[...] = dw_t[...].T

    if leading:
        finish_gradient(count, ctl, dw, dw_outs)


def cross_backward(lengths, plots, w, q_t, lse, kv_t, heads, lead=None, follow=None):
    hq = heads * DH
    slots, width = q_t.shape[1], w.shape[1]
    count = kv_t.shape[1]
    outs = [
        (sds((slots, width), F32), by_rows(width), NEAR),
        (sds((count, width), F32), full((count, width)), NEAR if lead is not None else None),
    ]
    scratch = [
        pltpu.VMEM((2 * hq, count), F32),
        pltpu.VMEM((hq, ROWS), F32),
        pltpu.VMEM((hq, ROWS), BF16),
        pltpu.VMEM((heads, count, DH), BF16),
        pltpu.VMEM((heads, count, DH), BF16),
    ]
    heads_part = [
        (lse, by_cols(8)),
        (kv_t, full(kv_t.shape)),
    ]
    if lead is not None:
        ctl, split, second, part, other, cot, gain, normed, memory, mixed_t = lead
        ins = [
            (ctl, SMEM),
            (lengths, SMEM),
            (plots, SMEM),
            (second, by_rows(width)),
            (part, by_rows(width), NEAR),
            (other, by_rows(width), NEAR),
            (cot, by_rows(width)),
            (gain, full(gain.shape)),
            (normed, by_rows(width)),
            (memory, full(memory.shape)),
            (w, full(w.shape)),
            (q_t, by_cols(hq)),
            (mixed_t, by_cols(hq)),
        ] + heads_part
        outs += [
            (sds((slots, width), F32), by_rows(width), FREE),
            (sds((slots, width), BF16), by_rows(width), FREE),
            (sds((8, width), F32), full((8, width))),
        ]
        outs += gradient_outs(split, width, 4 * hq)
        scratch += [pltpu.VMEM((4 * hq, width), F32), pltpu.VMEM((width, 4 * hq), F32)]
    else:
        split = 0
        branch, base_grad, base_mem, mixed_t = follow
        ins = [
            (lengths, SMEM),
            (plots, SMEM),
            (branch, by_rows(width), FREE),
            (w, full(w.shape)),
            (q_t, by_cols(hq)),
            (mixed_t, by_cols(hq)),
        ] + heads_part
        ins += [(base_grad, by_rows(width), NEAR), (base_mem, full(base_mem.shape), NEAR)]
    flops = 2 * slots * width * hq * (8 if lead is not None else 4) + heads * 20 * slots * PATCH * DH
    return run(
        functools.partial(cross_backward_kernel, lead is not None, heads, split),
        slots // ROWS, ins, outs, scratch, flops, "cross_backward", heads * slots * PATCH * 2,
    )


def self_backward_kernel(leading, heads, count, *refs):
    hq = heads * DH
    if leading:
        (ctl, lengths, first, part, other, carried, gain, tokens, gain_in, w, qkv_t, mixed_t, lse) = refs[:13]
        (grad_in, grad_first, branch_out, grad_gain) = refs[13:17]
        dw_outs = refs[17:-6]
        (dkv, k_rows, v_rows, dqkv, dw_t, dw) = refs[-6:]
    else:
        (lengths, branch_in, w, qkv_t, mixed_t, lse, base_grad) = refs[:7]
        (grad_in, dkv, k_rows, v_rows, dqkv) = refs[7:]
    step = pl.program_id(0)
    last = pl.num_programs(0) - 1
    block = last - step
    base = pl.multiple_of(block * ROWS, ROWS)
    here = pl.ds(base, ROWS)

    @pl.when(step == 0)
    def _start():
        dkv[...] = jnp.zeros_like(dkv)
        for h in range(heads):
            k_rows[h] = qkv_t[hq + h * DH : hq + (h + 1) * DH, :].T
            v_rows[h] = qkv_t[2 * hq + h * DH : 2 * hq + (h + 1) * DH, :].T
        if leading:
            dw_t[...] = jnp.zeros_like(dw_t)
            grad_gain[...] = jnp.zeros_like(grad_gain)

    if leading:
        grad_rows, gain_rows, _ = norm_vjp(first[...], gain[...], part[...] + other[...])
        total = carried[...] + grad_rows
        grad_first[...] = total
        branch = total.astype(BF16)
        branch_out[...] = branch
        grad_gain[0:1, :] += gain_rows
    else:
        branch = branch_in[...]
    dm_all = nt(w[3 * hq : 4 * hq, :], branch).astype(BF16)

    def attend(low, width):
        window = pl.ds(low, width)
        bias = self_bias(lengths, base, low, width)
        for h in range(heads):
            own = slice(h * DH, (h + 1) * DH)
            key = slice(hq + h * DH, hq + (h + 1) * DH)
            val = slice(hq + h * DH, hq + (h + 1) * DH)
            query = qkv_t[own, here]
            dmix = dm_all[own]
            p = jnp.exp(nn(k_rows[h, window, :], query) + bias - lse[h : h + 1, :])
            dp = nn(v_rows[h, window, :], dmix)
            inner = jnp.sum(dmix.astype(F32) * mixed_t[own, :].astype(F32), axis=0, keepdims=True)
            ds = (p * (dp - inner)).astype(BF16)
            dkv[own, window] += nt(query, ds)
            dkv[val, window] += nt(dmix, p.astype(BF16))
            dqkv[own, :] = (nn(qkv_t[key, window], ds) * SCALE).astype(BF16)

    window_cases(block, attend)
    dqkv[hq : 3 * hq, :] = dkv[:, here].astype(BF16)
    rows = dqkv[...]
    back = tn(rows, w[0 : 3 * hq, :])
    grad_in[...] = back if leading else back + base_grad[...]
    if leading:
        normed = normed_of(tokens[...].astype(F32), gain_in[...]).astype(BF16)
        dw_t[0 : 3 * hq, :] += nn(rows, normed)
        dw_t[3 * hq : 4 * hq, :] += nn(mixed_t[...], branch)

        @pl.when(step == last)
        def _finish():
            dw[...] = dw_t[...].T

        finish_gradient(count, ctl, dw, dw_outs)


def self_backward(lengths, w, qkv_t, lse, heads, lead=None, follow=None):
    hq = heads * DH
    slots, width = qkv_t.shape[1], w.shape[1]
    last = slots // ROWS - 1
    rows = pl.BlockSpec((ROWS, width), lambda i: (last - i, 0))

    def cols(height):
        return pl.BlockSpec((height, ROWS), lambda i: (0, last - i))

    outs = [(sds((slots, width), F32), rows, NEAR)]
    scratch = [
        pltpu.VMEM((2 * hq, slots), F32),
        pltpu.VMEM((heads, slots, DH), BF16),
        pltpu.VMEM((heads, slots, DH), BF16),
        pltpu.VMEM((3 * hq, ROWS), BF16),
    ]
    if lead is not None:
        ctl, count, first, part, other, carried, gain, tokens, gain_in, mixed_t = lead
        ins = [
            (ctl, SMEM),
            (lengths, SMEM),
            (first, rows),
            (part, rows, NEAR),
            (other, rows, NEAR),
            (carried, rows, FREE),
            (gain, full(gain.shape)),
            (tokens, rows),
            (gain_in, full(gain_in.shape)),
            (w, full(w.shape)),
            (qkv_t, full(qkv_t.shape)),
            (mixed_t, cols(hq)),
            (lse, cols(8)),
        ]
        outs += [
            (sds((slots, width), F32), rows, FREE),
            (sds((slots, width), BF16), rows, FREE),
            (sds((8, width), F32), full((8, width))),
        ]
        outs += gradient_outs(count, width, 4 * hq)
        scratch += [pltpu.VMEM((4 * hq, width), F32), pltpu.VMEM((width, 4 * hq), F32)]
    else:
        count = 0
        branch, base_grad, mixed_t = follow
        ins = [
            (lengths, SMEM),
            (branch, rows, FREE),
            (w, full(w.shape)),
            (qkv_t, full(qkv_t.shape)),
            (mixed_t, cols(hq)),
            (lse, cols(8)),
            (base_grad, rows, NEAR),
        ]
    flops = 2 * slots * width * hq * (8 if lead is not None else 4) + heads * 10 * slots * slots * DH
    return run(
        functools.partial(self_backward_kernel, lead is not None, heads, count),
        slots // ROWS, ins, outs, scratch, flops, "self_backward", heads * slots * slots,
    )


def tail_kernel(tokens, part, other, carried, gain, grad_tokens, grad_gain):
    @pl.when(pl.program_id(0) == 0)
    def _zero():
        grad_gain[...] = jnp.zeros_like(grad_gain)

    grad_rows, gain_rows, _ = norm_vjp(tokens[...].astype(F32), gain[...], part[...] + other[...])
    grad_tokens[...] = carried[...] + grad_rows
    grad_gain[0:1, :] += gain_rows


def tail(tokens, part, other, carried, gain):
    slots, width = tokens.shape
    ins = [
        (tokens, by_rows(width)),
        (part, by_rows(width), NEAR),
        (other, by_rows(width), NEAR),
        (carried, by_rows(width), FREE),
        (gain, full(gain.shape)),
    ]
    outs = [
        (sds((slots, width), F32), by_rows(width)),
        (sds((8, width), F32), full((8, width))),
    ]
    return run(tail_kernel, slots // ROWS, ins, outs, [], 20 * slots * width, "last_norm")


def swap(value, axis, bit):
    count = lax.axis_size(axis)
    return lax.ppermute(value, axis, [(i, i ^ bit) for i in range(count)])


def after(value, *others):
    return lax.optimization_barrier((value,) + others)[0]


def y_pieces(w, x, z):
    quarter = w.shape[0] // 4
    pieces = w.reshape(4, quarter, w.shape[1])
    mine = jnp.concatenate(
        [jnp.where(x == 0, pieces[0], pieces[1]), jnp.where(z == 0, pieces[2], pieces[3])], axis=0
    )
    return mine.astype(F32)


def hand_on(by_y):
    quarter = by_y.shape[0] // 2
    return swap(by_y[:quarter], "dp", 1), swap(by_y[quarter:], "dp", 2)


def hand_on_again(y0, y1, by_x, by_z):
    far_z = swap(jnp.concatenate([y0, by_x], axis=0), "dp", 2)
    far_x = swap(jnp.concatenate([y1, by_z], axis=0), "dp", 1)
    return far_z, far_x


def halves_of_quarter(w, x, z):
    eighth = w.shape[0] // 8
    start = (2 * z + x) * 2 * eighth
    halves = [lax.dynamic_slice_in_dim(w, start + k * eighth, eighth, axis=0) for k in range(2)]
    return [half.astype(F32) for half in halves]


def together(*values):
    return lax.optimization_barrier(values)


def split_bits(grad_rows, count):
    return count >= 4 and (grad_rows // count) % 8 == 0


def write_split(source, low, high, count, bit, mine, sent, kept):
    own = source.shape[0] // count
    for r in range(count // 2):
        base = (r // bit) * 2 * bit + r % bit
        rows = slice(r * own, (r + 1) * own)
        kept[rows, :] = source[pl.ds(pl.multiple_of((base + mine * bit) * own, 8), own), low:high]
        sent[rows, :] = source[pl.ds(pl.multiple_of((base + (1 - mine) * bit) * own, 8), own), low:high]


def last_bits(pair):
    for rs in pair:
        rs.finish()
    both = Halving.__new__(Halving)
    both.__dict__.update(pair[0].__dict__)
    both.grad = jnp.concatenate([rs.grad for rs in pair], axis=-1)
    return both


class Halving:
    def __init__(self, grad, order, halves=None):
        self.halves = halves
        self.count = lax.axis_size("dp")
        self.place = lax.axis_index("dp")
        self.order = list(order)
        bit = 8
        while bit < self.count:
            self.order.append(bit)
            bit *= 2
        self.left = [b for b in (1 << k for k in range(self.count.bit_length() - 1))][::-1]
        if halves is None:
            self.grad = grad.reshape((2,) * len(self.left) + (grad.shape[0] // self.count, grad.shape[1]))

    def send(self):
        bit = self.order.pop(0)
        axis = self.left.index(bit)
        self.left.pop(axis)
        if self.halves is not None:
            sent, kept = self.halves
            self.halves = None
            shape = (2,) * len(self.left) + (kept.shape[0] * 2 // self.count, kept.shape[1])
            self.kept = kept.reshape(shape)
            return sent.reshape(shape), bit
        mine = (self.place // bit) % 2
        sent = lax.dynamic_index_in_dim(self.grad, 1 - mine, axis=axis, keepdims=False)
        self.kept = lax.dynamic_index_in_dim(self.grad, mine, axis=axis, keepdims=False)
        return sent, bit

    def start(self, *others):
        sent, bit = self.send()
        shape = sent.shape
        flat = sent.reshape(-1, shape[-1])
        if others:
            flat = after(flat, *others)
        self.flat = flat
        self.got = swap(flat, "dp", bit)

    def finish(self):
        self.grad = self.kept + self.got.reshape(self.kept.shape)

    def rest(self):
        while self.order:
            self.start()
            self.finish()
        return self.grad.reshape(-1, self.grad.shape[-1])


def exchange_sums(value, axis):
    bit = 1
    while bit * 2 < lax.axis_size(axis):
        value = value + swap(value, axis, bit)
        bit *= 2
    return [value, swap(value, axis, bit)]


def lane_pick(width, edges, values):
    lanes = lax.broadcasted_iota(jnp.int32, (1, width), 1)
    picked = values[-1]
    for edge, value in zip(edges[-2::-1], values[-2::-1]):
        picked = jnp.where(lanes < edge, value, picked)
    return picked


def groups_of(hq, units):
    return (
        ((2 * units, 3 * units), (0, 1)),
        ((hq, 3 * hq, 4 * hq), (2, 3, 4)),
        ((3 * hq, 4 * hq), (5, 6)),
    )


def joined(refs):
    return tuple(ref[...] for ref in refs)


def square_sums_kernel(groups, *refs):
    rows, cols = refs[3:]
    places = lax.broadcasted_iota(jnp.int32, (1, rows.shape[1]), 1)
    sums = jnp.zeros(rows.shape, F32)
    at = 0
    for grad, (edges, names) in zip(joined(refs[:3]), groups):
        square = grad * grad
        cols[:, at : at + grad.shape[1]] = jnp.sum(square, axis=0, keepdims=True)
        at += grad.shape[1]
        lanes = lax.broadcasted_iota(jnp.int32, (1, grad.shape[1]), 1)
        low = 0
        for edge, name in zip(edges, names):
            inside = (lanes >= low) & (lanes < edge)
            total = jnp.sum(jnp.where(inside, square, 0.0), axis=1, keepdims=True)
            sums = jnp.where(places == name, total, sums)
            low = edge
    rows[...] = sums


def message_kernel(groups, ways, rows, other, cols, gain_a, gain_b, gain_c, rows_out, message):
    total = rows[...] + other[...]
    rows_out[...] = total
    places = lax.broadcasted_iota(jnp.int32, (1, total.shape[1]), 1)
    scale = jnp.zeros((1, total.shape[1]), F32)
    for edges, names in groups:
        low = 0
        for edge, name in zip(edges, names):
            scale = jnp.where(places == name, 1.0 / ((edge - low) * ways), scale)
            low = edge
    at = cols.shape[1]
    message[:, :at] = cols[...]
    message[:, at : at + 128] = jnp.sum(total * scale + 1e-30, axis=0, keepdims=True)
    at += 128
    for gain in (gain_a, gain_b, gain_c):
        message[:, at : at + gain.shape[1]] = gain[0:1, :]
        at += gain.shape[1]


def update_kernel(groups, ways, model_width, hq, units, *refs):
    rows = refs[3]
    (g_qkv, g_so, g_cq, g_ckv, g_co, g_gu, g_d) = refs[-15:-8]
    (s_qkv, s_so, s_cq, s_ckv, s_co, s_gu, s_d, summed) = refs[-8:]
    summed[...] = refs[4][...] + refs[5][...]
    whole = joined(refs[:3])
    total_at = sum(g.shape[1] for g in whole)
    steps = []
    at = 0
    for grad, (edges, names) in zip(whole, groups):
        width = grad.shape[1]
        col_mean = summed[:, at : at + width] / model_width + 1e-30
        at += width
        row_mean, mean_rows = [], []
        low = 0
        for edge, name in zip(edges, names):
            row_mean.append(rows[:, name : name + 1] / ((edge - low) * ways) + 1e-30)
            mean_rows.append(summed[:, total_at + name : total_at + name + 1] / model_width)
            low = edge
        factor = lane_pick(width, edges, row_mean) * col_mean / lane_pick(width, edges, mean_rows)
        steps.append(grad * lax.rsqrt(factor))
    for (f, b, a), (qkv, so, cq, ckv, co, gu, d) in (
        (whole, (g_qkv, g_so, g_cq, g_ckv, g_co, g_gu, g_d)),
        (steps, (s_qkv, s_so, s_cq, s_ckv, s_co, s_gu, s_d)),
    ):
        for k in range(3):
            qkv[k] = a[:, k * hq : (k + 1) * hq]
        so[...] = a[:, 3 * hq :]
        cq[...] = b[:, :hq]
        co[...] = b[:, 3 * hq :]
        d[...] = f[:, 2 * units :]
        for k in range(2):
            ckv[:, k, :] = b[:, (k + 1) * hq : (k + 2) * hq]
            gu[:, k, :] = f[:, k * units : (k + 1) * units]


def whole_block(array):
    return (array, full(array.shape))


def square_sums(grads, hq, units):
    own_rows = grads[0].shape[0]
    total = 4 * hq * 2 + 3 * units
    outs = [
        (sds((own_rows, 128), F32), full((own_rows, 128))),
        (sds((1, total), F32), full((1, total))),
    ]
    return run(
        functools.partial(square_sums_kernel, groups_of(hq, units)), 1,
        [whole_block(g) for g in grads], outs, [], 4 * own_rows * total, "square_sums",
    )


def message_of(rows, other, cols, gain_parts, hq, units):
    length = cols.shape[1] + 128 + sum(g.shape[1] for g in gain_parts)
    outs = [(sds(rows.shape, F32), full(rows.shape)), (sds((1, length), F32), full((1, length)))]
    return run(
        functools.partial(message_kernel, groups_of(hq, units), lax.axis_size("mp")), 1,
        [whole_block(g) for g in (rows, other, cols, *gain_parts)], outs, [], length, "message_sums",
    )


def updates(grads, rows, parts, model_width, hq, units):
    own_rows = grads[0].shape[0]
    shapes = [
        (3, own_rows, hq), (own_rows, hq), (own_rows, hq), (own_rows, 2, hq), (own_rows, hq),
        (own_rows, 2, units), (own_rows, units),
    ]
    outs = [(sds(shape, F32), full(shape)) for shape in shapes + shapes + [parts[0].shape]]
    results = run(
        functools.partial(update_kernel, groups_of(hq, units), lax.axis_size("mp"), model_width, hq, units),
        1, [whole_block(g) for g in (*grads, rows, *parts)], outs, [], 8 * own_rows * (8 * hq + 3 * units),
        "updates",
    )
    results = list(results)
    results[0] = results[0].transpose(1, 0, 2)
    results[7] = results[7].transpose(1, 0, 2)
    return results


def on_device(
    tokens,
    memory,
    cotangent,
    table_lengths,
    table_plots,
    gains,
    w_qkv,
    w_self_out,
    w_cross_query,
    w_cross_kv,
    w_cross_out,
    w_gate_up,
    w_down,
):
    slots, width = tokens.shape
    hq = w_self_out.shape[1]
    heads = hq // DH
    units = w_down.shape[1]
    place = lax.axis_index("dp")
    x, z = place % 2, (place // 2) % 2
    ctl = jnp.stack([x, z]).astype(jnp.int32)
    gain_rows = gains.T
    gain_a, gain_b, gain_c = gain_rows[0:1], gain_rows[1:2], gain_rows[2:3]

    w_a = jnp.concatenate([w_qkv.transpose(1, 2, 0).reshape(3 * hq, width), w_self_out.T], axis=0)
    w_b = jnp.concatenate(
        [w_cross_query.T, w_cross_kv.transpose(1, 2, 0).reshape(2 * hq, width), w_cross_out.T], axis=0
    )
    w_f = jnp.concatenate(
        [w_gate_up.transpose(1, 2, 0).reshape(2 * units, width), w_down.T], axis=0
    )
    cut_f = w_f.shape[0] * 5 // 6
    ways = lax.axis_size("dp")

    ya0, ya1 = (swap(half, "mp", 2) for half in halves_of_quarter(w_a, x, z))
    send_b = y_pieces(w_b, x, z)
    send_f0, send_f1 = halves_of_quarter(w_f[:cut_f], x, z)
    ya0, ya1, send_b, send_f0, send_f1, tokens_late = together(
        ya0, ya1, send_b, send_f0, send_f1, tokens
    )

    y_b = swap(send_b, "mp", 2)
    xa0, za1 = swap(ya0, "dp", 1), swap(ya1, "dp", 2)
    xa1, za0 = swap(ya1, "dp", 1), swap(ya0, "dp", 2)
    qkv0, mixed_a0, lse_a0, part = self_forward(table_lengths, tokens_late, gain_a, w_a, heads)
    xa0, xa1, za0, za1, part, memory_late = together(xa0, xa1, za0, za1, part, memory)
    da0, da1 = swap(xa0, "dp", 2), swap(za1, "dp", 1)
    y_f0 = swap(after(send_f0, xa0), "mp", 2)
    kv0 = memory_forward(memory_late, w_b, heads)
    send_g = w_f[cut_f:].astype(F32)
    da0, da1, kv0, send_g = together(da0, da1, kv0, send_g)
    far_a = (ya0, ya1, xa0, xa1, za0, za1, da0, da1)
    qkv1, mixed_a1, lse_a1, part, w_a1 = self_forward(
        table_lengths, tokens, gain_a, None, heads, remote=(ctl, far_a, part)
    )
    part, send_f1, y_b, y_f0 = together(part, send_f1, y_b, y_f0)

    part_other = swap(part, "mp", 1)
    y_f1 = swap(send_f1, "mp", 2)
    x_b, z_b = hand_on(y_b)
    q0, mixed_b0, lse_b0, part, first, normed_b = cross_forward(
        table_lengths, table_plots, heads, lead=(tokens, part, part_other, gain_b, w_b, kv0)
    )
    x_b, z_b, y_f1, part, send_g = together(x_b, z_b, y_f1, part, send_g)
    x_f0, z_f1 = swap(y_f0, "dp", 1), swap(y_f1, "dp", 2)
    q1, mixed_b1, lse_b1, part, w_b1, kv1 = cross_forward(
        table_lengths, table_plots, heads, follow=(normed_b, ctl, memory, part, (y_b, x_b, z_b))
    )
    send_g, x_f0, z_f1, part = together(send_g, x_f0, z_f1, part)
    far_z, far_x = hand_on_again(y_f0, y_f1, x_f0, z_f1)

    part_other = swap(part, "mp", 1)
    y_g = swap(send_g, "mp", 2)
    res, back, second, normed_c, *grad_f = feed(
        units, lead=(ctl, ways, first, part, part_other, gain_c, cotangent, w_f)
    )
    y_g, far_z, far_x, *grad_f = together(y_g, far_z, far_x, *grad_f)
    far_f = ((y_f0, y_f1, x_f0, z_f1, far_z, far_x), (y_g,))
    rs_f = halvings(grad_f)
    for rs in rs_f:
        rs.start()
    res, back = feed(units, follow=(ctl, normed_c, cotangent, far_f, res, back))
    back_other = swap(back, "mp", 1)
    back, back_mem, grad_second, branch_b, gain_grad_c, *grad_b = cross_backward(
        table_lengths, table_plots, w_b, q0, lse_b0, kv0, heads,
        lead=(ctl, ways, second, back, back_other, cotangent, gain_c, normed_b, memory, mixed_b0),
    )
    rs_f[0].got, rs_f[1].got, res, lse_b1, *grad_b = together(
        rs_f[0].got, rs_f[1].got, res, lse_b1, *grad_b
    )
    res_other = swap(res, "mp", 1)

    for rs in rs_f:
        rs.finish()
        rs.start()
    back, back_mem = cross_backward(
        table_lengths, table_plots, w_b1, q1, lse_b1, kv1, heads,
        follow=(branch_b, back, back_mem, mixed_b1),
    )
    rs_f[0].got, rs_f[1].got, back, res_other = together(
        rs_f[0].got, rs_f[1].got, back, res_other
    )

    back_other = swap(back, "mp", 1)
    rs_b = halvings(grad_b)
    rs_f = last_bits(rs_f)
    rs_f.start()
    for rs in rs_b:
        rs.start(rs_f.flat)
    back, grad_first, branch_a, gain_grad_b, *grad_a = self_backward(
        table_lengths, w_a, qkv0, lse_a0, heads,
        lead=(ctl, ways, first, back, back_other, grad_second, gain_b, tokens, gain_a, mixed_a0),
    )
    rs_b[0].got, rs_b[1].got, rs_f.got, back_mem, lse_a1, *grad_a = together(
        rs_b[0].got, rs_b[1].got, rs_f.got, back_mem, lse_a1, *grad_a
    )
    mem_other = swap(back_mem, "mp", 1)

    rs_a = halvings(grad_a)
    for rs in rs_a:
        rs.start()
    for rs in rs_b:
        rs.finish()
        rs.start()
    (back,) = self_backward(table_lengths, w_a1, qkv1, lse_a1, heads, follow=(branch_a, back, mixed_a1))
    grad_memory = back_mem + mem_other
    rs_a[0].got, rs_a[1].got, rs_b[0].got, rs_b[1].got, back, grad_memory = together(
        rs_a[0].got, rs_a[1].got, rs_b[0].got, rs_b[1].got, back, grad_memory
    )

    back_other = swap(back, "mp", 1)
    rs_b = last_bits(rs_b)
    rs_b.start()
    for rs in rs_a:
        rs.finish()
        rs.start(rs_b.flat)
    grad_tokens, gain_grad_a = tail(tokens, back, back_other, grad_first, gain_a)
    rs_a[0].got, rs_a[1].got, gain_grad_a, res, res_other, second = together(
        rs_a[0].got, rs_a[1].got, gain_grad_a, res, res_other, second
    )
    rs_a = last_bits(rs_a)
    rs_a.start()
    layer_out = (second + (res + res_other)).astype(BF16)
    rs_a.got, rs_b.got, layer_out = together(rs_a.got, rs_b.got, layer_out)
    grads = []
    for rs in (rs_f, rs_b, rs_a):
        rs.finish()
        grads.append(rs.rest())

    row_sums, col_sums = square_sums(grads, hq, units)
    row_sums, message = message_of(
        *exchange_sums(row_sums, "mp"), col_sums, (gain_grad_a, gain_grad_b, gain_grad_c), hq, units
    )
    parts = exchange_sums(message, "dp")
    *results, message = updates(grads, row_sums, parts, width, hq, units)
    own_rows = grads[0].shape[0]
    grad_gains = lax.dynamic_slice_in_dim(
        message[:, col_sums.shape[1] + 128 :].reshape(3, width), place * own_rows, own_rows, axis=1
    ).T
    return (layer_out, grad_tokens, grad_memory, grad_gains, *results)


def solution(mesh):
    split = P("dp", None)
    cols = P(None, "mp")
    cols3 = P(None, None, "mp")
    both = P("dp", "mp")
    both3 = P("dp", None, "mp")
    return jax.shard_map(
        on_device,
        mesh=mesh,
        in_specs=(
            split, split, split, split, split, P(),
            cols3, cols, cols, cols3, cols, cols3, cols,
        ),
        out_specs=(
            split, split, split, split,
            both3, both, both, both3, both, both3, both,
            both3, both, both, both3, both, both3, both,
        ),
        check_vma=False,
    )
```

```python
import functools
import math

import jax
import jax.numpy as jnp
from jax import lax
from jax.experimental import pallas as pl
from jax.experimental.pallas import tpu as pltpu
from jax.sharding import PartitionSpec as P

DH = 64
PATCH = 256
LONGEST = 512
ROWS = 256
SPAN = LONGEST // ROWS
F32 = jnp.float32
BF16 = jnp.bfloat16
NEG = -1e30
SCALE = 1.0 / math.sqrt(DH)
FREE, NEAR = "free", "near"
VMEM_BYTES = 30 * 1024 * 1024
SMALL = 1 << 15


def nn(a, b):
    return lax.dot_general(a, b, (((1,), (0,)), ((), ())), preferred_element_type=F32)


def nt(a, b):
    return lax.dot_general(a, b, (((1,), (1,)), ((), ())), preferred_element_type=F32)


def tn(a, b):
    return lax.dot_general(a, b, (((0,), (0,)), ((), ())), preferred_element_type=F32)


def normed_of(rows, gain):
    return rows * lax.rsqrt(jnp.mean(rows * rows, axis=-1, keepdims=True) + 1e-06) * gain


def norm_vjp(rows, gain, grad):
    inv = lax.rsqrt(jnp.mean(rows * rows, axis=-1, keepdims=True) + 1e-06)
    scaled = rows * inv
    hg = grad * gain
    inner = jnp.mean(hg * scaled, axis=-1, keepdims=True)
    grad_rows = inv * (hg - scaled * inner)
    grad_gain = jnp.sum(grad * scaled, axis=0, keepdims=True)
    return grad_rows, grad_gain, scaled


def place_pieces(dst, ctl, groups):
    x, z = ctl[0], ctl[1]
    base = 0
    for refs in groups:
        q = refs[0].shape[0] // 2
        if len(refs) == 1:
            dst[base : base + 2 * q, :] = refs[0][...].astype(BF16)
            base += 2 * q
        elif len(refs) == 8:
            q = 2 * q
            me, by_x = 2 * z + x, 2 * z + 1 - x
            by_z, far = 2 * (1 - z) + x, 2 * (1 - z) + 1 - x
            for k, who in enumerate((me, by_x, by_z, far)):
                for half in range(2):
                    offset = pl.multiple_of(base + (2 * who + half) * q, 16)
                    dst[pl.ds(offset, q), :] = refs[2 * k + half][...].astype(BF16)
            base += 8 * q
        elif len(refs) == 4:
            y0, y1, x0, z1 = refs
            q, r = y0.shape[0], y1.shape[0]
            for offset, ref in ((x * q, y0), ((1 - x) * q, x0), (2 * q + z * r, y1), (2 * q + (1 - z) * r, z1)):
                dst[pl.ds(pl.multiple_of(base + offset, 16), ref.shape[0]), :] = ref[...].astype(BF16)
            base += 2 * q + 2 * r
        elif len(refs) == 3:
            by_y, by_x, by_z = refs

            def put(offset, value, base=base, q=q):
                dst[pl.ds(pl.multiple_of(base + offset, 16), q), :] = value.astype(BF16)

            put(x * q, by_y[:q, :])
            put((1 - x) * q, by_x[...])
            put((2 + z) * q, by_y[q:, :])
            put((3 - z) * q, by_z[...])
            base += 4 * q
        else:
            y0, y1, by_x, by_z, far_z, far_x = refs
            q = 2 * q

            def put(who, half, value, base=base, q=q):
                dst[pl.ds(pl.multiple_of(base + who * (2 * q) + half * q, 16), q), :] = value.astype(BF16)

            me, other_x = 2 * z + x, 2 * z + 1 - x
            other_z, other = 2 * (1 - z) + x, 2 * (1 - z) + 1 - x
            put(me, 0, y0[...])
            put(me, 1, y1[...])
            put(other_x, 0, by_x[...])
            put(other_z, 1, by_z[...])
            put(other_z, 0, far_z[:q, :])
            put(other, 0, far_z[q:, :])
            put(other_x, 1, far_x[:q, :])
            put(other, 1, far_x[q:, :])
            base += 8 * q


def table_ends(lengths):
    ends = []
    total = lengths[0, 0]
    for j in range(1, lengths.shape[1]):
        ends.append(total)
        total = total + lengths[0, j]
    return ends


def query_places(base):
    return lax.broadcasted_iota(jnp.int32, (1, ROWS), 1) + base


def self_bias(lengths, base, low, width):
    places = query_places(base)
    start = jnp.zeros_like(places)
    for end in table_ends(lengths):
        start = jnp.where(places >= end, end, start)
    keys = lax.broadcasted_iota(jnp.int32, (width, ROWS), 0) + low
    return jnp.where((keys >= start) & (keys <= places), 0.0, NEG)


def window_cases(lengths, block, body):
    base = block * ROWS
    start = jnp.int32(0)
    for end in table_ends(lengths):
        start = jnp.where(base >= end, end, start)
    needed = block - start // ROWS
    for back in range(SPAN + 1):

        @pl.when(needed == back)
        def _run(back=back):
            body(pl.multiple_of((block - back) * ROWS, ROWS), (back + 1) * ROWS)


def full(shape):
    return pl.BlockSpec(shape, lambda i: (0,) * len(shape))


def by_rows(width):
    return pl.BlockSpec((ROWS, width), lambda i: (i, 0))


def by_cols(height):
    return pl.BlockSpec((height, ROWS), lambda i: (0, i))


SMEM = pl.BlockSpec(memory_space=pltpu.SMEM)


def run(kernel, grid, ins, outs, scratch, flops, name, transcendentals=0):
    moved = sum(entry[0].size * entry[0].dtype.itemsize for entry in ins) + sum(
        math.prod(entry[0].shape) * jnp.dtype(entry[0].dtype).itemsize for entry in outs
    )
    arrays = [
        entry[0]
        if entry[-1] is FREE or entry[1] is SMEM or entry[0].size < SMALL
        else pltpu.with_memory_space_constraint(entry[0], pltpu.VMEM if entry[-1] is NEAR else pltpu.HBM)
        for entry in ins
    ]
    shapes = [
        entry[0]
        if entry[-1] is FREE or math.prod(entry[0].shape) < SMALL
        else (pltpu.VMEM if entry[-1] is NEAR else pltpu.HBM)(entry[0].shape, entry[0].dtype)
        for entry in outs
    ]
    return pl.pallas_call(
        kernel,
        grid=(grid,),
        in_specs=[entry[1] for entry in ins],
        out_specs=[entry[1] for entry in outs],
        out_shape=shapes,
        scratch_shapes=scratch,
        compiler_params=pltpu.CompilerParams(
            vmem_limit_bytes=VMEM_BYTES, dimension_semantics=("arbitrary",)
        ),
        cost_estimate=pl.CostEstimate(
            flops=flops // 64, bytes_accessed=moved // 64, transcendentals=transcendentals // 64
        ),
        name=name,
    )(*arrays)


def sds(shape, dtype):
    return jax.ShapeDtypeStruct(shape, dtype)


def self_forward_kernel(remote, heads, *refs):
    if remote:
        (lengths, ctl, tokens, gain, base_out) = refs[:5]
        pieces = refs[5:-6]
        (qkv_t, mixed_t, lse, out, w_out, k_rows) = refs[-6:]
        w = w_out
    else:
        (lengths, tokens, gain, w) = refs[:4]
        (qkv_t, mixed_t, lse, out, k_rows) = refs[4:]
    block = pl.program_id(0)
    hq = heads * DH
    if remote:

        @pl.when(block == 0)
        def _place():
            place_pieces(w, ctl, [pieces])

    base = pl.multiple_of(block * ROWS, ROWS)
    here = pl.ds(base, ROWS)
    normed = normed_of(tokens[...].astype(F32), gain[...]).astype(BF16)
    qkv = nt(w[0 : 3 * hq, :], normed).astype(BF16)
    q_all = (qkv[:hq].astype(F32) * SCALE).astype(BF16)
    qkv_t[0:hq, here] = q_all
    qkv_t[hq : 3 * hq, here] = qkv[hq:]
    for h in range(heads):
        k_rows[h, here, :] = qkv[hq + h * DH : hq + (h + 1) * DH].T

    def attend(low, width):
        window = pl.ds(low, width)
        bias = self_bias(lengths, base, low, width)
        for h in range(heads):
            own = slice(h * DH, (h + 1) * DH)
            s = nn(k_rows[h, window, :], q_all[own]) + bias
            top = jnp.max(s, axis=0, keepdims=True)
            e = jnp.exp(s - top)
            total = jnp.sum(e, axis=0, keepdims=True)
            o = nn(qkv_t[2 * hq + h * DH : 2 * hq + (h + 1) * DH, window], e.astype(BF16))
            mixed_t[own, :] = (o * (1.0 / total)).astype(BF16)
            lse[h : h + 1, :] = top + jnp.log(total)

    window_cases(lengths, block, attend)
    part = tn(mixed_t[...], w[3 * hq : 4 * hq, :])
    out[...] = part + base_out[...] if remote else part


def self_forward(lengths, tokens, gain, w, heads, remote=None):
    slots, width = tokens.shape
    hq = heads * DH
    outs = [
        (sds((3 * hq, slots), BF16), full((3 * hq, slots))),
        (sds((hq, slots), BF16), by_cols(hq)),
        (sds((8, slots), F32), by_cols(8)),
        (sds((slots, width), F32), by_rows(width), NEAR),
    ]
    scratch = [pltpu.VMEM((heads, slots, DH), BF16)]
    if remote is None:
        ins = [(lengths, SMEM), (tokens, by_rows(width)), (gain, full(gain.shape)), (w, full(w.shape))]
    else:
        ctl, pieces, base_out = remote
        ins = [
            (lengths, SMEM),
            (ctl, SMEM),
            (tokens, by_rows(width)),
            (gain, full(gain.shape)),
            (base_out, by_rows(width), NEAR),
        ]
        ins += [(piece, full(piece.shape)) for piece in pieces]
        outs.append((sds((4 * hq, width), BF16), full((4 * hq, width))))
    flops = 2 * slots * width * 4 * hq + heads * 4 * slots * slots * DH
    return run(
        functools.partial(self_forward_kernel, remote is not None, heads),
        slots // ROWS, ins, outs, scratch, flops, "self_forward", heads * slots * slots,
    )


def memory_kernel(hq, memory, w, kv_t):
    kv_t[...] = nt(w[hq : 3 * hq, :], memory[...]).astype(BF16)


def memory_forward(memory, w, heads):
    count, width = memory.shape
    hq = heads * DH
    (kv_t,) = run(
        functools.partial(memory_kernel, hq), count // ROWS,
        [(memory, by_rows(width)), (w, full(w.shape))],
        [(sds((2 * hq, count), BF16), by_cols(2 * hq))], [], 2 * count * width * 2 * hq, "memory_forward",
    )
    return kv_t


def rows_of_heads(rows, columns, heads):
    for h in range(heads):
        rows[h] = columns[h * DH : (h + 1) * DH, :].T


def tables_of_block(lengths, base, body):
    ends = table_ends(lengths)
    places = query_places(base)
    segment = jnp.zeros_like(places)
    first_table = jnp.int32(0)
    last_table = jnp.int32(0)
    for end in ends:
        segment = segment + (places >= end).astype(jnp.int32)
        first_table = first_table + (base >= end).astype(jnp.int32)
        last_table = last_table + (base + ROWS - 1 >= end).astype(jnp.int32)

    def step(table, carry):
        body(table, segment == table)
        return carry

    lax.fori_loop(first_table, last_table + 1, step, 0)


def cross_forward_kernel(leading, heads, *refs):
    hq = heads * DH
    k_rows = refs[-1]
    if leading:
        (lengths, plots, tokens, part, other, gain, w, kv_t) = refs[:8]
        (q_t, mixed_t, lse, out, first, normed_out) = refs[8:-1]
    else:
        (lengths, plots, ctl, normed_in, memory, base_out) = refs[:6]
        (q_t, mixed_t, lse, out, w, kv_t) = refs[-7:-1]

    @pl.when(pl.program_id(0) == 0)
    def _start():
        if not leading:
            place_pieces(w, ctl, [refs[6:-7]])
            for m in range(memory.shape[0] // ROWS):
                here = slice(m * ROWS, (m + 1) * ROWS)
                kv_t[:, here] = nt(w[hq : 3 * hq, :], memory[here, :]).astype(BF16)
        rows_of_heads(k_rows, kv_t, heads)

    if leading:
        rows = tokens[...].astype(F32) + (part[...] + other[...])
        first[...] = rows
        normed = normed_of(rows, gain[...]).astype(BF16)
        normed_out[...] = normed
    else:
        normed = normed_in[...]
    base = pl.multiple_of(pl.program_id(0) * ROWS, ROWS)
    query = nt(w[0:hq, :], normed).astype(BF16)
    q_all = (query.astype(F32) * SCALE).astype(BF16)
    q_t[...] = q_all

    def table(j, member):
        plot = pl.ds(pl.multiple_of(plots[0, j] * PATCH, PATCH), PATCH)
        for h in range(heads):
            own = slice(h * DH, (h + 1) * DH)
            s = nn(k_rows[h, plot, :], q_t[own, :])
            top = jnp.max(s, axis=0, keepdims=True)
            e = jnp.exp(s - top)
            total = jnp.sum(e, axis=0, keepdims=True)
            o = nn(kv_t[hq + h * DH : hq + (h + 1) * DH, plot], e.astype(BF16))
            o = o * (1.0 / total)
            mixed_t[own, :] = jnp.where(member, o, mixed_t[own, :].astype(F32)).astype(BF16)
            lse[h : h + 1, :] = jnp.where(member, top + jnp.log(total), lse[h : h + 1, :])

    tables_of_block(lengths, base, table)
    part_out = tn(mixed_t[...], w[3 * hq : 4 * hq, :])
    out[...] = part_out if leading else part_out + base_out[...]


def cross_forward(lengths, plots, heads, lead=None, follow=None):
    hq = heads * DH
    slots, width = (lead or follow)[0].shape
    outs = [
        (sds((hq, slots), BF16), by_cols(hq)),
        (sds((hq, slots), BF16), by_cols(hq)),
        (sds((8, slots), F32), by_cols(8)),
        (sds((slots, width), F32), by_rows(width), NEAR),
    ]
    if lead is not None:
        tokens, part, other, gain, w, kv_t = lead
        count = kv_t.shape[1]
        ins = [
            (lengths, SMEM),
            (plots, SMEM),
            (tokens, by_rows(width)),
            (part, by_rows(width), NEAR),
            (other, by_rows(width), NEAR),
            (gain, full(gain.shape)),
            (w, full(w.shape)),
            (kv_t, full(kv_t.shape)),
        ]
        outs += [
            (sds((slots, width), F32), by_rows(width)),
            (sds((slots, width), BF16), by_rows(width)),
        ]
    else:
        normed, ctl, memory, base_out, pieces = follow
        count = memory.shape[0]
        ins = [
            (lengths, SMEM),
            (plots, SMEM),
            (ctl, SMEM),
            (normed, by_rows(width)),
            (memory, full(memory.shape)),
            (base_out, by_rows(width), NEAR),
        ]
        ins += [(piece, full(piece.shape)) for piece in pieces]
        outs += [
            (sds((4 * hq, width), BF16), full((4 * hq, width))),
            (sds((2 * hq, count), BF16), full((2 * hq, count))),
        ]
    flops = 2 * slots * width * 2 * hq + heads * 8 * slots * PATCH * DH
    return run(
        functools.partial(cross_forward_kernel, lead is not None, heads),
        slots // ROWS, ins, outs, [pltpu.VMEM((heads, count, DH), BF16)], flops, "cross_forward",
        heads * slots * PATCH * 2,
    )


def column_parts(width, cuts):
    edges = [0] + [width * cut // 12 for cut in cuts] + [width]
    bits = [1] * ((len(cuts) + 1) // 2) + [2] * ((len(cuts) + 1) // 2)
    return list(zip(edges[:-1], edges[1:], bits))


HALVES, QUARTERS = (6,), (2, 6, 8)


def gradient_outs(count, rows, width, cuts=HALVES):
    if split_bits(rows, count):
        return [
            (sds((rows // 2, high - low), F32), full((rows // 2, high - low)))
            for low, high, _ in column_parts(width, cuts)
            for _ in range(2)
        ]
    return [(sds((rows, width), F32), full((rows, width)))]


def finish_gradient(count, ctl, source, outs, cuts=HALVES):
    @pl.when(pl.program_id(0) == pl.num_programs(0) - 1)
    def _write():
        if len(outs) == 1:
            outs[0][...] = source[...]
        else:
            for k, (low, high, bit) in enumerate(column_parts(source.shape[1], cuts)):
                write_split(source, low, high, count, bit, ctl[bit - 1], outs[2 * k], outs[2 * k + 1])


def halvings(outs, cuts=HALVES):
    order = {1: (1, 2, 4), 2: (2, 1, 4)}
    if len(outs) == 1:
        parts = column_parts(outs[0].shape[1], cuts)
        return [Halving(outs[0][:, low:high], order[bit]) for low, high, bit in parts]
    bits = [bit for _, _, bit in column_parts(12, cuts)]
    return [Halving(None, order[bit], outs[2 * k : 2 * k + 2]) for k, bit in enumerate(bits)]


def feed_kernel(leading, units, count, *refs):
    if leading:
        (ctl, first, part, other, gain, cot, w) = refs[:7]
        (result, grad_in, second, normed_out) = refs[7:11]
        dw_outs = refs[11:-4]
        dw, normed_all, cot_all, inner_all = refs[-4:]
        rows = first[...] + (part[...] + other[...])
        second[...] = rows
        normed = normed_of(rows, gain[...]).astype(BF16)
        normed_out[...] = normed
    else:
        (ctl, normed_in, cot, base_result, base_grad) = refs[:5]
        pieces = refs[5:-3]
        (result, grad_in, w) = refs[-3:]
        normed = normed_in[...]

        @pl.when(pl.program_id(0) == 0)
        def _place():
            place_pieces(w, ctl, [pieces[:6], pieces[6:]])

    cot_rows = cot[...]
    gate_up = nt(normed, w[0 : 2 * units, :])
    gate, up = gate_up[:, :units], gate_up[:, units:]
    c0 = math.sqrt(2.0 / math.pi)
    square = gate * gate
    th = jnp.tanh(c0 * gate * (1.0 + 0.044715 * square))
    half = 0.5 * (1.0 + th)
    gelu = gate * half
    slope = half + (0.5 * c0) * gate * (1.0 - th * th) * (1.0 + (3 * 0.044715) * square)
    hidden = (gelu * up).astype(BF16)
    res = nn(hidden, w[2 * units : 3 * units, :])
    grad_hidden = nt(cot_rows, w[2 * units : 3 * units, :])
    grad_gate = (grad_hidden * up * slope).astype(BF16)
    grad_up = (grad_hidden * gelu).astype(BF16)
    back = nn(grad_gate, w[0:units, :]) + nn(grad_up, w[units : 2 * units, :])
    if leading:
        result[...] = res
        grad_in[...] = back
        here = pl.ds(pl.multiple_of(pl.program_id(0) * ROWS, ROWS), ROWS)
        normed_all[here, :] = normed
        cot_all[here, :] = cot_rows
        inner_all[here, 0:units] = grad_gate
        inner_all[here, units : 2 * units] = grad_up
        inner_all[here, 2 * units : 3 * units] = hidden

        @pl.when(pl.program_id(0) == pl.num_programs(0) - 1)
        def _weights():
            for m in range(dw.shape[0] // ROWS):
                rows = slice(m * ROWS, (m + 1) * ROWS)
                dw[rows, 0 : 2 * units] = tn(normed_all[:, rows], inner_all[:, 0 : 2 * units])
                dw[rows, 2 * units : 3 * units] = tn(cot_all[:, rows], inner_all[:, 2 * units : 3 * units])

        finish_gradient(count, ctl, dw, dw_outs, QUARTERS)
    else:
        result[...] = res + base_result[...]
        grad_in[...] = back + base_grad[...]


def feed(units, lead=None, follow=None):
    if lead is not None:
        ctl, count, first, part, other, gain, cot, w = lead
        slots, width = first.shape
        ins = [
            (ctl, SMEM),
            (first, by_rows(width)),
            (part, by_rows(width), NEAR),
            (other, by_rows(width), NEAR),
            (gain, full(gain.shape)),
            (cot, by_rows(width)),
            (w, full(w.shape)),
        ]
    else:
        ctl, normed, cot, pieces, base_result, base_grad = follow
        slots, width = normed.shape
        ins = [(ctl, SMEM), (normed, by_rows(width), FREE), (cot, by_rows(width))]
        ins += [(base_result, by_rows(width), FREE), (base_grad, by_rows(width), NEAR)]
        ins += [(piece, full(piece.shape)) for group in pieces for piece in group]
    outs = [
        (sds((slots, width), F32), by_rows(width), FREE),
        (sds((slots, width), F32), by_rows(width), NEAR),
    ]
    scratch = []
    if lead is not None:
        outs += [
            (sds((slots, width), F32), by_rows(width)),
            (sds((slots, width), BF16), by_rows(width), FREE),
        ]
        outs += gradient_outs(count, width, 3 * units, QUARTERS)
        scratch = [
            pltpu.VMEM((width, 3 * units), F32),
            pltpu.VMEM((slots, width), BF16),
            pltpu.VMEM((slots, width), BF16),
            pltpu.VMEM((slots, 3 * units), BF16),
        ]
    else:
        count = 0
        scratch = [pltpu.VMEM((3 * units, width), BF16)]
    flops = 2 * slots * width * units * (9 if lead is not None else 6)
    return run(
        functools.partial(feed_kernel, lead is not None, units, count),
        slots // ROWS, ins, outs, scratch, flops, "feed", slots * units,
    )


def cross_backward_kernel(leading, heads, count, *refs):
    hq = heads * DH
    if leading:
        (ctl, lengths, plots, second, part, other, cot, gain, normed, memory) = refs[:10]
        (w, q_t, mixed_t, lse, kv_t) = refs[10:15]
        (dq_out, dkv_out, grad_second, branch_out, grad_gain) = refs[15:20]
        dw_outs = refs[20:-7]
        (dkv, dq, dm, k_rows, v_rows, dw_t, dw) = refs[-7:]
    else:
        (lengths, plots, branch_in, w, q_t, mixed_t, lse, kv_t, near_dq, near_dkv, near_w) = refs[:11]
        (grad_in, grad_mem, dkv, dq, dm, k_rows, v_rows) = refs[11:]
    block = pl.program_id(0)
    last = pl.num_programs(0) - 1
    base = pl.multiple_of(block * ROWS, ROWS)

    @pl.when(block == 0)
    def _zero():
        dkv[...] = jnp.zeros_like(dkv)
        rows_of_heads(k_rows, kv_t[0:hq, :], heads)
        rows_of_heads(v_rows, kv_t[hq : 2 * hq, :], heads)
        if leading:
            dw_t[...] = jnp.zeros_like(dw_t)
            grad_gain[...] = jnp.zeros_like(grad_gain)

    if leading:
        grad_rows, gain_rows, _ = norm_vjp(second[...], gain[...], part[...] + other[...])
        total = cot[...].astype(F32) + grad_rows
        grad_second[...] = total
        branch = total.astype(BF16)
        branch_out[...] = branch
        grad_gain[0:1, :] += gain_rows
    else:
        branch = branch_in[...]
    dm[...] = nt(w[3 * hq : 4 * hq, :], branch).astype(BF16)
    dq[...] = jnp.zeros_like(dq)

    def table(j, member):
        plot = pl.ds(pl.multiple_of(plots[0, j] * PATCH, PATCH), PATCH)
        for h in range(heads):
            own = slice(h * DH, (h + 1) * DH)
            val = slice(hq + h * DH, hq + (h + 1) * DH)
            query = q_t[own, :]
            dmix = jnp.where(member, dm[own, :].astype(F32), 0.0).astype(BF16)
            level = jnp.where(member, lse[h : h + 1, :], -NEG)
            p = jnp.exp(nn(k_rows[h, plot, :], query) - level)
            dp = nn(v_rows[h, plot, :], dmix)
            inner = jnp.sum(dmix.astype(F32) * mixed_t[own, :].astype(F32), axis=0, keepdims=True)
            ds = (p * (dp - inner)).astype(BF16)
            dkv[own, plot] += nt(query, ds)
            dkv[val, plot] += nt(dmix, p.astype(BF16))
            dq[own, :] += nn(kv_t[own, plot], ds)

    tables_of_block(lengths, base, table)
    grad_query = (dq[...] * SCALE).astype(BF16)
    if leading:
        dq_out[...] = grad_query
        dw_t[0:hq, :] += nn(grad_query, normed[...])
        dw_t[3 * hq : 4 * hq, :] += nn(mixed_t[...], branch)
    else:
        grad_in[...] = tn(grad_query, w[0:hq, :]) + tn(near_dq[...], near_w[0:hq, :])

    @pl.when(block == last)
    def _finish():
        for m in range(dkv.shape[1] // ROWS):
            here = slice(m * ROWS, (m + 1) * ROWS)
            rows = dkv[:, here].astype(BF16)
            if not leading:
                back_mem = tn(rows, w[hq : 3 * hq, :])
                grad_mem[here, :] = back_mem + tn(near_dkv[:, here], near_w[hq : 3 * hq, :])
            else:
                dkv_out[:, here] = rows
                dw_t[hq : 3 * hq, :] += nn(rows, memory[here, :])
        if leading:
            dw[...] = dw_t[...].T

    if leading:
        finish_gradient(count, ctl, dw, dw_outs)


def cross_backward(lengths, plots, w, q_t, lse, kv_t, heads, lead=None, follow=None):
    hq = heads * DH
    slots, width = q_t.shape[1], w.shape[1]
    count = kv_t.shape[1]
    scratch = [
        pltpu.VMEM((2 * hq, count), F32),
        pltpu.VMEM((hq, ROWS), F32),
        pltpu.VMEM((hq, ROWS), BF16),
        pltpu.VMEM((heads, count, DH), BF16),
        pltpu.VMEM((heads, count, DH), BF16),
    ]
    heads_part = [
        (lse, by_cols(8)),
        (kv_t, full(kv_t.shape)),
    ]
    if lead is not None:
        ctl, split, second, part, other, cot, gain, normed, memory, mixed_t = lead
        ins = [
            (ctl, SMEM),
            (lengths, SMEM),
            (plots, SMEM),
            (second, by_rows(width)),
            (part, by_rows(width), NEAR),
            (other, by_rows(width), NEAR),
            (cot, by_rows(width)),
            (gain, full(gain.shape)),
            (normed, by_rows(width)),
            (memory, full(memory.shape)),
            (w, full(w.shape)),
            (q_t, by_cols(hq)),
            (mixed_t, by_cols(hq)),
        ] + heads_part
        outs = [
            (sds((hq, slots), BF16), by_cols(hq)),
            (sds((2 * hq, count), BF16), full((2 * hq, count))),
            (sds((slots, width), F32), by_rows(width), FREE),
            (sds((slots, width), BF16), by_rows(width)),
            (sds((8, width), F32), full((8, width))),
        ]
        outs += gradient_outs(split, width, 4 * hq)
        scratch += [pltpu.VMEM((4 * hq, width), F32), pltpu.VMEM((width, 4 * hq), F32)]
    else:
        split = 0
        branch, mixed_t, near_dq, near_dkv, near_w = follow
        outs = [
            (sds((slots, width), F32), by_rows(width), NEAR),
            (sds((count, width), F32), full((count, width))),
        ]
        ins = [
            (lengths, SMEM),
            (plots, SMEM),
            (branch, by_rows(width)),
            (w, full(w.shape)),
            (q_t, by_cols(hq)),
            (mixed_t, by_cols(hq)),
        ] + heads_part
        ins += [(near_dq, by_cols(hq)), (near_dkv, full(near_dkv.shape)), (near_w, full(near_w.shape))]
    flops = 2 * slots * width * hq * (8 if lead is not None else 4) + heads * 20 * slots * PATCH * DH
    return run(
        functools.partial(cross_backward_kernel, lead is not None, heads, split),
        slots // ROWS, ins, outs, scratch, flops, "cross_backward", heads * slots * PATCH * 2,
    )


def self_backward_kernel(leading, heads, count, *refs):
    hq = heads * DH
    if leading:
        (ctl, lengths, first, part, other, carried, gain, tokens, gain_in, w, qkv_t, mixed_t, lse) = refs[:13]
        (dqkv_out, grad_first, branch_out, grad_gain) = refs[13:17]
        dw_outs = refs[17:-6]
        (dkv, k_rows, v_rows, dqkv, dw_t, dw) = refs[-6:]
    else:
        (lengths, branch_in, w, qkv_t, mixed_t, lse, near_rows, near_w) = refs[:8]
        (grad_in, dkv, k_rows, v_rows, dqkv) = refs[8:]
    step = pl.program_id(0)
    last = pl.num_programs(0) - 1
    block = last - step
    base = pl.multiple_of(block * ROWS, ROWS)
    here = pl.ds(base, ROWS)

    @pl.when(step == 0)
    def _start():
        dkv[...] = jnp.zeros_like(dkv)
        for h in range(heads):
            k_rows[h] = qkv_t[hq + h * DH : hq + (h + 1) * DH, :].T
            v_rows[h] = qkv_t[2 * hq + h * DH : 2 * hq + (h + 1) * DH, :].T
        if leading:
            dw_t[...] = jnp.zeros_like(dw_t)
            grad_gain[...] = jnp.zeros_like(grad_gain)

    if leading:
        grad_rows, gain_rows, _ = norm_vjp(first[...], gain[...], part[...] + other[...])
        total = carried[...] + grad_rows
        grad_first[...] = total
        branch = total.astype(BF16)
        branch_out[...] = branch
        grad_gain[0:1, :] += gain_rows
    else:
        branch = branch_in[...]
    dm_all = nt(w[3 * hq : 4 * hq, :], branch).astype(BF16)

    def attend(low, width):
        window = pl.ds(low, width)
        bias = self_bias(lengths, base, low, width)
        for h in range(heads):
            own = slice(h * DH, (h + 1) * DH)
            key = slice(hq + h * DH, hq + (h + 1) * DH)
            val = slice(hq + h * DH, hq + (h + 1) * DH)
            query = qkv_t[own, here]
            dmix = dm_all[own]
            p = jnp.exp(nn(k_rows[h, window, :], query) + bias - lse[h : h + 1, :])
            dp = nn(v_rows[h, window, :], dmix)
            inner = jnp.sum(dmix.astype(F32) * mixed_t[own, :].astype(F32), axis=0, keepdims=True)
            ds = (p * (dp - inner)).astype(BF16)
            dkv[own, window] += nt(query, ds)
            dkv[val, window] += nt(dmix, p.astype(BF16))
            dqkv[own, :] = (nn(qkv_t[key, window], ds) * SCALE).astype(BF16)

    window_cases(lengths, block, attend)
    dqkv[hq : 3 * hq, :] = dkv[:, here].astype(BF16)
    rows = dqkv[...]
    if not leading:
        grad_in[...] = tn(rows, w[0 : 3 * hq, :]) + tn(near_rows[...], near_w[0 : 3 * hq, :])
    else:
        dqkv_out[...] = rows
        normed = normed_of(tokens[...].astype(F32), gain_in[...]).astype(BF16)
        dw_t[0 : 3 * hq, :] += nn(rows, normed)
        dw_t[3 * hq : 4 * hq, :] += nn(mixed_t[...], branch)

        @pl.when(step == last)
        def _finish():
            dw[...] = dw_t[...].T

        finish_gradient(count, ctl, dw, dw_outs)


def self_backward(lengths, w, qkv_t, lse, heads, lead=None, follow=None):
    hq = heads * DH
    slots, width = qkv_t.shape[1], w.shape[1]
    last = slots // ROWS - 1
    rows = pl.BlockSpec((ROWS, width), lambda i: (last - i, 0))

    def cols(height):
        return pl.BlockSpec((height, ROWS), lambda i: (0, last - i))

    scratch = [
        pltpu.VMEM((2 * hq, slots), F32),
        pltpu.VMEM((heads, slots, DH), BF16),
        pltpu.VMEM((heads, slots, DH), BF16),
        pltpu.VMEM((3 * hq, ROWS), BF16),
    ]
    if lead is not None:
        ctl, count, first, part, other, carried, gain, tokens, gain_in, mixed_t = lead
        ins = [
            (ctl, SMEM),
            (lengths, SMEM),
            (first, rows),
            (part, rows, NEAR),
            (other, rows, NEAR),
            (carried, rows, FREE),
            (gain, full(gain.shape)),
            (tokens, rows),
            (gain_in, full(gain_in.shape)),
            (w, full(w.shape)),
            (qkv_t, full(qkv_t.shape)),
            (mixed_t, cols(hq)),
            (lse, cols(8)),
        ]
        outs = [
            (sds((3 * hq, slots), BF16), cols(3 * hq)),
            (sds((slots, width), F32), rows),
            (sds((slots, width), BF16), rows),
            (sds((8, width), F32), full((8, width))),
        ]
        outs += gradient_outs(count, width, 4 * hq)
        scratch += [pltpu.VMEM((4 * hq, width), F32), pltpu.VMEM((width, 4 * hq), F32)]
    else:
        count = 0
        branch, mixed_t, near_rows, near_w = follow
        outs = [(sds((slots, width), F32), rows, NEAR)]
        ins = [
            (lengths, SMEM),
            (branch, rows),
            (w, full(w.shape)),
            (qkv_t, full(qkv_t.shape)),
            (mixed_t, cols(hq)),
            (lse, cols(8)),
            (near_rows, cols(3 * hq)),
            (near_w, full(near_w.shape)),
        ]
    flops = 2 * slots * width * hq * (8 if lead is not None else 4) + heads * 10 * slots * slots * DH
    return run(
        functools.partial(self_backward_kernel, lead is not None, heads, count),
        slots // ROWS, ins, outs, scratch, flops, "self_backward", heads * slots * slots,
    )


def tail_kernel(tokens, part, other, carried, gain, grad_tokens, grad_gain):
    @pl.when(pl.program_id(0) == 0)
    def _zero():
        grad_gain[...] = jnp.zeros_like(grad_gain)

    grad_rows, gain_rows, _ = norm_vjp(tokens[...].astype(F32), gain[...], part[...] + other[...])
    grad_tokens[...] = carried[...] + grad_rows
    grad_gain[0:1, :] += gain_rows


def tail(tokens, part, other, carried, gain):
    slots, width = tokens.shape
    ins = [
        (tokens, by_rows(width)),
        (part, by_rows(width), NEAR),
        (other, by_rows(width), NEAR),
        (carried, by_rows(width)),
        (gain, full(gain.shape)),
    ]
    outs = [
        (sds((slots, width), F32), by_rows(width)),
        (sds((8, width), F32), full((8, width))),
    ]
    return run(tail_kernel, slots // ROWS, ins, outs, [], 20 * slots * width, "last_norm")


def swap(value, axis, bit):
    count = lax.axis_size(axis)
    return lax.ppermute(value, axis, [(i, i ^ bit) for i in range(count)])


def y_pieces(w, x, z):
    quarter = w.shape[0] // 4
    pieces = w.reshape(4, quarter, w.shape[1])
    mine = jnp.concatenate(
        [jnp.where(x == 0, pieces[0], pieces[1]), jnp.where(z == 0, pieces[2], pieces[3])], axis=0
    )
    return mine.astype(F32)


def hand_on(by_y):
    quarter = by_y.shape[0] // 2
    return swap(by_y[:quarter], "dp", 1), swap(by_y[quarter:], "dp", 2)


def hand_on_again(y0, y1, by_x, by_z):
    far_z = swap(jnp.concatenate([y0, by_x], axis=0), "dp", 2)
    far_x = swap(jnp.concatenate([y1, by_z], axis=0), "dp", 1)
    return far_z, far_x


def halves_of_quarter(w, x, z):
    eighth = w.shape[0] // 8
    start = (2 * z + x) * 2 * eighth
    halves = [lax.dynamic_slice_in_dim(w, start + k * eighth, eighth, axis=0) for k in range(2)]
    return [half.astype(F32) for half in halves]


def together(*values):
    return lax.optimization_barrier(values)


def split_bits(grad_rows, count):
    return count >= 4 and (grad_rows // count) % 8 == 0


def write_split(source, low, high, count, bit, mine, sent, kept):
    own = source.shape[0] // count
    for r in range(count // 2):
        base = (r // bit) * 2 * bit + r % bit
        rows = slice(r * own, (r + 1) * own)
        kept[rows, :] = source[pl.ds(pl.multiple_of((base + mine * bit) * own, 8), own), low:high]
        sent[rows, :] = source[pl.ds(pl.multiple_of((base + (1 - mine) * bit) * own, 8), own), low:high]


def second_stage_kernel(own, widths, ctl, *refs):
    for side, mine in ((0, ctl[1]), (1, ctl[0])):
        pairs = refs[4 * side : 4 * side + 4]
        sent, kept = refs[8 + 2 * side : 10 + 2 * side]
        for r in range(sent.shape[0] // own):
            rows = slice(r * own, (r + 1) * own)
            for dst, bit in ((sent, 1 - mine), (kept, mine)):
                here = pl.ds(pl.multiple_of((2 * r + bit) * own, 8), own)
                dst[rows, : widths[0]] = pairs[0][here, :] + pairs[1][here, :]
                dst[rows, widths[0] :] = pairs[2][here, :] + pairs[3][here, :]


def second_stage(group, ctl):
    if group[0].kept.shape[-2] % 8 or group[0].count < 8:
        return [last_bits(group[0:2]), last_bits(group[2:4])]
    ins, widths = [(ctl, SMEM)], []
    for rs in group:
        flat = rs.kept.reshape(rs.got.shape)
        ins += [whole_block(flat), whole_block(rs.got)]
        widths.append(flat.shape[1])
    rows, total = ins[1][0].shape[0] // 2, widths[0] + widths[1]
    outs = [(sds((rows, total), F32), full((rows, total))) for _ in range(4)]
    own = group[0].kept.shape[-2]
    arrays = run(
        functools.partial(second_stage_kernel, own, widths[:2]), 1, ins, outs, [], rows * total * 4, "second_stage"
    )
    halves = []
    for side, order in enumerate(((2, 4), (1, 4))):
        rs = Halving(None, order, arrays[2 * side : 2 * side + 2])
        rs.left.remove(3 - order[0])
        halves.append(rs)
    return halves


def last_bits(group, finished=0):
    for rs in group[finished:]:
        rs.finish()
    both = Halving.__new__(Halving)
    both.__dict__.update(group[0].__dict__)
    both.grad = jnp.concatenate([rs.grad for rs in group], axis=-1)
    return both


class Halving:
    def __init__(self, grad, order, halves=None):
        self.halves = halves
        self.count = lax.axis_size("dp")
        self.place = lax.axis_index("dp")
        self.order = list(order)
        bit = 8
        while bit < self.count:
            self.order.append(bit)
            bit *= 2
        self.left = [b for b in (1 << k for k in range(self.count.bit_length() - 1))][::-1]
        if halves is None:
            self.grad = grad.reshape((2,) * len(self.left) + (grad.shape[0] // self.count, grad.shape[1]))

    def send(self):
        bit = self.order.pop(0)
        axis = self.left.index(bit)
        self.left.pop(axis)
        if self.halves is not None:
            sent, kept = self.halves
            self.halves = None
            shape = (2,) * len(self.left) + (kept.shape[0] >> len(self.left), kept.shape[1])
            self.kept = kept.reshape(shape)
            return sent.reshape(shape), bit
        mine = (self.place // bit) % 2
        sent = lax.dynamic_index_in_dim(self.grad, 1 - mine, axis=axis, keepdims=False)
        self.kept = lax.dynamic_index_in_dim(self.grad, mine, axis=axis, keepdims=False)
        return sent, bit

    def start(self):
        self.prepare()
        self.go()

    def prepare(self):
        sent, self.bit = self.send()
        self.flat = sent.reshape(-1, sent.shape[-1])

    def go(self):
        self.got = swap(self.flat, "dp", self.bit)

    def finish(self):
        self.grad = self.kept + self.got.reshape(self.kept.shape)

    def rest(self):
        while self.order:
            self.start()
            self.finish()
        return self.grad.reshape(-1, self.grad.shape[-1])


def exchange_sums(value, axis):
    bit = 1
    while bit * 4 < lax.axis_size(axis):
        value = value + swap(value, axis, bit)
        bit *= 2
    return [value] + [swap(value, axis, k * bit) for k in range(1, lax.axis_size(axis) // bit)]


def lane_pick(width, edges, values):
    lanes = lax.broadcasted_iota(jnp.int32, (1, width), 1)
    picked = values[-1]
    for edge, value in zip(edges[-2::-1], values[-2::-1]):
        picked = jnp.where(lanes < edge, value, picked)
    return picked


def groups_of(hq, units):
    return (
        ((2 * units, 3 * units), (0, 1)),
        ((hq, 3 * hq, 4 * hq), (2, 3, 4)),
        ((3 * hq, 4 * hq), (5, 6)),
    )


def joined(refs):
    grad_f0, grad_f1, grad_b, grad_a = (ref[...] for ref in refs)
    return jnp.concatenate([grad_f0, grad_f1], axis=1), grad_b, grad_a


def square_sums_kernel(groups, *refs):
    rows, cols = refs[4:]
    places = lax.broadcasted_iota(jnp.int32, (1, rows.shape[1]), 1)
    sums = jnp.zeros(rows.shape, F32)
    at = 0
    for grad, (edges, names) in zip(joined(refs[:4]), groups):
        square = grad * grad
        cols[:, at : at + grad.shape[1]] = jnp.sum(square, axis=0, keepdims=True)
        at += grad.shape[1]
        lanes = lax.broadcasted_iota(jnp.int32, (1, grad.shape[1]), 1)
        low = 0
        for edge, name in zip(edges, names):
            inside = (lanes >= low) & (lanes < edge)
            total = jnp.sum(jnp.where(inside, square, 0.0), axis=1, keepdims=True)
            sums = jnp.where(places == name, total, sums)
            low = edge
    rows[...] = sums


def message_kernel(groups, ways, *refs):
    cols, gain_a, gain_b, gain_c, rows_out, message = refs[-6:]
    total = refs[0][...]
    for part in refs[1:-6]:
        total = total + part[...]
    rows_out[...] = total
    places = lax.broadcasted_iota(jnp.int32, (1, total.shape[1]), 1)
    scale = jnp.zeros((1, total.shape[1]), F32)
    for edges, names in groups:
        low = 0
        for edge, name in zip(edges, names):
            scale = jnp.where(places == name, 1.0 / ((edge - low) * ways), scale)
            low = edge
    at = cols.shape[1]
    message[:, :at] = cols[...]
    message[:, at : at + 128] = jnp.sum(total * scale + 1e-30, axis=0, keepdims=True)
    at += 128
    for gain in (gain_a, gain_b, gain_c):
        message[:, at : at + gain.shape[1]] = gain[0:1, :]
        at += gain.shape[1]


def update_kernel(groups, ways, model_width, hq, units, *refs):
    rows = refs[4]
    (g_qkv, g_so, g_cq, g_ckv, g_co, g_gu, g_d) = refs[-15:-8]
    (s_qkv, s_so, s_cq, s_ckv, s_co, s_gu, s_d, summed) = refs[-8:]
    total = refs[5][...]
    for part in refs[6:-15]:
        total = total + part[...]
    summed[...] = total
    whole = joined(refs[:4])
    total_at = sum(g.shape[1] for g in whole)
    steps = []
    at = 0
    for grad, (edges, names) in zip(whole, groups):
        width = grad.shape[1]
        col_mean = summed[:, at : at + width] / model_width + 1e-30
        at += width
        row_mean, mean_rows = [], []
        low = 0
        for edge, name in zip(edges, names):
            row_mean.append(rows[:, name : name + 1] / ((edge - low) * ways) + 1e-30)
            mean_rows.append(summed[:, total_at + name : total_at + name + 1] / model_width)
            low = edge
        factor = lane_pick(width, edges, row_mean) * col_mean / lane_pick(width, edges, mean_rows)
        steps.append(grad * lax.rsqrt(factor))
    for (f, b, a), (qkv, so, cq, ckv, co, gu, d) in (
        (whole, (g_qkv, g_so, g_cq, g_ckv, g_co, g_gu, g_d)),
        (steps, (s_qkv, s_so, s_cq, s_ckv, s_co, s_gu, s_d)),
    ):
        for k in range(3):
            qkv[k] = a[:, k * hq : (k + 1) * hq]
        so[...] = a[:, 3 * hq :]
        cq[...] = b[:, :hq]
        co[...] = b[:, 3 * hq :]
        d[...] = f[:, 2 * units :]
        for k in range(2):
            ckv[:, k, :] = b[:, (k + 1) * hq : (k + 2) * hq]
            gu[:, k, :] = f[:, k * units : (k + 1) * units]


def whole_block(array):
    return (array, full(array.shape))


def square_sums(grads, hq, units):
    own_rows = grads[0].shape[0]
    total = 4 * hq * 2 + 3 * units
    outs = [
        (sds((own_rows, 128), F32), full((own_rows, 128))),
        (sds((1, total), F32), full((1, total))),
    ]
    return run(
        functools.partial(square_sums_kernel, groups_of(hq, units)), 1,
        [whole_block(g) for g in grads], outs, [], 4 * own_rows * total, "square_sums",
    )


def message_of(parts, cols, gain_parts, hq, units):
    rows = parts[0]
    length = cols.shape[1] + 128 + sum(g.shape[1] for g in gain_parts)
    outs = [(sds(rows.shape, F32), full(rows.shape)), (sds((1, length), F32), full((1, length)))]
    return run(
        functools.partial(message_kernel, groups_of(hq, units), lax.axis_size("mp")), 1,
        [whole_block(g) for g in (*parts, cols, *gain_parts)], outs, [], length, "message_sums",
    )


def updates(grads, rows, parts, model_width, hq, units):
    own_rows = grads[0].shape[0]
    shapes = [
        (3, own_rows, hq), (own_rows, hq), (own_rows, hq), (own_rows, 2, hq), (own_rows, hq),
        (own_rows, 2, units), (own_rows, units),
    ]
    outs = [(sds(shape, F32), full(shape)) for shape in shapes + shapes + [parts[0].shape]]
    results = run(
        functools.partial(update_kernel, groups_of(hq, units), lax.axis_size("mp"), model_width, hq, units),
        1, [whole_block(g) for g in (*grads, rows, *parts)], outs, [], 8 * own_rows * (8 * hq + 3 * units),
        "updates",
    )
    results = list(results)
    results[0] = results[0].transpose(1, 0, 2)
    results[7] = results[7].transpose(1, 0, 2)
    return results


def on_device(
    tokens,
    memory,
    cotangent,
    table_lengths,
    table_plots,
    gains,
    w_qkv,
    w_self_out,
    w_cross_query,
    w_cross_kv,
    w_cross_out,
    w_gate_up,
    w_down,
):
    slots, width = tokens.shape
    hq = w_self_out.shape[1]
    heads = hq // DH
    units = w_down.shape[1]
    place = lax.axis_index("dp")
    x, z = place % 2, (place // 2) % 2
    ctl = jnp.stack([x, z]).astype(jnp.int32)
    gain_rows = gains.T
    gain_a, gain_b, gain_c = gain_rows[0:1], gain_rows[1:2], gain_rows[2:3]

    w_a = jnp.concatenate([w_qkv.transpose(1, 2, 0).reshape(3 * hq, width), w_self_out.T], axis=0)
    w_b = jnp.concatenate(
        [w_cross_query.T, w_cross_kv.transpose(1, 2, 0).reshape(2 * hq, width), w_cross_out.T], axis=0
    )
    w_f = jnp.concatenate(
        [w_gate_up.transpose(1, 2, 0).reshape(2 * units, width), w_down.T], axis=0
    )
    cut_f = w_f.shape[0] * 5 // 6
    ways = lax.axis_size("dp")

    ya0, ya1 = (swap(half, "mp", 2) for half in halves_of_quarter(w_a, x, z))
    send_b = y_pieces(w_b, x, z)
    send_f0, send_f1 = halves_of_quarter(w_f[:cut_f], x, z)
    ya0, ya1, send_b, send_f0, send_f1, w_a, w_b, w_f = together(
        ya0, ya1, send_b, send_f0, send_f1, w_a, w_b, w_f
    )

    y_b = swap(send_b, "mp", 2)
    xa0, za1 = swap(ya0, "dp", 1), swap(ya1, "dp", 2)
    xa1, za0 = swap(ya1, "dp", 1), swap(ya0, "dp", 2)
    qkv0, mixed_a0, lse_a0, part = self_forward(table_lengths, tokens, gain_a, w_a, heads)
    xa0, xa1, za0, za1, part, memory_late, send_f0 = together(xa0, xa1, za0, za1, part, memory, send_f0)
    da0, da1 = swap(xa0, "dp", 2), swap(za1, "dp", 1)
    y_f0 = swap(send_f0, "mp", 2)
    kv0 = memory_forward(memory_late, w_b, heads)
    send_g = w_f[cut_f:].astype(F32)
    da0, da1, kv0, send_g = together(da0, da1, kv0, send_g)
    far_a = (ya0, ya1, xa0, xa1, za0, za1, da0, da1)
    qkv1, mixed_a1, lse_a1, part, w_a1 = self_forward(
        table_lengths, tokens, gain_a, None, heads, remote=(ctl, far_a, part)
    )
    part, send_f1, y_b, y_f0 = together(part, send_f1, y_b, y_f0)

    part_other = swap(part, "mp", 1)
    y_f1 = swap(send_f1, "mp", 2)
    x_b, z_b = hand_on(y_b)
    q0, mixed_b0, lse_b0, part, first, normed_b = cross_forward(
        table_lengths, table_plots, heads, lead=(tokens, part, part_other, gain_b, w_b, kv0)
    )
    x_b, z_b, y_f1, part, send_g = together(x_b, z_b, y_f1, part, send_g)
    x_f0, z_f1 = swap(y_f0, "dp", 1), swap(y_f1, "dp", 2)
    q1, mixed_b1, lse_b1, part, w_b1, kv1 = cross_forward(
        table_lengths, table_plots, heads, follow=(normed_b, ctl, memory, part, (y_b, x_b, z_b))
    )
    send_g, x_f0, z_f1, part = together(send_g, x_f0, z_f1, part)
    far_z, far_x = hand_on_again(y_f0, y_f1, x_f0, z_f1)

    part_other = swap(part, "mp", 1)
    y_g = swap(send_g, "mp", 2)
    res, back, second, normed_c, *grad_f = feed(
        units, lead=(ctl, ways, first, part, part_other, gain_c, cotangent, w_f)
    )
    y_g, far_z, far_x, *grad_f = together(y_g, far_z, far_x, *grad_f)
    far_f = ((y_f0, y_f1, x_f0, z_f1, far_z, far_x), (y_g,))
    rs_f = halvings(grad_f, QUARTERS)
    rs_f[0].start()
    rs_f[2].start()
    res, back = feed(units, follow=(ctl, normed_c, cotangent, far_f, res, back))
    rs_f[0].got, rs_f[2].got, back = together(rs_f[0].got, rs_f[2].got, back)
    rs_f[1].start()
    rs_f[3].start()
    back_other = swap(back, "mp", 1)
    near_dq, near_dkv, grad_second, branch_b, gain_grad_c, *grad_b = cross_backward(
        table_lengths, table_plots, w_b, q0, lse_b0, kv0, heads,
        lead=(ctl, ways, second, back, back_other, cotangent, gain_c, normed_b, memory, mixed_b0),
    )
    rs_f[1].got, rs_f[3].got, res, lse_b1, *grad_b = together(
        rs_f[1].got, rs_f[3].got, res, lse_b1, *grad_b
    )
    rs_f = second_stage(rs_f, ctl)
    res_other = swap(res, "mp", 1)

    for rs in rs_f:
        rs.start()
    back, back_mem = cross_backward(
        table_lengths, table_plots, w_b1, q1, lse_b1, kv1, heads,
        follow=(branch_b, mixed_b1, near_dq, near_dkv, w_b),
    )
    rs_f[0].got, rs_f[1].got, back, res_other = together(
        rs_f[0].got, rs_f[1].got, back, res_other
    )

    back_other = swap(back, "mp", 1)
    rs_b = halvings(grad_b)
    for rs in rs_f:
        rs.finish()
    rs_f[1].start()
    for rs in rs_b:
        rs.start()
    near_rows, grad_first, branch_a, gain_grad_b, *grad_a = self_backward(
        table_lengths, w_a, qkv0, lse_a0, heads,
        lead=(ctl, ways, first, back, back_other, grad_second, gain_b, tokens, gain_a, mixed_a0),
    )
    rs_b[0].got, rs_b[1].got, rs_f[1].got, back_mem, lse_a1, *grad_a = together(
        rs_b[0].got, rs_b[1].got, rs_f[1].got, back_mem, lse_a1, *grad_a
    )
    mem_other = swap(back_mem, "mp", 1)

    rs_a = halvings(grad_a)
    for rs in rs_a:
        rs.start()
    for rs in rs_b:
        rs.finish()
        rs.start()
    rs_f[0].start()
    (back,) = self_backward(table_lengths, w_a1, qkv1, lse_a1, heads, follow=(branch_a, mixed_a1, near_rows, w_a))
    grad_memory = back_mem + mem_other
    rs_a[0].got, rs_a[1].got, rs_b[0].got, rs_b[1].got, rs_f[0].got, back, grad_memory = together(
        rs_a[0].got, rs_a[1].got, rs_b[0].got, rs_b[1].got, rs_f[0].got, back, grad_memory
    )

    back_other = swap(back, "mp", 1)
    rs_b = last_bits(rs_b)
    rs_b.start()
    for rs in rs_a:
        rs.finish()
        rs.start()
    grad_tokens, gain_grad_a = tail(tokens, back, back_other, grad_first, gain_a)
    rs_a[0].got, rs_a[1].got, rs_b.got, gain_grad_a, res, res_other, second = together(
        rs_a[0].got, rs_a[1].got, rs_b.got, gain_grad_a, res, res_other, second
    )
    rs_a = last_bits(rs_a)
    rs_a.start()
    layer_out = (second + (res + res_other)).astype(BF16)
    rs_a.got, layer_out = together(rs_a.got, layer_out)
    grads = []
    for rs in (*rs_f, rs_b, rs_a):
        rs.finish()
        grads.append(rs.rest())

    row_sums, col_sums = square_sums(grads, hq, units)
    row_sums, message = message_of(
        exchange_sums(row_sums, "mp"), col_sums, (gain_grad_a, gain_grad_b, gain_grad_c), hq, units
    )
    parts = exchange_sums(message, "dp")
    *results, message = updates(grads, row_sums, parts, width, hq, units)
    own_rows = grads[0].shape[0]
    grad_gains = lax.dynamic_slice_in_dim(
        message[:, col_sums.shape[1] + 128 :].reshape(3, width), place * own_rows, own_rows, axis=1
    ).T
    return (layer_out, grad_tokens, grad_memory, grad_gains, *results)


def solution(mesh):
    split = P("dp", None)
    cols = P(None, "mp")
    cols3 = P(None, None, "mp")
    both = P("dp", "mp")
    both3 = P("dp", None, "mp")
    return jax.shard_map(
        on_device,
        mesh=mesh,
        in_specs=(
            split, split, split, split, split, P(),
            cols3, cols, cols, cols3, cols, cols3, cols,
        ),
        out_specs=(
            split, split, split, split,
            both3, both, both, both3, both, both3, both,
            both3, both, both, both3, both, both3, both,
        ),
        check_vma=False,
    )
```

```python
import functools
import math

import jax
import jax.numpy as jnp
from jax import lax
from jax.experimental import pallas as pl
from jax.experimental.pallas import tpu as pltpu
from jax.sharding import PartitionSpec as P

DH = 64
PATCH = 256
LONGEST = 512
ROWS = 256
SPAN = LONGEST // ROWS
F32 = jnp.float32
BF16 = jnp.bfloat16
NEG = -1e30
SCALE = 1.0 / math.sqrt(DH)
FREE, NEAR = "free", "near"
VMEM_BYTES = 30 * 1024 * 1024
SMALL = 1 << 15


def nn(a, b):
    return lax.dot_general(a, b, (((1,), (0,)), ((), ())), preferred_element_type=F32)


def nt(a, b):
    return lax.dot_general(a, b, (((1,), (1,)), ((), ())), preferred_element_type=F32)


def tn(a, b):
    return lax.dot_general(a, b, (((0,), (0,)), ((), ())), preferred_element_type=F32)


def normed_of(rows, gain):
    return rows * lax.rsqrt(jnp.mean(rows * rows, axis=-1, keepdims=True) + 1e-06) * gain


def norm_vjp(rows, gain, grad):
    inv = lax.rsqrt(jnp.mean(rows * rows, axis=-1, keepdims=True) + 1e-06)
    scaled = rows * inv
    hg = grad * gain
    inner = jnp.mean(hg * scaled, axis=-1, keepdims=True)
    grad_rows = inv * (hg - scaled * inner)
    grad_gain = jnp.sum(grad * scaled, axis=0, keepdims=True)
    return grad_rows, grad_gain, scaled


def place_pieces(dst, ctl, groups):
    x, z = ctl[0], ctl[1]
    base = 0
    for refs in groups:
        q = refs[0].shape[0] // 2
        if len(refs) == 1:
            dst[base : base + 2 * q, :] = refs[0][...].astype(BF16)
            base += 2 * q
        elif len(refs) == 8:
            q = 2 * q
            me, by_x = 2 * z + x, 2 * z + 1 - x
            by_z, far = 2 * (1 - z) + x, 2 * (1 - z) + 1 - x
            for k, who in enumerate((me, by_x, by_z, far)):
                for half in range(2):
                    offset = pl.multiple_of(base + (2 * who + half) * q, 16)
                    dst[pl.ds(offset, q), :] = refs[2 * k + half][...].astype(BF16)
            base += 8 * q
        elif len(refs) == 4:
            y0, y1, x0, z1 = refs
            q, r = y0.shape[0], y1.shape[0]
            for offset, ref in ((x * q, y0), ((1 - x) * q, x0), (2 * q + z * r, y1), (2 * q + (1 - z) * r, z1)):
                dst[pl.ds(pl.multiple_of(base + offset, 16), ref.shape[0]), :] = ref[...].astype(BF16)
            base += 2 * q + 2 * r
        elif len(refs) == 3:
            by_y, by_x, by_z = refs

            def put(offset, value, base=base, q=q):
                dst[pl.ds(pl.multiple_of(base + offset, 16), q), :] = value.astype(BF16)

            put(x * q, by_y[:q, :])
            put((1 - x) * q, by_x[...])
            put((2 + z) * q, by_y[q:, :])
            put((3 - z) * q, by_z[...])
            base += 4 * q
        else:
            y0, y1, by_x, by_z, far_z, far_x = refs
            q = 2 * q

            def put(who, half, value, base=base, q=q):
                dst[pl.ds(pl.multiple_of(base + who * (2 * q) + half * q, 16), q), :] = value.astype(BF16)

            me, other_x = 2 * z + x, 2 * z + 1 - x
            other_z, other = 2 * (1 - z) + x, 2 * (1 - z) + 1 - x
            put(me, 0, y0[...])
            put(me, 1, y1[...])
            put(other_x, 0, by_x[...])
            put(other_z, 1, by_z[...])
            put(other_z, 0, far_z[:q, :])
            put(other, 0, far_z[q:, :])
            put(other_x, 1, far_x[:q, :])
            put(other, 1, far_x[q:, :])
            base += 8 * q


def table_ends(lengths):
    ends = []
    total = lengths[0, 0]
    for j in range(1, lengths.shape[1]):
        ends.append(total)
        total = total + lengths[0, j]
    return ends


def query_places(base):
    return lax.broadcasted_iota(jnp.int32, (1, ROWS), 1) + base


def self_bias(lengths, base, low, width):
    places = query_places(base)
    start = jnp.zeros_like(places)
    for end in table_ends(lengths):
        start = jnp.where(places >= end, end, start)
    keys = lax.broadcasted_iota(jnp.int32, (width, ROWS), 0) + low
    return jnp.where((keys >= start) & (keys <= places), 0.0, NEG)


def window_cases(lengths, block, body):
    base = block * ROWS
    start = jnp.int32(0)
    for end in table_ends(lengths):
        start = jnp.where(base >= end, end, start)
    needed = block - start // ROWS
    for back in range(SPAN + 1):

        @pl.when(needed == back)
        def _run(back=back):
            body(pl.multiple_of((block - back) * ROWS, ROWS), (back + 1) * ROWS)


def full(shape):
    return pl.BlockSpec(shape, lambda i: (0,) * len(shape))


def by_rows(width):
    return pl.BlockSpec((ROWS, width), lambda i: (i, 0))


def by_cols(height):
    return pl.BlockSpec((height, ROWS), lambda i: (0, i))


SMEM = pl.BlockSpec(memory_space=pltpu.SMEM)


def run(kernel, grid, ins, outs, scratch, flops, name, transcendentals=0):
    moved = sum(entry[0].size * entry[0].dtype.itemsize for entry in ins) + sum(
        math.prod(entry[0].shape) * jnp.dtype(entry[0].dtype).itemsize for entry in outs
    )
    arrays = [
        entry[0]
        if entry[-1] is FREE or entry[1] is SMEM or entry[0].size < SMALL
        else pltpu.with_memory_space_constraint(entry[0], pltpu.VMEM if entry[-1] is NEAR else pltpu.HBM)
        for entry in ins
    ]
    shapes = [
        entry[0]
        if entry[-1] is FREE or math.prod(entry[0].shape) < SMALL
        else (pltpu.VMEM if entry[-1] is NEAR else pltpu.HBM)(entry[0].shape, entry[0].dtype)
        for entry in outs
    ]
    return pl.pallas_call(
        kernel,
        grid=(grid,),
        in_specs=[entry[1] for entry in ins],
        out_specs=[entry[1] for entry in outs],
        out_shape=shapes,
        scratch_shapes=scratch,
        compiler_params=pltpu.CompilerParams(
            vmem_limit_bytes=VMEM_BYTES, dimension_semantics=("arbitrary",)
        ),
        cost_estimate=pl.CostEstimate(
            flops=flops // 64, bytes_accessed=moved // 64, transcendentals=transcendentals // 64
        ),
        name=name,
    )(*arrays)


def sds(shape, dtype):
    return jax.ShapeDtypeStruct(shape, dtype)


def self_forward_kernel(remote, heads, *refs):
    if remote:
        (lengths, ctl, tokens, gain, base_out) = refs[:5]
        pieces = refs[5:-6]
        (qkv_t, mixed_t, lse, out, w_out, k_rows) = refs[-6:]
        w = w_out
    else:
        (lengths, tokens, gain, w) = refs[:4]
        (qkv_t, mixed_t, lse, out, k_rows) = refs[4:]
    block = pl.program_id(0)
    hq = heads * DH
    if remote:

        @pl.when(block == 0)
        def _place():
            place_pieces(w, ctl, [pieces])

    base = pl.multiple_of(block * ROWS, ROWS)
    here = pl.ds(base, ROWS)
    normed = normed_of(tokens[...].astype(F32), gain[...]).astype(BF16)
    qkv = nt(w[0 : 3 * hq, :], normed).astype(BF16)
    q_all = (qkv[:hq].astype(F32) * SCALE).astype(BF16)
    qkv_t[0:hq, here] = q_all
    qkv_t[hq : 3 * hq, here] = qkv[hq:]
    for h in range(heads):
        k_rows[h, here, :] = qkv[hq + h * DH : hq + (h + 1) * DH].T

    def attend(low, width):
        window = pl.ds(low, width)
        bias = self_bias(lengths, base, low, width)
        for h in range(heads):
            own = slice(h * DH, (h + 1) * DH)
            s = nn(k_rows[h, window, :], q_all[own]) + bias
            top = jnp.max(s, axis=0, keepdims=True)
            e = jnp.exp(s - top)
            total = jnp.sum(e, axis=0, keepdims=True)
            o = nn(qkv_t[2 * hq + h * DH : 2 * hq + (h + 1) * DH, window], e.astype(BF16))
            mixed_t[own, :] = (o * (1.0 / total)).astype(BF16)
            lse[h : h + 1, :] = top + jnp.log(total)

    window_cases(lengths, block, attend)
    part = tn(mixed_t[...], w[3 * hq : 4 * hq, :])
    out[...] = part + base_out[...] if remote else part


def self_forward(lengths, tokens, gain, w, heads, remote=None):
    slots, width = tokens.shape
    hq = heads * DH
    outs = [
        (sds((3 * hq, slots), BF16), full((3 * hq, slots))),
        (sds((hq, slots), BF16), by_cols(hq)),
        (sds((8, slots), F32), by_cols(8)),
        (sds((slots, width), F32), by_rows(width), NEAR),
    ]
    scratch = [pltpu.VMEM((heads, slots, DH), BF16)]
    if remote is None:
        ins = [(lengths, SMEM), (tokens, by_rows(width)), (gain, full(gain.shape)), (w, full(w.shape))]
    else:
        ctl, pieces, base_out = remote
        ins = [
            (lengths, SMEM),
            (ctl, SMEM),
            (tokens, by_rows(width)),
            (gain, full(gain.shape)),
            (base_out, by_rows(width), NEAR),
        ]
        ins += [(piece, full(piece.shape)) for piece in pieces]
        outs.append((sds((4 * hq, width), BF16), full((4 * hq, width))))
    flops = 2 * slots * width * 4 * hq + heads * 4 * slots * slots * DH
    return run(
        functools.partial(self_forward_kernel, remote is not None, heads),
        slots // ROWS, ins, outs, scratch, flops, "self_forward", heads * slots * slots,
    )


def memory_kernel(hq, memory, w, kv_t):
    kv_t[...] = nt(w[hq : 3 * hq, :], memory[...]).astype(BF16)


def memory_forward(memory, w, heads):
    count, width = memory.shape
    hq = heads * DH
    (kv_t,) = run(
        functools.partial(memory_kernel, hq), count // ROWS,
        [(memory, by_rows(width)), (w, full(w.shape))],
        [(sds((2 * hq, count), BF16), by_cols(2 * hq))], [], 2 * count * width * 2 * hq, "memory_forward",
    )
    return kv_t


def rows_of_heads(rows, columns, heads):
    for h in range(heads):
        rows[h] = columns[h * DH : (h + 1) * DH, :].T


def tables_of_block(lengths, base, body):
    ends = table_ends(lengths)
    places = query_places(base)
    segment = jnp.zeros_like(places)
    first_table = jnp.int32(0)
    last_table = jnp.int32(0)
    for end in ends:
        segment = segment + (places >= end).astype(jnp.int32)
        first_table = first_table + (base >= end).astype(jnp.int32)
        last_table = last_table + (base + ROWS - 1 >= end).astype(jnp.int32)

    def step(table, carry):
        body(table, segment == table)
        return carry

    lax.fori_loop(first_table, last_table + 1, step, 0)


def cross_forward_kernel(leading, heads, *refs):
    hq = heads * DH
    k_rows = refs[-1]
    if leading:
        (lengths, plots, tokens, part, other, gain, w, kv_t) = refs[:8]
        (q_t, mixed_t, lse, out, first, normed_out) = refs[8:-1]
    else:
        (lengths, plots, ctl, normed_in, memory, base_out) = refs[:6]
        (q_t, mixed_t, lse, out, w, kv_t) = refs[-7:-1]

    @pl.when(pl.program_id(0) == 0)
    def _start():
        if not leading:
            place_pieces(w, ctl, [refs[6:-7]])
            for m in range(memory.shape[0] // ROWS):
                here = slice(m * ROWS, (m + 1) * ROWS)
                kv_t[:, here] = nt(w[hq : 3 * hq, :], memory[here, :]).astype(BF16)
        rows_of_heads(k_rows, kv_t, heads)

    if leading:
        rows = tokens[...].astype(F32) + (part[...] + other[...])
        first[...] = rows
        normed = normed_of(rows, gain[...]).astype(BF16)
        normed_out[...] = normed
    else:
        normed = normed_in[...]
    base = pl.multiple_of(pl.program_id(0) * ROWS, ROWS)
    query = nt(w[0:hq, :], normed).astype(BF16)
    q_all = (query.astype(F32) * SCALE).astype(BF16)
    q_t[...] = q_all

    def table(j, member):
        plot = pl.ds(pl.multiple_of(plots[0, j] * PATCH, PATCH), PATCH)
        for h in range(heads):
            own = slice(h * DH, (h + 1) * DH)
            s = nn(k_rows[h, plot, :], q_t[own, :])
            top = jnp.max(s, axis=0, keepdims=True)
            e = jnp.exp(s - top)
            total = jnp.sum(e, axis=0, keepdims=True)
            o = nn(kv_t[hq + h * DH : hq + (h + 1) * DH, plot], e.astype(BF16))
            o = o * (1.0 / total)
            mixed_t[own, :] = jnp.where(member, o, mixed_t[own, :].astype(F32)).astype(BF16)
            lse[h : h + 1, :] = jnp.where(member, top + jnp.log(total), lse[h : h + 1, :])

    tables_of_block(lengths, base, table)
    part_out = tn(mixed_t[...], w[3 * hq : 4 * hq, :])
    out[...] = part_out if leading else part_out + base_out[...]


def cross_forward(lengths, plots, heads, lead=None, follow=None):
    hq = heads * DH
    slots, width = (lead or follow)[0].shape
    outs = [
        (sds((hq, slots), BF16), by_cols(hq)),
        (sds((hq, slots), BF16), by_cols(hq)),
        (sds((8, slots), F32), by_cols(8)),
        (sds((slots, width), F32), by_rows(width), NEAR),
    ]
    if lead is not None:
        tokens, part, other, gain, w, kv_t = lead
        count = kv_t.shape[1]
        ins = [
            (lengths, SMEM),
            (plots, SMEM),
            (tokens, by_rows(width)),
            (part, by_rows(width), NEAR),
            (other, by_rows(width), NEAR),
            (gain, full(gain.shape)),
            (w, full(w.shape)),
            (kv_t, full(kv_t.shape)),
        ]
        outs += [
            (sds((slots, width), F32), by_rows(width)),
            (sds((slots, width), BF16), by_rows(width)),
        ]
    else:
        normed, ctl, memory, base_out, pieces = follow
        count = memory.shape[0]
        ins = [
            (lengths, SMEM),
            (plots, SMEM),
            (ctl, SMEM),
            (normed, by_rows(width)),
            (memory, full(memory.shape)),
            (base_out, by_rows(width), NEAR),
        ]
        ins += [(piece, full(piece.shape)) for piece in pieces]
        outs += [
            (sds((4 * hq, width), BF16), full((4 * hq, width))),
            (sds((2 * hq, count), BF16), full((2 * hq, count))),
        ]
    flops = 2 * slots * width * 2 * hq + heads * 8 * slots * PATCH * DH
    return run(
        functools.partial(cross_forward_kernel, lead is not None, heads),
        slots // ROWS, ins, outs, [pltpu.VMEM((heads, count, DH), BF16)], flops, "cross_forward",
        heads * slots * PATCH * 2,
    )


def column_parts(width, cuts):
    edges = [0] + [width * cut // 12 for cut in cuts] + [width]
    bits = [1] * ((len(cuts) + 1) // 2) + [2] * ((len(cuts) + 1) // 2)
    return list(zip(edges[:-1], edges[1:], bits))


HALVES, THIRDS, QUARTERS = (6,), (8,), (2, 6, 8)


def gradient_outs(count, rows, width, cuts=HALVES):
    if split_bits(rows, count):
        return [
            (sds((rows // 2, high - low), F32), full((rows // 2, high - low)))
            for low, high, _ in column_parts(width, cuts)
            for _ in range(2)
        ]
    return [(sds((rows, width), F32), full((rows, width)))]


def finish_gradient(count, ctl, source, outs, cuts=HALVES):
    @pl.when(pl.program_id(0) == pl.num_programs(0) - 1)
    def _write():
        if len(outs) == 1:
            outs[0][...] = source[...]
        else:
            for k, (low, high, bit) in enumerate(column_parts(source.shape[1], cuts)):
                write_split(source, low, high, count, bit, ctl[bit - 1], outs[2 * k], outs[2 * k + 1])


def halvings(outs, cuts=HALVES):
    order = {1: (1, 2, 4), 2: (2, 1, 4)}
    if len(outs) == 1:
        parts = column_parts(outs[0].shape[1], cuts)
        return [Halving(outs[0][:, low:high], order[bit]) for low, high, bit in parts]
    bits = [bit for _, _, bit in column_parts(12, cuts)]
    return [Halving(None, order[bit], outs[2 * k : 2 * k + 2]) for k, bit in enumerate(bits)]


def feed_kernel(leading, units, count, *refs):
    if leading:
        (ctl, first, part, other, gain, cot, w) = refs[:7]
        (result, grad_in, second, normed_out) = refs[7:11]
        dw_outs = refs[11:-4]
        dw, normed_all, cot_all, inner_all = refs[-4:]
        rows = first[...] + (part[...] + other[...])
        second[...] = rows
        normed = normed_of(rows, gain[...]).astype(BF16)
        normed_out[...] = normed
    else:
        (ctl, normed_in, cot, base_result, base_grad) = refs[:5]
        pieces = refs[5:-3]
        (result, grad_in, w) = refs[-3:]
        normed = normed_in[...]

        @pl.when(pl.program_id(0) == 0)
        def _place():
            place_pieces(w, ctl, [pieces[:6], pieces[6:]])

    cot_rows = cot[...]
    gate_up = nt(normed, w[0 : 2 * units, :])
    gate, up = gate_up[:, :units], gate_up[:, units:]
    c0 = math.sqrt(2.0 / math.pi)
    square = gate * gate
    th = jnp.tanh(c0 * gate * (1.0 + 0.044715 * square))
    half = 0.5 * (1.0 + th)
    gelu = gate * half
    slope = half + (0.5 * c0) * gate * (1.0 - th * th) * (1.0 + (3 * 0.044715) * square)
    hidden = (gelu * up).astype(BF16)
    res = nn(hidden, w[2 * units : 3 * units, :])
    grad_hidden = nt(cot_rows, w[2 * units : 3 * units, :])
    grad_gate = (grad_hidden * up * slope).astype(BF16)
    grad_up = (grad_hidden * gelu).astype(BF16)
    back = nn(grad_gate, w[0:units, :]) + nn(grad_up, w[units : 2 * units, :])
    if leading:
        result[...] = res
        grad_in[...] = back
        here = pl.ds(pl.multiple_of(pl.program_id(0) * ROWS, ROWS), ROWS)
        normed_all[here, :] = normed
        cot_all[here, :] = cot_rows
        inner_all[here, 0:units] = grad_gate
        inner_all[here, units : 2 * units] = grad_up
        inner_all[here, 2 * units : 3 * units] = hidden

        @pl.when(pl.program_id(0) == pl.num_programs(0) - 1)
        def _weights():
            for m in range(dw.shape[0] // ROWS):
                rows = slice(m * ROWS, (m + 1) * ROWS)
                dw[rows, 0 : 2 * units] = tn(normed_all[:, rows], inner_all[:, 0 : 2 * units])
                dw[rows, 2 * units : 3 * units] = tn(cot_all[:, rows], inner_all[:, 2 * units : 3 * units])

        finish_gradient(count, ctl, dw, dw_outs, QUARTERS)
    else:
        result[...] = res + base_result[...]
        grad_in[...] = back + base_grad[...]


def feed(units, lead=None, follow=None):
    if lead is not None:
        ctl, count, first, part, other, gain, cot, w = lead
        slots, width = first.shape
        ins = [
            (ctl, SMEM),
            (first, by_rows(width)),
            (part, by_rows(width), NEAR),
            (other, by_rows(width), NEAR),
            (gain, full(gain.shape)),
            (cot, by_rows(width)),
            (w, full(w.shape)),
        ]
    else:
        ctl, normed, cot, pieces, base_result, base_grad = follow
        slots, width = normed.shape
        ins = [(ctl, SMEM), (normed, by_rows(width), FREE), (cot, by_rows(width))]
        ins += [(base_result, by_rows(width), FREE), (base_grad, by_rows(width), NEAR)]
        ins += [(piece, full(piece.shape)) for group in pieces for piece in group]
    outs = [
        (sds((slots, width), F32), by_rows(width), FREE),
        (sds((slots, width), F32), by_rows(width), NEAR),
    ]
    scratch = []
    if lead is not None:
        outs += [
            (sds((slots, width), F32), by_rows(width)),
            (sds((slots, width), BF16), by_rows(width), FREE),
        ]
        outs += gradient_outs(count, width, 3 * units, QUARTERS)
        scratch = [
            pltpu.VMEM((width, 3 * units), F32),
            pltpu.VMEM((slots, width), BF16),
            pltpu.VMEM((slots, width), BF16),
            pltpu.VMEM((slots, 3 * units), BF16),
        ]
    else:
        count = 0
        scratch = [pltpu.VMEM((3 * units, width), BF16)]
    flops = 2 * slots * width * units * (9 if lead is not None else 6)
    return run(
        functools.partial(feed_kernel, lead is not None, units, count),
        slots // ROWS, ins, outs, scratch, flops, "feed", slots * units,
    )


def cross_backward_kernel(leading, heads, count, *refs):
    hq = heads * DH
    if leading:
        (ctl, lengths, plots, second, part, other, cot, gain, normed, memory) = refs[:10]
        (w, q_t, mixed_t, lse, kv_t) = refs[10:15]
        (dq_out, dkv_out, branch_out, grad_gain) = refs[15:19]
        dw_outs = refs[19:-7]
        (dkv, dq, dm, k_rows, v_rows, dw_t, dw) = refs[-7:]
    else:
        (lengths, plots, branch_in, w, q_t, mixed_t, lse, kv_t, near_dq, near_dkv, near_w) = refs[:11]
        (grad_in, grad_mem, dkv, dq, dm, k_rows, v_rows) = refs[11:]
    block = pl.program_id(0)
    last = pl.num_programs(0) - 1
    base = pl.multiple_of(block * ROWS, ROWS)

    @pl.when(block == 0)
    def _zero():
        dkv[...] = jnp.zeros_like(dkv)
        rows_of_heads(k_rows, kv_t[0:hq, :], heads)
        rows_of_heads(v_rows, kv_t[hq : 2 * hq, :], heads)
        if leading:
            dw_t[...] = jnp.zeros_like(dw_t)
            grad_gain[...] = jnp.zeros_like(grad_gain)

    if leading:
        grad_rows, gain_rows, _ = norm_vjp(second[...], gain[...], part[...] + other[...])
        branch = (cot[...].astype(F32) + grad_rows).astype(BF16)
        branch_out[...] = branch
        grad_gain[0:1, :] += gain_rows
    else:
        branch = branch_in[...]
    dm[...] = nt(w[3 * hq : 4 * hq, :], branch).astype(BF16)
    dq[...] = jnp.zeros_like(dq)

    def table(j, member):
        plot = pl.ds(pl.multiple_of(plots[0, j] * PATCH, PATCH), PATCH)
        for h in range(heads):
            own = slice(h * DH, (h + 1) * DH)
            val = slice(hq + h * DH, hq + (h + 1) * DH)
            query = q_t[own, :]
            dmix = jnp.where(member, dm[own, :].astype(F32), 0.0).astype(BF16)
            level = jnp.where(member, lse[h : h + 1, :], -NEG)
            p = jnp.exp(nn(k_rows[h, plot, :], query) - level)
            dp = nn(v_rows[h, plot, :], dmix)
            inner = jnp.sum(dmix.astype(F32) * mixed_t[own, :].astype(F32), axis=0, keepdims=True)
            ds = (p * (dp - inner)).astype(BF16)
            dkv[own, plot] += nt(query, ds)
            dkv[val, plot] += nt(dmix, p.astype(BF16))
            dq[own, :] += nn(kv_t[own, plot], ds)

    tables_of_block(lengths, base, table)
    grad_query = (dq[...] * SCALE).astype(BF16)
    if leading:
        dq_out[...] = grad_query
        dw_t[0:hq, :] += nn(grad_query, normed[...])
        dw_t[3 * hq : 4 * hq, :] += nn(mixed_t[...], branch)
    else:
        grad_in[...] = tn(grad_query, w[0:hq, :]) + tn(near_dq[...], near_w[0:hq, :])

    @pl.when(block == last)
    def _finish():
        for m in range(dkv.shape[1] // ROWS):
            here = slice(m * ROWS, (m + 1) * ROWS)
            rows = dkv[:, here].astype(BF16)
            if not leading:
                back_mem = tn(rows, w[hq : 3 * hq, :])
                grad_mem[here, :] = back_mem + tn(near_dkv[:, here], near_w[hq : 3 * hq, :])
            else:
                dkv_out[:, here] = rows
                dw_t[hq : 3 * hq, :] += nn(rows, memory[here, :])
        if leading:
            dw[...] = dw_t[...].T

    if leading:
        finish_gradient(count, ctl, dw, dw_outs)


def cross_backward(lengths, plots, w, q_t, lse, kv_t, heads, lead=None, follow=None):
    hq = heads * DH
    slots, width = q_t.shape[1], w.shape[1]
    count = kv_t.shape[1]
    scratch = [
        pltpu.VMEM((2 * hq, count), F32),
        pltpu.VMEM((hq, ROWS), F32),
        pltpu.VMEM((hq, ROWS), BF16),
        pltpu.VMEM((heads, count, DH), BF16),
        pltpu.VMEM((heads, count, DH), BF16),
    ]
    heads_part = [
        (lse, by_cols(8)),
        (kv_t, full(kv_t.shape)),
    ]
    if lead is not None:
        ctl, split, second, part, other, cot, gain, normed, memory, mixed_t = lead
        ins = [
            (ctl, SMEM),
            (lengths, SMEM),
            (plots, SMEM),
            (second, by_rows(width)),
            (part, by_rows(width), NEAR),
            (other, by_rows(width), NEAR),
            (cot, by_rows(width)),
            (gain, full(gain.shape)),
            (normed, by_rows(width)),
            (memory, full(memory.shape)),
            (w, full(w.shape)),
            (q_t, by_cols(hq)),
            (mixed_t, by_cols(hq)),
        ] + heads_part
        outs = [
            (sds((hq, slots), BF16), by_cols(hq)),
            (sds((2 * hq, count), BF16), full((2 * hq, count))),
            (sds((slots, width), BF16), by_rows(width)),
            (sds((8, width), F32), full((8, width))),
        ]
        outs += gradient_outs(split, width, 4 * hq)
        scratch += [pltpu.VMEM((4 * hq, width), F32), pltpu.VMEM((width, 4 * hq), F32)]
    else:
        split = 0
        branch, mixed_t, near_dq, near_dkv, near_w = follow
        outs = [
            (sds((slots, width), F32), by_rows(width), NEAR),
            (sds((count, width), F32), full((count, width))),
        ]
        ins = [
            (lengths, SMEM),
            (plots, SMEM),
            (branch, by_rows(width)),
            (w, full(w.shape)),
            (q_t, by_cols(hq)),
            (mixed_t, by_cols(hq)),
        ] + heads_part
        ins += [(near_dq, by_cols(hq)), (near_dkv, full(near_dkv.shape)), (near_w, full(near_w.shape))]
    flops = 2 * slots * width * hq * (8 if lead is not None else 4) + heads * 20 * slots * PATCH * DH
    return run(
        functools.partial(cross_backward_kernel, lead is not None, heads, split),
        slots // ROWS, ins, outs, scratch, flops, "cross_backward", heads * slots * PATCH * 2,
    )


def self_backward_kernel(leading, heads, count, *refs):
    hq = heads * DH
    if leading:
        (ctl, lengths, first, part, other, carried, gain, tokens, gain_in, w, qkv_t, mixed_t, lse) = refs[:13]
        (dqkv_out, branch_out, grad_gain) = refs[13:16]
        dw_outs = refs[16:-6]
        (dkv, k_rows, v_rows, dqkv, dw_t, dw) = refs[-6:]
    else:
        (lengths, branch_in, w, qkv_t, mixed_t, lse, near_rows, near_w) = refs[:8]
        (grad_in, dkv, k_rows, v_rows, dqkv) = refs[8:]
    step = pl.program_id(0)
    last = pl.num_programs(0) - 1
    block = last - step
    base = pl.multiple_of(block * ROWS, ROWS)
    here = pl.ds(base, ROWS)

    @pl.when(step == 0)
    def _start():
        dkv[...] = jnp.zeros_like(dkv)
        for h in range(heads):
            k_rows[h] = qkv_t[hq + h * DH : hq + (h + 1) * DH, :].T
            v_rows[h] = qkv_t[2 * hq + h * DH : 2 * hq + (h + 1) * DH, :].T
        if leading:
            dw_t[...] = jnp.zeros_like(dw_t)
            grad_gain[...] = jnp.zeros_like(grad_gain)

    if leading:
        grad_rows, gain_rows, _ = norm_vjp(first[...], gain[...], part[...] + other[...])
        branch = (carried[...].astype(F32) + grad_rows).astype(BF16)
        branch_out[...] = branch
        grad_gain[0:1, :] += gain_rows
    else:
        branch = branch_in[...]
    dm_all = nt(w[3 * hq : 4 * hq, :], branch).astype(BF16)

    def attend(low, width):
        window = pl.ds(low, width)
        bias = self_bias(lengths, base, low, width)
        for h in range(heads):
            own = slice(h * DH, (h + 1) * DH)
            key = slice(hq + h * DH, hq + (h + 1) * DH)
            val = slice(hq + h * DH, hq + (h + 1) * DH)
            query = qkv_t[own, here]
            dmix = dm_all[own]
            p = jnp.exp(nn(k_rows[h, window, :], query) + bias - lse[h : h + 1, :])
            dp = nn(v_rows[h, window, :], dmix)
            inner = jnp.sum(dmix.astype(F32) * mixed_t[own, :].astype(F32), axis=0, keepdims=True)
            ds = (p * (dp - inner)).astype(BF16)
            dkv[own, window] += nt(query, ds)
            dkv[val, window] += nt(dmix, p.astype(BF16))
            dqkv[own, :] = (nn(qkv_t[key, window], ds) * SCALE).astype(BF16)

    window_cases(lengths, block, attend)
    dqkv[hq : 3 * hq, :] = dkv[:, here].astype(BF16)
    rows = dqkv[...]
    if not leading:
        grad_in[...] = tn(rows, w[0 : 3 * hq, :]) + tn(near_rows[...], near_w[0 : 3 * hq, :])
    else:
        dqkv_out[...] = rows
        normed = normed_of(tokens[...].astype(F32), gain_in[...]).astype(BF16)
        dw_t[0 : 3 * hq, :] += nn(rows, normed)
        dw_t[3 * hq : 4 * hq, :] += nn(mixed_t[...], branch)

        @pl.when(step == last)
        def _finish():
            dw[...] = dw_t[...].T

        finish_gradient(count, ctl, dw, dw_outs, THIRDS)


def self_backward(lengths, w, qkv_t, lse, heads, lead=None, follow=None):
    hq = heads * DH
    slots, width = qkv_t.shape[1], w.shape[1]
    last = slots // ROWS - 1
    rows = pl.BlockSpec((ROWS, width), lambda i: (last - i, 0))

    def cols(height):
        return pl.BlockSpec((height, ROWS), lambda i: (0, last - i))

    scratch = [
        pltpu.VMEM((2 * hq, slots), F32),
        pltpu.VMEM((heads, slots, DH), BF16),
        pltpu.VMEM((heads, slots, DH), BF16),
        pltpu.VMEM((3 * hq, ROWS), BF16),
    ]
    if lead is not None:
        ctl, count, first, part, other, carried, gain, tokens, gain_in, mixed_t = lead
        ins = [
            (ctl, SMEM),
            (lengths, SMEM),
            (first, rows),
            (part, rows, NEAR),
            (other, rows, NEAR),
            (carried, rows),
            (gain, full(gain.shape)),
            (tokens, rows),
            (gain_in, full(gain_in.shape)),
            (w, full(w.shape)),
            (qkv_t, full(qkv_t.shape)),
            (mixed_t, cols(hq)),
            (lse, cols(8)),
        ]
        outs = [
            (sds((3 * hq, slots), BF16), cols(3 * hq)),
            (sds((slots, width), BF16), rows),
            (sds((8, width), F32), full((8, width))),
        ]
        outs += gradient_outs(count, width, 4 * hq, THIRDS)
        scratch += [pltpu.VMEM((4 * hq, width), F32), pltpu.VMEM((width, 4 * hq), F32)]
    else:
        count = 0
        branch, mixed_t, near_rows, near_w = follow
        outs = [(sds((slots, width), F32), rows, NEAR)]
        ins = [
            (lengths, SMEM),
            (branch, rows),
            (w, full(w.shape)),
            (qkv_t, full(qkv_t.shape)),
            (mixed_t, cols(hq)),
            (lse, cols(8)),
            (near_rows, cols(3 * hq)),
            (near_w, full(near_w.shape)),
        ]
    flops = 2 * slots * width * hq * (8 if lead is not None else 4) + heads * 10 * slots * slots * DH
    return run(
        functools.partial(self_backward_kernel, lead is not None, heads, count),
        slots // ROWS, ins, outs, scratch, flops, "self_backward", heads * slots * slots,
    )


def tail_kernel(tokens, part, other, carried, gain, grad_tokens, grad_gain):
    @pl.when(pl.program_id(0) == 0)
    def _zero():
        grad_gain[...] = jnp.zeros_like(grad_gain)

    grad_rows, gain_rows, _ = norm_vjp(tokens[...].astype(F32), gain[...], part[...] + other[...])
    grad_tokens[...] = carried[...].astype(F32) + grad_rows
    grad_gain[0:1, :] += gain_rows


def tail(tokens, part, other, carried, gain):
    slots, width = tokens.shape
    rows = slots // 2

    def by_halves():
        return pl.BlockSpec((rows, width), lambda i: (i, 0))

    ins = [
        (tokens, by_halves()),
        (part, by_halves(), NEAR),
        (other, by_halves(), NEAR),
        (carried, by_halves()),
        (gain, full(gain.shape)),
    ]
    outs = [
        (sds((slots, width), F32), by_halves()),
        (sds((8, width), F32), full((8, width))),
    ]
    return run(tail_kernel, slots // rows, ins, outs, [], 20 * slots * width, "last_norm")


def swap(value, axis, bit):
    count = lax.axis_size(axis)
    return lax.ppermute(value, axis, [(i, i ^ bit) for i in range(count)])


def y_pieces(w, x, z):
    quarter = w.shape[0] // 4
    pieces = w.reshape(4, quarter, w.shape[1])
    mine = jnp.concatenate(
        [jnp.where(x == 0, pieces[0], pieces[1]), jnp.where(z == 0, pieces[2], pieces[3])], axis=0
    )
    return mine.astype(F32)


def hand_on(by_y):
    quarter = by_y.shape[0] // 2
    return swap(by_y[:quarter], "dp", 1), swap(by_y[quarter:], "dp", 2)


def hand_on_again(y0, y1, by_x, by_z):
    far_z = swap(jnp.concatenate([y0, by_x], axis=0), "dp", 2)
    far_x = swap(jnp.concatenate([y1, by_z], axis=0), "dp", 1)
    return far_z, far_x


def halves_of_quarter(w, x, z):
    eighth = w.shape[0] // 8
    start = (2 * z + x) * 2 * eighth
    halves = [lax.dynamic_slice_in_dim(w, start + k * eighth, eighth, axis=0) for k in range(2)]
    return [half.astype(F32) for half in halves]


def together(*values):
    return lax.optimization_barrier(values)


def split_bits(grad_rows, count):
    return count >= 4 and (grad_rows // count) % 8 == 0


def write_split(source, low, high, count, bit, mine, sent, kept):
    own = source.shape[0] // count
    for r in range(count // 2):
        base = (r // bit) * 2 * bit + r % bit
        rows = slice(r * own, (r + 1) * own)
        kept[rows, :] = source[pl.ds(pl.multiple_of((base + mine * bit) * own, 8), own), low:high]
        sent[rows, :] = source[pl.ds(pl.multiple_of((base + (1 - mine) * bit) * own, 8), own), low:high]


def second_stage_kernel(own, widths, ctl, *refs):
    for side, mine in ((0, ctl[1]), (1, ctl[0])):
        pairs = refs[4 * side : 4 * side + 4]
        sent, kept = refs[8 + 2 * side : 10 + 2 * side]
        for r in range(sent.shape[0] // own):
            rows = slice(r * own, (r + 1) * own)
            for dst, bit in ((sent, 1 - mine), (kept, mine)):
                here = pl.ds(pl.multiple_of((2 * r + bit) * own, 8), own)
                dst[rows, : widths[0]] = pairs[0][here, :] + pairs[1][here, :]
                dst[rows, widths[0] :] = pairs[2][here, :] + pairs[3][here, :]


def second_stage(group, ctl):
    if group[0].kept.shape[-2] % 8 or group[0].count < 8:
        return [last_bits(group[0:2]), last_bits(group[2:4])]
    ins, widths = [(ctl, SMEM)], []
    for rs in group:
        flat = rs.kept.reshape(rs.got.shape)
        ins += [whole_block(flat), whole_block(rs.got)]
        widths.append(flat.shape[1])
    rows, total = ins[1][0].shape[0] // 2, widths[0] + widths[1]
    outs = [(sds((rows, total), F32), full((rows, total))) for _ in range(4)]
    own = group[0].kept.shape[-2]
    arrays = run(
        functools.partial(second_stage_kernel, own, widths[:2]), 1, ins, outs, [], rows * total * 4, "second_stage"
    )
    halves = []
    for side, order in enumerate(((2, 4), (1, 4))):
        rs = Halving(None, order, arrays[2 * side : 2 * side + 2])
        rs.left.remove(3 - order[0])
        halves.append(rs)
    return halves


def last_bits(group, finished=0):
    for rs in group[finished:]:
        rs.finish()
    both = Halving.__new__(Halving)
    both.__dict__.update(group[0].__dict__)
    both.grad = jnp.concatenate([rs.grad for rs in group], axis=-1)
    return both


class Halving:
    def __init__(self, grad, order, halves=None):
        self.halves = halves
        self.count = lax.axis_size("dp")
        self.place = lax.axis_index("dp")
        self.order = list(order)
        bit = 8
        while bit < self.count:
            self.order.append(bit)
            bit *= 2
        self.left = [b for b in (1 << k for k in range(self.count.bit_length() - 1))][::-1]
        if halves is None:
            self.grad = grad.reshape((2,) * len(self.left) + (grad.shape[0] // self.count, grad.shape[1]))

    def send(self):
        bit = self.order.pop(0)
        axis = self.left.index(bit)
        self.left.pop(axis)
        if self.halves is not None:
            sent, kept = self.halves
            self.halves = None
            shape = (2,) * len(self.left) + (kept.shape[0] >> len(self.left), kept.shape[1])
            self.kept = kept.reshape(shape)
            return sent.reshape(shape), bit
        mine = (self.place // bit) % 2
        sent = lax.dynamic_index_in_dim(self.grad, 1 - mine, axis=axis, keepdims=False)
        self.kept = lax.dynamic_index_in_dim(self.grad, mine, axis=axis, keepdims=False)
        return sent, bit

    def start(self):
        self.prepare()
        self.go()

    def prepare(self):
        sent, self.bit = self.send()
        self.flat = sent.reshape(-1, sent.shape[-1])

    def go(self):
        self.got = swap(self.flat, "dp", self.bit)

    def finish(self):
        self.grad = self.kept + self.got.reshape(self.kept.shape)

    def rest(self):
        while self.order:
            self.start()
            self.finish()
        return self.grad.reshape(-1, self.grad.shape[-1])


def exchange_sums(value, axis):
    bit = 1
    while bit * 4 < lax.axis_size(axis):
        value = value + swap(value, axis, bit)
        bit *= 2
    return [value] + [swap(value, axis, k * bit) for k in range(1, lax.axis_size(axis) // bit)]


def lane_pick(width, edges, values):
    lanes = lax.broadcasted_iota(jnp.int32, (1, width), 1)
    picked = values[-1]
    for edge, value in zip(edges[-2::-1], values[-2::-1]):
        picked = jnp.where(lanes < edge, value, picked)
    return picked


def groups_of(hq, units):
    return (
        ((2 * units, 3 * units), (0, 1)),
        ((hq, 3 * hq, 4 * hq), (2, 3, 4)),
        ((3 * hq, 4 * hq), (5, 6)),
    )


def joined(refs):
    grad_f0, grad_f1, grad_b, grad_a = (ref[...] for ref in refs)
    return jnp.concatenate([grad_f0, grad_f1], axis=1), grad_b, grad_a


def square_sums_kernel(groups, *refs):
    rows, cols = refs[4:]
    places = lax.broadcasted_iota(jnp.int32, (1, rows.shape[1]), 1)
    sums = jnp.zeros(rows.shape, F32)
    at = 0
    for grad, (edges, names) in zip(joined(refs[:4]), groups):
        square = grad * grad
        cols[:, at : at + grad.shape[1]] = jnp.sum(square, axis=0, keepdims=True)
        at += grad.shape[1]
        lanes = lax.broadcasted_iota(jnp.int32, (1, grad.shape[1]), 1)
        low = 0
        for edge, name in zip(edges, names):
            inside = (lanes >= low) & (lanes < edge)
            total = jnp.sum(jnp.where(inside, square, 0.0), axis=1, keepdims=True)
            sums = jnp.where(places == name, total, sums)
            low = edge
    rows[...] = sums


def message_kernel(groups, ways, *refs):
    cols, gain_a, gain_b, gain_c, rows_out, message = refs[-6:]
    total = refs[0][...]
    for part in refs[1:-6]:
        total = total + part[...]
    rows_out[...] = total
    places = lax.broadcasted_iota(jnp.int32, (1, total.shape[1]), 1)
    scale = jnp.zeros((1, total.shape[1]), F32)
    for edges, names in groups:
        low = 0
        for edge, name in zip(edges, names):
            scale = jnp.where(places == name, 1.0 / ((edge - low) * ways), scale)
            low = edge
    at = cols.shape[1]
    message[:, :at] = cols[...]
    message[:, at : at + 128] = jnp.sum(total * scale + 1e-30, axis=0, keepdims=True)
    at += 128
    for gain in (gain_a, gain_b, gain_c):
        message[:, at : at + gain.shape[1]] = gain[0:1, :]
        at += gain.shape[1]


def update_kernel(groups, ways, model_width, hq, units, *refs):
    rows = refs[4]
    (g_qkv, g_so, g_cq, g_ckv, g_co, g_gu, g_d) = refs[-15:-8]
    (s_qkv, s_so, s_cq, s_ckv, s_co, s_gu, s_d, summed) = refs[-8:]
    total = refs[5][...]
    for part in refs[6:-15]:
        total = total + part[...]
    summed[...] = total
    whole = joined(refs[:4])
    total_at = sum(g.shape[1] for g in whole)
    steps = []
    at = 0
    for grad, (edges, names) in zip(whole, groups):
        width = grad.shape[1]
        col_mean = summed[:, at : at + width] / model_width + 1e-30
        at += width
        row_mean, mean_rows = [], []
        low = 0
        for edge, name in zip(edges, names):
            row_mean.append(rows[:, name : name + 1] / ((edge - low) * ways) + 1e-30)
            mean_rows.append(summed[:, total_at + name : total_at + name + 1] / model_width)
            low = edge
        factor = lane_pick(width, edges, row_mean) * col_mean / lane_pick(width, edges, mean_rows)
        steps.append(grad * lax.rsqrt(factor))
    for (f, b, a), (qkv, so, cq, ckv, co, gu, d) in (
        (whole, (g_qkv, g_so, g_cq, g_ckv, g_co, g_gu, g_d)),
        (steps, (s_qkv, s_so, s_cq, s_ckv, s_co, s_gu, s_d)),
    ):
        for k in range(3):
            qkv[k] = a[:, k * hq : (k + 1) * hq]
        so[...] = a[:, 3 * hq :]
        cq[...] = b[:, :hq]
        co[...] = b[:, 3 * hq :]
        d[...] = f[:, 2 * units :]
        for k in range(2):
            ckv[:, k, :] = b[:, (k + 1) * hq : (k + 2) * hq]
            gu[:, k, :] = f[:, k * units : (k + 1) * units]


def whole_block(array):
    return (array, full(array.shape))


def square_sums(grads, hq, units):
    own_rows = grads[0].shape[0]
    total = 4 * hq * 2 + 3 * units
    outs = [
        (sds((own_rows, 128), F32), full((own_rows, 128))),
        (sds((1, total), F32), full((1, total))),
    ]
    return run(
        functools.partial(square_sums_kernel, groups_of(hq, units)), 1,
        [whole_block(g) for g in grads], outs, [], 4 * own_rows * total, "square_sums",
    )


def message_of(parts, cols, gain_parts, hq, units):
    rows = parts[0]
    length = cols.shape[1] + 128 + sum(g.shape[1] for g in gain_parts)
    outs = [(sds(rows.shape, F32), full(rows.shape)), (sds((1, length), F32), full((1, length)))]
    return run(
        functools.partial(message_kernel, groups_of(hq, units), lax.axis_size("mp")), 1,
        [whole_block(g) for g in (*parts, cols, *gain_parts)], outs, [], length, "message_sums",
    )


def updates(grads, rows, parts, model_width, hq, units):
    own_rows = grads[0].shape[0]
    shapes = [
        (3, own_rows, hq), (own_rows, hq), (own_rows, hq), (own_rows, 2, hq), (own_rows, hq),
        (own_rows, 2, units), (own_rows, units),
    ]
    outs = [(sds(shape, F32), full(shape)) for shape in shapes + shapes + [parts[0].shape]]
    results = run(
        functools.partial(update_kernel, groups_of(hq, units), lax.axis_size("mp"), model_width, hq, units),
        1, [whole_block(g) for g in (*grads, rows, *parts)], outs, [], 8 * own_rows * (8 * hq + 3 * units),
        "updates",
    )
    results = list(results)
    results[0] = results[0].transpose(1, 0, 2)
    results[7] = results[7].transpose(1, 0, 2)
    return results


def on_device(
    tokens,
    memory,
    cotangent,
    table_lengths,
    table_plots,
    gains,
    w_qkv,
    w_self_out,
    w_cross_query,
    w_cross_kv,
    w_cross_out,
    w_gate_up,
    w_down,
):
    slots, width = tokens.shape
    hq = w_self_out.shape[1]
    heads = hq // DH
    units = w_down.shape[1]
    place = lax.axis_index("dp")
    x, z = place % 2, (place // 2) % 2
    ctl = jnp.stack([x, z]).astype(jnp.int32)
    gain_rows = gains.T
    gain_a, gain_b, gain_c = gain_rows[0:1], gain_rows[1:2], gain_rows[2:3]

    w_a = jnp.concatenate([w_qkv.transpose(1, 2, 0).reshape(3 * hq, width), w_self_out.T], axis=0)
    w_b = jnp.concatenate(
        [w_cross_query.T, w_cross_kv.transpose(1, 2, 0).reshape(2 * hq, width), w_cross_out.T], axis=0
    )
    w_f = jnp.concatenate(
        [w_gate_up.transpose(1, 2, 0).reshape(2 * units, width), w_down.T], axis=0
    )
    cut_f = w_f.shape[0] * 5 // 6
    ways = lax.axis_size("dp")

    ya0, ya1 = (swap(half, "mp", 2) for half in halves_of_quarter(w_a, x, z))
    send_b = y_pieces(w_b, x, z)
    send_f0, send_f1 = halves_of_quarter(w_f[:cut_f], x, z)
    ya0, ya1, send_b, send_f0, send_f1, w_a, w_b, w_f = together(
        ya0, ya1, send_b, send_f0, send_f1, w_a, w_b, w_f
    )

    y_b = swap(send_b, "mp", 2)
    xa0, za1 = swap(ya0, "dp", 1), swap(ya1, "dp", 2)
    xa1, za0 = swap(ya1, "dp", 1), swap(ya0, "dp", 2)
    qkv0, mixed_a0, lse_a0, part = self_forward(table_lengths, tokens, gain_a, w_a, heads)
    xa0, xa1, za0, za1, part, memory_late, send_f0 = together(xa0, xa1, za0, za1, part, memory, send_f0)
    da0, da1 = swap(xa0, "dp", 2), swap(za1, "dp", 1)
    y_f0 = swap(send_f0, "mp", 2)
    kv0 = memory_forward(memory_late, w_b, heads)
    send_g = w_f[cut_f:].astype(F32)
    da0, da1, kv0, send_g = together(da0, da1, kv0, send_g)
    far_a = (ya0, ya1, xa0, xa1, za0, za1, da0, da1)
    qkv1, mixed_a1, lse_a1, part, w_a1 = self_forward(
        table_lengths, tokens, gain_a, None, heads, remote=(ctl, far_a, part)
    )
    part, send_f1, y_b, y_f0 = together(part, send_f1, y_b, y_f0)

    part_other = swap(part, "mp", 1)
    y_f1 = swap(send_f1, "mp", 2)
    x_b, z_b = hand_on(y_b)
    q0, mixed_b0, lse_b0, part, first, normed_b = cross_forward(
        table_lengths, table_plots, heads, lead=(tokens, part, part_other, gain_b, w_b, kv0)
    )
    x_b, z_b, y_f1, part, send_g = together(x_b, z_b, y_f1, part, send_g)
    x_f0, z_f1 = swap(y_f0, "dp", 1), swap(y_f1, "dp", 2)
    q1, mixed_b1, lse_b1, part, w_b1, kv1 = cross_forward(
        table_lengths, table_plots, heads, follow=(normed_b, ctl, memory, part, (y_b, x_b, z_b))
    )
    send_g, x_f0, z_f1, part = together(send_g, x_f0, z_f1, part)
    far_z, far_x = hand_on_again(y_f0, y_f1, x_f0, z_f1)

    part_other = swap(part, "mp", 1)
    y_g = swap(send_g, "mp", 2)
    res, back, second, normed_c, *grad_f = feed(
        units, lead=(ctl, ways, first, part, part_other, gain_c, cotangent, w_f)
    )
    y_g, far_z, far_x, *grad_f = together(y_g, far_z, far_x, *grad_f)
    far_f = ((y_f0, y_f1, x_f0, z_f1, far_z, far_x), (y_g,))
    rs_f = halvings(grad_f, QUARTERS)
    rs_f[0].start()
    rs_f[2].start()
    res, back = feed(units, follow=(ctl, normed_c, cotangent, far_f, res, back))
    rs_f[0].got, rs_f[2].got, back = together(rs_f[0].got, rs_f[2].got, back)
    rs_f[1].start()
    rs_f[3].start()
    back_other = swap(back, "mp", 1)
    near_dq, near_dkv, branch_b, gain_grad_c, *grad_b = cross_backward(
        table_lengths, table_plots, w_b, q0, lse_b0, kv0, heads,
        lead=(ctl, ways, second, back, back_other, cotangent, gain_c, normed_b, memory, mixed_b0),
    )
    rs_f[1].got, rs_f[3].got, res, lse_b1, *grad_b = together(
        rs_f[1].got, rs_f[3].got, res, lse_b1, *grad_b
    )
    rs_f = second_stage(rs_f, ctl)
    res_other = swap(res, "mp", 1)

    for rs in rs_f:
        rs.start()
    back, back_mem = cross_backward(
        table_lengths, table_plots, w_b1, q1, lse_b1, kv1, heads,
        follow=(branch_b, mixed_b1, near_dq, near_dkv, w_b),
    )
    rs_f[0].got, rs_f[1].got, back, res_other = together(
        rs_f[0].got, rs_f[1].got, back, res_other
    )

    back_other = swap(back, "mp", 1)
    rs_b = halvings(grad_b)
    for rs in rs_f:
        rs.finish()
    rs_f[1].start()
    for rs in rs_b:
        rs.start()
    near_rows, branch_a, gain_grad_b, *grad_a = self_backward(
        table_lengths, w_a, qkv0, lse_a0, heads,
        lead=(ctl, ways, first, back, back_other, branch_b, gain_b, tokens, gain_a, mixed_a0),
    )
    rs_b[0].got, rs_b[1].got, rs_f[1].got, back_mem, lse_a1, *grad_a = together(
        rs_b[0].got, rs_b[1].got, rs_f[1].got, back_mem, lse_a1, *grad_a
    )
    mem_other = swap(back_mem, "mp", 1)

    rs_a = halvings(grad_a, THIRDS)
    for rs in rs_a:
        rs.start()
    for rs in rs_b:
        rs.finish()
        rs.start()
    rs_f[0].start()
    (back,) = self_backward(table_lengths, w_a1, qkv1, lse_a1, heads, follow=(branch_a, mixed_a1, near_rows, w_a))
    grad_memory = back_mem + mem_other
    rs_a[0].got, rs_a[1].got, rs_b[0].got, rs_b[1].got, rs_f[0].got, back, grad_memory = together(
        rs_a[0].got, rs_a[1].got, rs_b[0].got, rs_b[1].got, rs_f[0].got, back, grad_memory
    )

    back_other = swap(back, "mp", 1)
    rs_b = last_bits(rs_b)
    rs_b.start()
    for rs in rs_a:
        rs.finish()
        rs.start()
    grad_tokens, gain_grad_a = tail(tokens, back, back_other, branch_a, gain_a)
    rs_a[0].got, rs_a[1].got, rs_b.got, gain_grad_a, res, res_other, second = together(
        rs_a[0].got, rs_a[1].got, rs_b.got, gain_grad_a, res, res_other, second
    )
    rs_a = last_bits(rs_a)
    rs_a.start()
    layer_out = (second + (res + res_other)).astype(BF16)
    rs_a.got, layer_out = together(rs_a.got, layer_out)
    grads = []
    for rs in (*rs_f, rs_b, rs_a):
        rs.finish()
        grads.append(rs.rest())

    row_sums, col_sums = square_sums(grads, hq, units)
    row_sums, message = message_of(
        exchange_sums(row_sums, "mp"), col_sums, (gain_grad_a, gain_grad_b, gain_grad_c), hq, units
    )
    parts = exchange_sums(message, "dp")
    *results, message = updates(grads, row_sums, parts, width, hq, units)
    own_rows = grads[0].shape[0]
    grad_gains = lax.dynamic_slice_in_dim(
        message[:, col_sums.shape[1] + 128 :].reshape(3, width), place * own_rows, own_rows, axis=1
    ).T
    return (layer_out, grad_tokens, grad_memory, grad_gains, *results)


def solution(mesh):
    split = P("dp", None)
    cols = P(None, "mp")
    cols3 = P(None, None, "mp")
    both = P("dp", "mp")
    both3 = P("dp", None, "mp")
    return jax.shard_map(
        on_device,
        mesh=mesh,
        in_specs=(
            split, split, split, split, split, P(),
            cols3, cols, cols, cols3, cols, cols3, cols,
        ),
        out_specs=(
            split, split, split, split,
            both3, both, both, both3, both, both3, both,
            both3, both, both, both3, both, both3, both,
        ),
        check_vma=False,
    )
```
